256 devices in a mesh: dp: 16 (over z, core), proto: 16 (over x, y).
Axes of the slice: x: 4, y: 4, z: 8, core: 2. Of those that a mesh axis runs over, the one named last changes fastest.
Arguments:
- student_rows: bfloat16 [64, 256, 256], P('dp'), may hold values from -8 to 8
- teacher_rows: bfloat16 [64, 256, 256], P('dp'), may hold values from -8 to 8
- prototypes: bfloat16 [256, 131072], P(None, 'proto'), may hold values from -8 to 8
- center: float32 [131072], P('proto'), may hold values from -1.2 to 1.2
- mask_index: int32 [64, 128], P('dp'), may hold values from 0 to 255, as said below
- mask_count: int32 [64], P('dp'), may hold values from 0 to 128, as said below
- loss_scale: float32 [], replicated, may hold values from 1024 to 4096
Outputs:
- loss: float32 [], replicated
- student_grad: float32 [64, 256, 256], P('dp')
- proto_grad: float32 [131072, 256], P(('proto', 'dp'))
- patch_center: float32 [131072], P('proto')
The draws below stay inside these ranges and needn't reach their ends.
Inputs may be any that keep to these rules, and one draw needn't show every extreme that they name: `mask_index`: for each image the first mask_count entries are distinct patch numbers; the later entries are patch numbers that are ignored. `mask_count`: the counts of all 64 images sum to 4096; some images have no masked patch.
All inputs are finite; a program needn't handle non-finite values.
Results may differ from the reference program's by a relative error of at most 0.022.
Values may be sent and summed in bfloat16 or wider, within the bound.
No kernel may reach another device: no remote copies, remote signals or barrier semaphores. Data moves between devices by JAX's collectives and lax.ppermute only.
A program may use at most 128 MiB of HBM per device.

```python
import math
import jax
import jax.numpy as jnp
from jax import lax

D = 256
PROTOS = 131072
PATCHES = 256
MAXM = 128
IMAGES = 64
TOTAL = 4096


def draw_prototypes(key, part):
    key = jax.random.fold_in(key, 21)
    base = 0.5 * jax.random.normal(key, (D, PROTOS), jnp.float32)
    return jnp.clip(base, -8.0, 8.0).astype(jnp.bfloat16)


def draw_student_rows(key, part):
    key = jax.random.fold_in(key, 31)
    first = jax.random.fold_in(key, 0)
    base = jax.random.normal(first, (IMAGES, PATCHES, D), jnp.float32)
    return jnp.clip(base, -8.0, 8.0).astype(jnp.bfloat16)


def draw_teacher_rows(key, part):
    key = jax.random.fold_in(key, 41)
    first = jax.random.fold_in(key, 0)
    fourth = jax.random.fold_in(key, 3)
    shared = jax.random.normal(fourth, (1, 1, D), jnp.float32)
    base = 0.7 * jax.random.normal(first, (IMAGES, PATCHES, D), jnp.float32) + 0.7 * shared
    return jnp.clip(base, -8.0, 8.0).astype(jnp.bfloat16)


def draw_mask_index(key, part):
    key = jax.random.fold_in(key, 13)
    keys = jax.random.split(key, IMAGES)
    orders = jax.vmap(lambda single: jax.random.permutation(single, PATCHES))(keys)
    return orders[:, :MAXM].astype(jnp.int32)


def draw_mask_count(key, part):
    key = jax.random.fold_in(key, 11)
    first, second, third = jax.random.split(key, 3)
    half = IMAGES // 2
    counts = jax.random.randint(first, (half,), 0, MAXM + 1)
    masked = jax.random.randint(third, (half,), 0, 2)
    counts = (counts * masked).at[0].set(0)
    full = jnp.concatenate([counts, MAXM - counts])
    order = jax.random.permutation(second, IMAGES)
    return full[order].astype(jnp.int32)


def levels(key, shape, shards, low, high):
    loudness = 1.0
    for dim, shards_of in shards:
        steps = jax.random.uniform(jax.random.fold_in(jax.random.fold_in(key, 6), dim), (shards_of,), jnp.float32, low / len(shards), high / len(shards))
        loudness = loudness * jnp.repeat(jnp.exp(steps), shape[dim] // shards_of).reshape((-1,) + (1,) * (len(shape) - 1 - dim))
    return loudness


def centred(stream_key, dims, deviation, most, shards=(), kind=jnp.bfloat16):
    values = jax.random.normal(stream_key, dims, jnp.float32) * deviation
    if len(shards) > 0:
        values = levels(stream_key, dims, shards, -0.22, 0.18) * values
    return jnp.clip(values, min=-most, max=most).astype(kind)


def setup_inputs(seed: int = 0) -> dict:
    seeds = jax.random.split(jax.random.key(seed), 8)
    student_rows = draw_student_rows(jax.random.fold_in(seeds[7], 71), 0)
    teacher_rows = draw_teacher_rows(jax.random.fold_in(seeds[7], 71), 0)
    prototypes = draw_prototypes(jax.random.fold_in(seeds[7], 71), 0)
    center = centred(seeds[3], (PROTOS,), 0.2, 1.2, ((0, 16),), jnp.float32)
    mask_index = draw_mask_index(jax.random.fold_in(seeds[7], 71), 0)
    mask_count = draw_mask_count(jax.random.fold_in(seeds[7], 71), 0)
    loss_scale = jnp.clip(jnp.exp(jax.random.uniform(seeds[6], (), jnp.float32, math.log(1024.0), math.log(4096.0))), 1024.0, 4096.0)
    return {"student_rows": student_rows, "teacher_rows": teacher_rows, "prototypes": prototypes, "center": center, "mask_index": mask_index, "mask_count": mask_count, "loss_scale": loss_scale}


teacher_temp = 0.04
student_temp = 0.1
norm_epsilon = 1e-06

def unit_rows(raw):
    values = raw.astype(jnp.float32)
    length = jnp.sqrt(lax.optimization_barrier(jnp.sum(values * values, axis=1, keepdims=True)) + norm_epsilon)
    return (values / length, length)

def reference(student_rows, teacher_rows, prototypes, center, mask_index, mask_count, loss_scale):
    ends = jnp.cumsum(mask_count).astype(jnp.int32)
    starts = (ends - mask_count).astype(jnp.int32)
    rank = jnp.arange(TOTAL, dtype=jnp.int32)
    image = lax.optimization_barrier(jnp.sum((ends[None, :] <= rank[:, None]).astype(jnp.int32), axis=1)).astype(jnp.int32)
    within = (rank - starts[image]).astype(jnp.int32)
    patch = mask_index[image, within].astype(jnp.int32)
    weight = 1.0 / (IMAGES * mask_count[image].astype(jnp.float32))
    block = min(TOTAL, 512)
    blocks = TOTAL // block

    def one_block(carry, item):
        loss_sum, col_sum, grad_sum = carry
        img_b, patch_b, weight_b = item
        s_unit, s_len = unit_rows(student_rows[img_b, patch_b])
        t_unit, t_len = unit_rows(teacher_rows[img_b, patch_b])
        s_half = s_unit.astype(jnp.bfloat16)
        t_half = t_unit.astype(jnp.bfloat16)
        s_logit = jnp.dot(s_half, prototypes, preferred_element_type=jnp.float32)
        t_logit = jnp.dot(t_half, prototypes, preferred_element_type=jnp.float32)
        col_sum = col_sum + lax.optimization_barrier(jnp.sum(t_logit, axis=0))
        t_prob = jax.nn.softmax((t_logit - center[None, :]) / teacher_temp, axis=1)
        s_arg = s_logit / student_temp
        s_lse = jax.nn.logsumexp(s_arg, axis=1)
        s_prob = jnp.exp(s_arg - s_lse[:, None])
        ce = s_lse - lax.optimization_barrier(jnp.sum(t_prob * s_arg, axis=1))
        loss_sum = loss_sum + jnp.sum(weight_b * ce)
        dlogit = (loss_scale * weight_b[:, None] * (s_prob - t_prob) / student_temp).astype(jnp.bfloat16)
        d_unit = jnp.dot(dlogit, prototypes.T, preferred_element_type=jnp.float32)
        grad_sum = grad_sum + jnp.dot(dlogit.T, s_half, preferred_element_type=jnp.float32)
        row_grad = (d_unit - s_unit * lax.optimization_barrier(jnp.sum(s_unit * d_unit, axis=1, keepdims=True))) / s_len
        return ((loss_sum, col_sum, grad_sum), row_grad)
    init = (jnp.zeros((), jnp.float32), jnp.zeros((PROTOS,), jnp.float32), jnp.zeros((PROTOS, D), jnp.float32))
    items = (image.reshape(blocks, block), patch.reshape(blocks, block), weight.reshape(blocks, block))
    (loss, col_sum, proto_grad), row_grads = lax.scan(one_block, init, items)
    row_grads = row_grads.reshape(TOTAL, D)
    student_grad = jnp.zeros((IMAGES, PATCHES, D), jnp.float32).at[image, patch].set(row_grads)
    patch_center = col_sum / TOTAL
    return (loss, student_grad, proto_grad, patch_center)
```

```python
import functools
import math

import jax
import jax.numpy as jnp
from jax import lax
from jax.experimental import pallas as pl
from jax.experimental.pallas import tpu as pltpu
from jax.sharding import Mesh, PartitionSpec as P

bf16 = jnp.bfloat16
f32 = jnp.float32
log2e = math.log2(math.e)
ln2 = math.log(2.0)
t_scale = log2e / 0.04
s_scale = log2e / 0.1
inverse_temp = 10.0
norm_epsilon = 1e-06
low = -1e30

Z, CORES, X, Y = 8, 2, 4, 4
D = 256
SLOTS = 128
IMAGES = 64
TOTAL = 4096
LOCAL = 4
ROWS = LOCAL * SLOTS
BOTH = 2 * ROWS
CHUNK = 512
TILE = 256

NT = (((1,), (1,)), ((), ()))
TN = (((0,), (0,)), ((), ()))


def dot(a, b, dims=(((1,), (0,)), ((), ()))):
    return lax.dot_general(a, b, dims, preferred_element_type=f32)


def params():
    return pltpu.CompilerParams(vmem_limit_bytes=48 * 1024 * 1024)


def cost(flops, nbytes, trans=0):
    return pl.CostEstimate(flops=flops, bytes_accessed=nbytes, transcendentals=trans)


def picks(index_ref, count, i):
    patch = lax.broadcasted_iota(jnp.int32, (D, SLOTS), 0)
    slot = lax.broadcasted_iota(jnp.int32, (D, SLOTS), 1)
    hit = (patch == index_ref[i : i + 1, :]) & (slot < count)
    return jnp.where(hit, 1.0, 0.0).astype(bf16)


def unit_rows(values):
    length = jnp.sqrt(jnp.sum(values * values, axis=1, keepdims=True) + norm_epsilon)
    return values / length, length


def prep_kernel(count_ref, index_ref, s_ref, t_ref, out_ref):
    for i in range(LOCAL):
        pick = picks(index_ref, count_ref[i], i)
        for which, ref in enumerate((s_ref, t_ref)):
            unit, _ = unit_rows(dot(pick, ref[i], TN))
            out_ref[which, i * SLOTS : (i + 1) * SLOTS, :] = unit.astype(bf16)


def prep(count, index, student, teacher):
    smem = pl.BlockSpec(memory_space=pltpu.SMEM)
    vmem = pl.BlockSpec(memory_space=pltpu.VMEM)
    return pl.pallas_call(
        prep_kernel,
        out_shape=jax.ShapeDtypeStruct((2, ROWS, D), bf16),
        in_specs=[smem, vmem, vmem, vmem],
        out_specs=vmem,
        compiler_params=params(),
        cost_estimate=cost(2 * 2 * ROWS * D * D, 1 << 21),
    )(count, index, student, teacher)


def turn_kernel(ids_ref, p_ref, c_ref, pt_ref, cb_ref):
    pt_ref[0] = p_ref[...].T
    cb_ref[0] = jnp.broadcast_to(c_ref[0] * -t_scale, (128, CHUNK)).T


def turn(ids, prototypes, center):
    grid = pltpu.PrefetchScalarGridSpec(
        num_scalar_prefetch=1,
        grid=(Z,),
        in_specs=[
            pl.BlockSpec((D, CHUNK), lambda i, ids: (0, 2 * i + ids[1])),
            pl.BlockSpec((1, 1, CHUNK), lambda i, ids: (2 * i + ids[1], 0, 0)),
        ],
        out_specs=[
            pl.BlockSpec((1, CHUNK, D), lambda i, ids: (i, 0, 0)),
            pl.BlockSpec((1, CHUNK, 128), lambda i, ids: (i, 0, 0)),
        ],
    )
    return pl.pallas_call(
        turn_kernel,
        grid_spec=grid,
        out_shape=[
            jax.ShapeDtypeStruct((Z, CHUNK, D), bf16),
            jax.ShapeDtypeStruct((Z, CHUNK, 128), f32),
        ],
        compiler_params=params(),
        cost_estimate=cost(0, 6 << 20),
    )(ids, prototypes, center.reshape(2 * Z, 1, CHUNK))


def wide(block, times):
    return jnp.concatenate([block] * times, axis=1)


def stats_kernel(count_ref, pt_ref, cb_ref, mine_ref, other_ref, out_ref, sum_ref, acc):
    step = pl.program_id(0)

    @pl.when(step == 0)
    def _():
        acc[...] = jnp.zeros(acc.shape, f32)
        acc[0] = jnp.full((8, BOTH), low, f32)
        acc[3] = jnp.full((8, BOTH), low, f32)

    protos = pt_ref[0]
    shift = wide(cb_ref[0], TILE // 128)
    for half, ref in enumerate((mine_ref, other_ref)):
        for j in range(ROWS // TILE):
            rows = slice(j * TILE, (j + 1) * TILE)
            at = slice(half * ROWS + j * TILE, half * ROWS + (j + 1) * TILE)
            t_arg = (dot(protos, ref[1, rows, :], NT) * t_scale + shift).reshape(CHUNK // 8, 8, TILE)
            s_arg = (dot(protos, ref[0, rows, :], NT) * s_scale).reshape(CHUNK // 8, 8, TILE)
            t_old, s_old = acc[0, :, at], acc[3, :, at]
            t_top = jnp.maximum(t_old, jnp.max(t_arg, axis=0))
            s_top = jnp.maximum(s_old, jnp.max(s_arg, axis=0))
            t_exp = jnp.exp2(t_arg - t_top[None])
            s_exp = jnp.exp2(s_arg - s_top[None])
            t_keep = jnp.exp2(t_old - t_top)
            s_keep = jnp.exp2(s_old - s_top)
            acc[0, :, at] = t_top
            acc[1, :, at] = acc[1, :, at] * t_keep + jnp.sum(t_exp, axis=0)
            acc[2, :, at] = acc[2, :, at] * t_keep + jnp.sum(t_exp * s_arg, axis=0)
            acc[3, :, at] = s_top
            acc[4, :, at] = acc[4, :, at] * s_keep + jnp.sum(s_exp, axis=0)

    @pl.when(step == Z - 1)
    def _():
        t_top = jnp.max(acc[0], axis=0, keepdims=True)
        s_top = jnp.max(acc[3], axis=0, keepdims=True)
        t_keep = jnp.exp2(acc[0] - t_top)
        s_keep = jnp.exp2(acc[3] - s_top)
        out_ref[0:1, :] = t_top
        out_ref[1:2, :] = jnp.sum(acc[1] * t_keep, axis=0, keepdims=True)
        out_ref[2:3, :] = jnp.sum(acc[2] * t_keep, axis=0, keepdims=True)
        out_ref[3:4, :] = s_top
        out_ref[4:5, :] = jnp.sum(acc[4] * s_keep, axis=0, keepdims=True)
        out_ref[5:8, :] = jnp.zeros((3, BOTH), f32)
        slot = lax.broadcasted_iota(jnp.int32, (1, SLOTS), 1)
        for i in range(LOCAL):
            count = jnp.full((1, SLOTS), count_ref[i], jnp.int32)
            weight = 1.0 / (IMAGES * jnp.maximum(count, 1).astype(f32))
            out_ref[5:6, i * SLOTS : (i + 1) * SLOTS] = jnp.where(slot < count, weight, 0.0)
        first = jnp.sum(mine_ref[1].astype(f32), axis=0, keepdims=True)
        second = jnp.sum(other_ref[1].astype(f32), axis=0, keepdims=True)
        sum_ref[...] = jnp.broadcast_to(first + second, (8, D))


def local_stats(count, turned, shifts, mine, other):
    whole = pl.BlockSpec((2, ROWS, D), lambda i, n: (0, 0, 0))
    grid = pltpu.PrefetchScalarGridSpec(
        num_scalar_prefetch=1,
        grid=(Z,),
        in_specs=[
            pl.BlockSpec((1, CHUNK, D), lambda i, n: (i, 0, 0)),
            pl.BlockSpec((1, CHUNK, 128), lambda i, n: (i, 0, 0)),
            whole,
            whole,
        ],
        out_specs=[
            pl.BlockSpec((8, BOTH), lambda i, n: (0, 0)),
            pl.BlockSpec((8, D), lambda i, n: (0, 0)),
        ],
        scratch_shapes=[pltpu.VMEM((5, 8, BOTH), f32)],
    )
    return pl.pallas_call(
        stats_kernel,
        grid_spec=grid,
        out_shape=[jax.ShapeDtypeStruct((8, BOTH), f32), jax.ShapeDtypeStruct((8, D), f32)],
        compiler_params=params(),
        cost_estimate=cost(4 * BOTH * Z * CHUNK * D, 6 << 20, 2 * BOTH * Z * CHUNK),
    )(count, turned, shifts, mine, other)


def tree(parts):
    while len(parts) > 1:
        parts = [parts[i] + parts[i + 1] for i in range(0, len(parts), 2)]
    return parts[0]


def merged(parts):
    t_top = functools.reduce(jnp.maximum, [p[0:1] for p in parts])
    s_top = functools.reduce(jnp.maximum, [p[3:4] for p in parts])
    t_keep = [jnp.exp2(p[0:1] - t_top) for p in parts]
    s_keep = [jnp.exp2(p[3:4] - s_top) for p in parts]
    t_sum = tree([p[1:2] * k for p, k in zip(parts, t_keep)])
    cross = tree([p[2:3] * k for p, k in zip(parts, t_keep)])
    s_sum = tree([p[4:5] * k for p, k in zip(parts, s_keep)])
    return t_top, t_sum, cross, s_top, s_sum


def core_merge_kernel(mine_ref, got_ref, out_ref):
    mine = mine_ref[...]
    got = jnp.concatenate([got_ref[:, ROWS:], got_ref[:, :ROWS]], axis=1)
    for i, row in enumerate(merged([mine, got])):
        out_ref[i : i + 1, :] = row
    out_ref[5:6, :] = mine[5:6] + got[5:6]
    out_ref[6:8, :] = jnp.zeros((2, BOTH), f32)


def merge_kernel(*refs):
    out_ref = refs[-1]
    parts = [ref[...] for ref in refs[:-1]]
    for i, row in enumerate(merged(parts)):
        out_ref[i : i + 1, :] = row
    out_ref[5:8, :] = parts[0][5:8]


def last_merge_kernel(scale_ref, a, b, c, d, sum_ref, coef_ref, misc_ref):
    parts = [ref[...] for ref in (a, b, c, d)]
    t_top, t_sum, cross, s_top, s_sum = merged(parts)
    weight = parts[0][5:6]
    live = weight > 0.0
    s_lse = s_top + jnp.log2(s_sum)
    ce = (s_lse - cross / t_sum) * ln2
    factor = jnp.log2(jnp.where(live, weight * (scale_ref[0] * inverse_temp), 1.0))
    coef_ref[0:1, :] = jnp.where(live, factor - s_lse, low)
    coef_ref[1:2, :] = jnp.where(live, factor - t_top - jnp.log2(t_sum), low)
    coef_ref[2:8, :] = jnp.zeros((6, BOTH), f32)
    part = jnp.where(live, weight * ce, 0.0)
    first = jnp.sum(part[:, :ROWS], axis=1, keepdims=True)
    second = jnp.sum(part[:, ROWS:], axis=1, keepdims=True)
    misc_ref[0:1, :] = sum_ref[0:1, :]
    misc_ref[1:8, :] = jnp.broadcast_to(first + second, (7, D))


def small_call(kernel, out_shape, *args, smem=()):
    specs = [
        pl.BlockSpec(memory_space=pltpu.SMEM if i in smem else pltpu.VMEM) for i in range(len(args))
    ]
    vmem = pl.BlockSpec(memory_space=pltpu.VMEM)
    return pl.pallas_call(
        kernel,
        out_shape=out_shape,
        in_specs=specs,
        out_specs=jax.tree.map(lambda _: vmem, out_shape),
        compiler_params=params(),
        cost_estimate=cost(1 << 20, 1 << 18),
    )(*args)


def swapped(axis, size, bit):
    return [(i, i ^ bit) for i in range(size)]


def swap(value, axis, size, bit):
    return lax.ppermute(value, axis, swapped(axis, size, bit))


def grad_kernel(n, split, ids_ref, order_ref, pt_ref, cb_ref, p_ref, mine_ref, other_ref, coef_ref, *refs):
    out_refs, du_ref = refs[:-1], refs[-1]
    step = pl.program_id(0)
    protos = pt_ref[0]
    shift = wide(cb_ref[0], TILE // 128)
    wide_p = p_ref[...]
    total = None
    for half, ref in enumerate((mine_ref, other_ref)):
        for j in range(ROWS // TILE):
            rows = slice(j * TILE, (j + 1) * TILE)
            at = slice(half * ROWS + j * TILE, half * ROWS + (j + 1) * TILE)
            s_rows = ref[0, rows, :]
            t_arg = dot(protos, ref[1, rows, :], NT) * t_scale + shift + coef_ref[1:2, at]
            s_arg = dot(protos, s_rows, NT) * s_scale + coef_ref[0:1, at]
            dlogit = (jnp.exp2(s_arg) - jnp.exp2(t_arg)).astype(bf16)
            part = dot(dlogit, s_rows)
            total = part if total is None else total + part
            du = dot(wide_p, dlogit)

            @pl.when(step == 0)
            def _(at=at, du=du):
                du_ref[:, at] = du

            @pl.when(step > 0)
            def _(at=at, du=du):
                du_ref[:, at] += du

    if split:
        out_refs[0][...] = total[: CHUNK // 2].astype(bf16)
        out_refs[1][...] = total[CHUNK // 2 :].astype(bf16)
    else:
        out_refs[0][0] = total


def grads(ids, offsets, split, turned, shifts, prototypes, mine, other, coef):
    n = len(offsets)
    order = lax.rem(ids[0] + jnp.array([d % Z for d in offsets], jnp.int32), Z)
    whole = pl.BlockSpec((2, ROWS, D), lambda i, ids, order: (0, 0, 0))
    if split:
        outs = [jax.ShapeDtypeStruct((CHUNK // 2, D), bf16)] * 2
        specs = [pl.BlockSpec((CHUNK // 2, D), lambda i, ids, order: (0, 0))] * 2
    else:
        outs = [jax.ShapeDtypeStruct((n, CHUNK, D), f32)]
        specs = [pl.BlockSpec((1, CHUNK, D), lambda i, ids, order: (i, 0, 0))]
    grid = pltpu.PrefetchScalarGridSpec(
        num_scalar_prefetch=2,
        grid=(n,),
        in_specs=[
            pl.BlockSpec((1, CHUNK, D), lambda i, ids, order: (order[i], 0, 0)),
            pl.BlockSpec((1, CHUNK, 128), lambda i, ids, order: (order[i], 0, 0)),
            pl.BlockSpec((D, CHUNK), lambda i, ids, order: (0, 2 * order[i] + ids[1])),
            whole,
            whole,
            pl.BlockSpec((8, BOTH), lambda i, ids, order: (0, 0)),
        ],
        out_specs=specs + [pl.BlockSpec((D, BOTH), lambda i, ids, order: (0, 0))],
    )
    return pl.pallas_call(
        functools.partial(grad_kernel, n, split),
        grid_spec=grid,
        out_shape=outs + [jax.ShapeDtypeStruct((D, BOTH), f32)],
        compiler_params=params(),
        cost_estimate=cost(8 * BOTH * n * CHUNK * D, 3 << 20, 2 * BOTH * n * CHUNK),
    )(ids, order, turned, shifts, prototypes, mine, other, coef)


def du_send_kernel(a, b, c, out_ref):
    out_ref[...] = (a[:, ROWS:] + b[:, ROWS:] + c[:, ROWS:]).astype(bf16)


def du_first_kernel(ids_ref, a, b, c, got_ref, *refs):
    outs, total = refs[:4], refs[4]
    total[...] = a[:, :ROWS] + b[:, :ROWS] + c[:, :ROWS] + got_ref[...].astype(f32)
    y = ids_ref[3]
    for k in range(Y):
        start = pl.multiple_of(jnp.bitwise_xor(y, k) * (D // Y), D // Y)
        outs[k][...] = total[pl.ds(start, D // Y), :].astype(bf16)


def du_second_kernel(ids_ref, a, b, c, d, *refs):
    outs, total = refs[:4], refs[4]
    total[...] = a[...].astype(f32) + b[...].astype(f32) + c[...].astype(f32) + d[...].astype(f32)
    x = ids_ref[2]
    part = D // (Y * X)
    for k in range(X):
        start = pl.multiple_of(jnp.bitwise_xor(x, k) * part, part)
        outs[k][...] = total[pl.ds(start, part), :].astype(bf16)


def du_sum_kernel(a, b, c, d, out_ref):
    out_ref[...] = (a[...].astype(f32) + b[...].astype(f32) + c[...].astype(f32) + d[...].astype(f32)).astype(bf16)


def du_join_kernel(ids_ref, a, b, c, d, out_ref, held):
    part = D // (Y * X)
    x = ids_ref[2]
    for k, ref in enumerate((a, b, c, d)):
        start = pl.multiple_of(jnp.bitwise_xor(x, k) * part, part)
        held[pl.ds(start, part), :] = ref[...].astype(f32)
    out_ref[...] = held[...].astype(bf16)


def final_kernel(ids_ref, count_ref, index_ref, s_ref, a, b, c, d, out_ref, held):
    y = ids_ref[3]
    for k, ref in enumerate((a, b, c, d)):
        start = pl.multiple_of(jnp.bitwise_xor(y, k) * (D // Y), D // Y)
        held[pl.ds(start, D // Y), :] = ref[...].astype(f32)
    for i in range(LOCAL):
        pick = picks(index_ref, count_ref[i], i)
        unit, length = unit_rows(dot(pick, s_ref[i], TN))
        d_unit = held[:, i * SLOTS : (i + 1) * SLOTS].T
        row = (d_unit - unit * jnp.sum(unit * d_unit, axis=1, keepdims=True)) / length
        top = row.astype(bf16)
        rest = (row - top.astype(f32)).astype(bf16)
        out_ref[i] = dot(pick, top) + dot(pick, rest)


def scratch_call(kernel, out_shape, scratch, *args, smem=()):
    specs = [
        pl.BlockSpec(memory_space=pltpu.SMEM if i in smem else pltpu.VMEM) for i in range(len(args))
    ]
    vmem = pl.BlockSpec(memory_space=pltpu.VMEM)
    return pl.pallas_call(
        kernel,
        out_shape=out_shape,
        in_specs=specs,
        out_specs=jax.tree.map(lambda _: vmem, out_shape),
        scratch_shapes=scratch,
        compiler_params=params(),
        cost_estimate=cost(1 << 20, 1 << 20),
    )(*args)


def center_kernel(misc_ref, p_ref, out_ref):
    total = jnp.broadcast_to(misc_ref[0:1, :], (8, D))
    top = total.astype(bf16)
    rest = total - top.astype(f32)
    middle = rest.astype(bf16)
    last = (rest - middle.astype(f32)).astype(bf16)
    p = p_ref[...]
    out_ref[...] = (dot(top, p) + dot(middle, p) + dot(last, p)) * (1.0 / TOTAL)


def centers(misc, prototypes):
    width = prototypes.shape[1]
    block = 2048
    out = pl.pallas_call(
        center_kernel,
        grid=(width // block,),
        in_specs=[
            pl.BlockSpec((8, D), lambda i: (0, 0)),
            pl.BlockSpec((D, block), lambda i: (0, i)),
        ],
        out_specs=pl.BlockSpec((8, block), lambda i: (0, i)),
        out_shape=jax.ShapeDtypeStruct((8, width), f32),
        compiler_params=params(),
        cost_estimate=cost(6 * 8 * D * width, 5 << 20),
    )(misc, prototypes)
    return out[0]


def shards(student_rows, teacher_rows, prototypes, center, mask_index, mask_count, loss_scale):
    z, core, x, y = (lax.axis_index(a) for a in ("z", "core", "x", "y"))
    ids = jnp.stack([z, core, x, y]).astype(jnp.int32)
    down = [(i, (i - 1) % Z) for i in range(Z)]
    up = [(i, (i + 1) % Z) for i in range(Z)]

    mine = prep(mask_count, mask_index, student_rows, teacher_rows)
    other = swap(mine, "core", CORES, 1)
    turned, shifts = turn(ids, prototypes, center)
    stats, row_sum = local_stats(mask_count, turned, shifts, mine, other)

    shape = jax.ShapeDtypeStruct((8, BOTH), f32)
    stats = small_call(core_merge_kernel, shape, stats, swap(stats, "core", CORES, 1))
    stats = small_call(merge_kernel, shape, stats, *[swap(stats, "y", Y, k) for k in (1, 2, 3)])
    coef, misc = small_call(
        last_merge_kernel,
        [shape, jax.ShapeDtypeStruct((8, D), f32)],
        loss_scale.reshape(1),
        stats,
        *[swap(stats, "x", X, k) for k in (1, 2, 3)],
        row_sum,
        smem=(0,),
    )

    common = (turned, shifts, prototypes, mine, other, coef)
    half_a, half_b, du_a = grads(ids, [4], True, *common)
    from_up = lax.ppermute(half_a, "z", down)
    from_down = lax.ppermute(half_b, "z", up)
    far, du_b = grads(ids, [-3, 3], False, *common)
    half = CHUNK // 2
    send_down = jnp.concatenate([far[0, :half] + from_up.astype(f32), far[0, half:]]).astype(bf16)
    send_up = jnp.concatenate([far[1, :half], far[1, half:] + from_down.astype(f32)]).astype(bf16)
    from_up = lax.ppermute(send_down, "z", down)
    from_down = lax.ppermute(send_up, "z", up)
    near, du_c = grads(ids, [-2, 2, -1, 1, 0], False, *common)
    from_up = lax.ppermute((near[0] + from_up.astype(f32)).astype(bf16), "z", down)
    from_down = lax.ppermute((near[1] + from_down.astype(f32)).astype(bf16), "z", up)
    from_up = lax.ppermute((near[2] + from_up.astype(f32)).astype(bf16), "z", down)
    from_down = lax.ppermute((near[3] + from_down.astype(f32)).astype(bf16), "z", up)
    proto_grad = near[4] + from_up.astype(f32) + from_down.astype(f32)

    for bit in (1, 2, 4):
        misc = misc + swap(misc, "z", Z, bit)
    loss = misc[1, 0]
    patch_center = centers(misc, prototypes)

    send = small_call(du_send_kernel, jax.ShapeDtypeStruct((D, ROWS), bf16), du_a, du_b, du_c)
    got = swap(send, "core", CORES, 1)
    part = D // Y
    pieces = scratch_call(
        du_first_kernel,
        [jax.ShapeDtypeStruct((part, ROWS), bf16)] * Y,
        [pltpu.VMEM((D, ROWS), f32)],
        ids, du_a, du_b, du_c, got,
        smem=(0,),
    )
    got = [swap(pieces[k], "y", Y, k) for k in (1, 2, 3)]
    pieces = scratch_call(
        du_second_kernel,
        [jax.ShapeDtypeStruct((part // X, ROWS), bf16)] * X,
        [pltpu.VMEM((part, ROWS), f32)],
        ids, pieces[0], *got,
        smem=(0,),
    )
    got = [swap(pieces[k], "x", X, k) for k in (1, 2, 3)]
    own = small_call(du_sum_kernel, jax.ShapeDtypeStruct((part // X, ROWS), bf16), pieces[0], *got)
    got = [swap(own, "x", X, k) for k in (1, 2, 3)]
    own = scratch_call(
        du_join_kernel,
        jax.ShapeDtypeStruct((part, ROWS), bf16),
        [pltpu.VMEM((part, ROWS), f32)],
        ids, own, *got,
        smem=(0,),
    )
    got = [swap(own, "y", Y, k) for k in (1, 2, 3)]
    student_grad = scratch_call(
        final_kernel,
        jax.ShapeDtypeStruct(student_rows.shape, f32),
        [pltpu.VMEM((D, ROWS), f32)],
        ids, mask_count, mask_index, student_rows, own, *got,
        smem=(0, 1),
    )
    return (loss, student_grad, proto_grad, patch_center)


def solution(mesh):
    fine = Mesh(mesh.devices.reshape(Z, CORES, X, Y), ("z", "core", "x", "y"))
    dp, proto = ("z", "core"), ("x", "y")
    in_specs = (
        P(dp, None, None),
        P(dp, None, None),
        P(None, proto),
        P(proto),
        P(dp, None),
        P(dp),
        P(),
    )
    out_specs = (P(), P(dp, None, None), P(proto + dp, None), P(proto))
    return jax.shard_map(shards, mesh=fine, in_specs=in_specs, out_specs=out_specs, check_vma=False)
```

```python
import functools
import math

import jax
import jax.numpy as jnp
from jax import lax
from jax.experimental import pallas as pl
from jax.experimental.pallas import tpu as pltpu
from jax.sharding import Mesh, PartitionSpec as P

bf16 = jnp.bfloat16
f32 = jnp.float32
log2e = math.log2(math.e)
ln2 = math.log(2.0)
t_scale = log2e / 0.04
s_scale = log2e / 0.1
inverse_temp = 10.0
norm_epsilon = 1e-06
low = -1e30

Z, CORES, X, Y = 8, 2, 4, 4
D = 256
SLOTS = 128
IMAGES = 64
TOTAL = 4096
LOCAL = 4
ROWS = LOCAL * SLOTS
BOTH = 2 * ROWS
CHUNK = 512
TILE = 256
EXTRA = 48

NT = (((1,), (1,)), ((), ()))
TN = (((0,), (0,)), ((), ()))


def dot(a, b, dims=(((1,), (0,)), ((), ()))):
    return lax.dot_general(a, b, dims, preferred_element_type=f32)


def params():
    return pltpu.CompilerParams(vmem_limit_bytes=48 * 1024 * 1024)


def cost(flops, nbytes, trans=0):
    return pl.CostEstimate(flops=flops, bytes_accessed=nbytes, transcendentals=trans)


def picks(index_ref, count, i):
    patch = lax.broadcasted_iota(jnp.int32, (D, SLOTS), 0)
    slot = lax.broadcasted_iota(jnp.int32, (D, SLOTS), 1)
    hit = (patch == index_ref[i : i + 1, :]) & (slot < count)
    return jnp.where(hit, 1.0, 0.0).astype(bf16)


def unit_rows(values):
    length = jnp.sqrt(jnp.sum(values * values, axis=1, keepdims=True) + norm_epsilon)
    return values / length, length


def prep_kernel(count_ref, index_ref, s_ref, t_ref, out_ref):
    for i in range(LOCAL):
        pick = picks(index_ref, count_ref[i], i)
        for which, ref in enumerate((s_ref, t_ref)):
            unit, _ = unit_rows(dot(pick, ref[i], TN))
            out_ref[which, i * SLOTS : (i + 1) * SLOTS, :] = unit.astype(bf16)


def prep(count, index, student, teacher):
    smem = pl.BlockSpec(memory_space=pltpu.SMEM)
    vmem = pl.BlockSpec(memory_space=pltpu.VMEM)
    return pl.pallas_call(
        prep_kernel,
        out_shape=jax.ShapeDtypeStruct((2, ROWS, D), bf16),
        in_specs=[smem, vmem, vmem, vmem],
        out_specs=vmem,
        compiler_params=params(),
        cost_estimate=cost(2 * 2 * ROWS * D * D, 1 << 21),
    )(count, index, student, teacher)


def wide(block, times):
    return jnp.concatenate([block] * times, axis=1)


def stats_kernel(ids_ref, p_ref, c_ref, mine_ref, other_ref, out_ref, sum_ref, pt_ref, cb_ref, acc):
    step = pl.program_id(0)

    @pl.when(step == 0)
    def _():
        acc[...] = jnp.zeros(acc.shape, f32)
        acc[0] = jnp.full((8, BOTH), low, f32)
        acc[3] = jnp.full((8, BOTH), low, f32)

    protos = p_ref[...].T
    pt_ref[0] = protos
    column = jnp.broadcast_to(c_ref[0] * -t_scale, (128, CHUNK)).T
    cb_ref[0] = column
    shift = wide(column, TILE // 128)
    for half, ref in enumerate((mine_ref, other_ref)):
        for j in range(ROWS // TILE):
            rows = slice(j * TILE, (j + 1) * TILE)
            at = slice(half * ROWS + j * TILE, half * ROWS + (j + 1) * TILE)
            t_arg = (dot(protos, ref[1, rows, :], NT) * t_scale + shift).reshape(CHUNK // 8, 8, TILE)
            s_arg = (dot(protos, ref[0, rows, :], NT) * s_scale).reshape(CHUNK // 8, 8, TILE)
            t_old, s_old = acc[0, :, at], acc[3, :, at]
            t_top = jnp.maximum(t_old, jnp.max(t_arg, axis=0))
            s_top = jnp.maximum(s_old, jnp.max(s_arg, axis=0))
            t_exp = jnp.exp2(t_arg - t_top[None])
            s_exp = jnp.exp2(s_arg - s_top[None])
            t_keep = jnp.exp2(t_old - t_top)
            s_keep = jnp.exp2(s_old - s_top)
            acc[0, :, at] = t_top
            acc[1, :, at] = acc[1, :, at] * t_keep + jnp.sum(t_exp, axis=0)
            acc[2, :, at] = acc[2, :, at] * t_keep + jnp.sum(t_exp * s_arg, axis=0)
            acc[3, :, at] = s_top
            acc[4, :, at] = acc[4, :, at] * s_keep + jnp.sum(s_exp, axis=0)

    @pl.when(step == Z - 1)
    def _():
        t_top = jnp.max(acc[0], axis=0, keepdims=True)
        s_top = jnp.max(acc[3], axis=0, keepdims=True)
        t_keep = jnp.exp2(acc[0] - t_top)
        s_keep = jnp.exp2(acc[3] - s_top)
        out_ref[0:1, :] = t_top
        out_ref[1:2, :] = jnp.sum(acc[1] * t_keep, axis=0, keepdims=True)
        out_ref[2:3, :] = jnp.sum(acc[2] * t_keep, axis=0, keepdims=True)
        out_ref[3:4, :] = s_top
        out_ref[4:5, :] = jnp.sum(acc[4] * s_keep, axis=0, keepdims=True)
        out_ref[5:8, :] = jnp.zeros((3, BOTH), f32)
        slot = lax.broadcasted_iota(jnp.int32, (1, SLOTS), 1)
        for i in range(LOCAL):
            count = jnp.full((1, SLOTS), ids_ref[4 + i], jnp.int32)
            weight = 1.0 / (IMAGES * jnp.maximum(count, 1).astype(f32))
            out_ref[5:6, i * SLOTS : (i + 1) * SLOTS] = jnp.where(slot < count, weight, 0.0)
        first = jnp.sum(mine_ref[1].astype(f32), axis=0, keepdims=True)
        second = jnp.sum(other_ref[1].astype(f32), axis=0, keepdims=True)
        sum_ref[...] = jnp.broadcast_to(first + second, (8, D))


def local_stats(ids, prototypes, center, mine, other):
    whole = pl.BlockSpec((2, ROWS, D), lambda i, ids: (0, 0, 0))
    grid = pltpu.PrefetchScalarGridSpec(
        num_scalar_prefetch=1,
        grid=(Z,),
        in_specs=[
            pl.BlockSpec((D, CHUNK), lambda i, ids: (0, 2 * i + ids[1])),
            pl.BlockSpec((1, 1, CHUNK), lambda i, ids: (2 * i + ids[1], 0, 0)),
            whole,
            whole,
        ],
        out_specs=[
            pl.BlockSpec((8, BOTH), lambda i, ids: (0, 0)),
            pl.BlockSpec((8, D), lambda i, ids: (0, 0)),
            pl.BlockSpec((1, CHUNK, D), lambda i, ids: (i, 0, 0)),
            pl.BlockSpec((1, CHUNK, 128), lambda i, ids: (i, 0, 0)),
        ],
        scratch_shapes=[pltpu.VMEM((5, 8, BOTH), f32)],
    )
    return pl.pallas_call(
        stats_kernel,
        grid_spec=grid,
        out_shape=[
            jax.ShapeDtypeStruct((8, BOTH), f32),
            jax.ShapeDtypeStruct((8, D), f32),
            jax.ShapeDtypeStruct((Z, CHUNK, D), bf16),
            jax.ShapeDtypeStruct((Z, CHUNK, 128), f32),
        ],
        compiler_params=params(),
        cost_estimate=cost(4 * BOTH * Z * CHUNK * D, 6 << 20, 2 * BOTH * Z * CHUNK),
    )(ids, prototypes, center.reshape(2 * Z, 1, CHUNK), mine, other)


def split3(value):
    top = value.astype(bf16)
    rest = value - top.astype(f32)
    middle = rest.astype(bf16)
    return top, middle, (rest - middle.astype(f32)).astype(bf16)


def tree(parts):
    while len(parts) > 1:
        parts = [parts[i] + parts[i + 1] for i in range(0, len(parts), 2)]
    return parts[0]


def merged(parts):
    t_top = functools.reduce(jnp.maximum, [p[0:1] for p in parts])
    s_top = functools.reduce(jnp.maximum, [p[3:4] for p in parts])
    t_keep = [jnp.exp2(p[0:1] - t_top) for p in parts]
    s_keep = [jnp.exp2(p[3:4] - s_top) for p in parts]
    t_sum = tree([p[1:2] * k for p, k in zip(parts, t_keep)])
    cross = tree([p[2:3] * k for p, k in zip(parts, t_keep)])
    s_sum = tree([p[4:5] * k for p, k in zip(parts, s_keep)])
    return t_top, t_sum, cross, s_top, s_sum


def core_merge_kernel(mine_ref, got_ref, out_ref):
    mine = mine_ref[...]
    got = jnp.concatenate([got_ref[:, ROWS:], got_ref[:, :ROWS]], axis=1)
    for i, row in enumerate(merged([mine, got])):
        out_ref[i : i + 1, :] = row
    out_ref[5:6, :] = mine[5:6] + got[5:6]
    out_ref[6:8, :] = jnp.zeros((2, BOTH), f32)


def merge_kernel(*refs):
    out_ref = refs[-1]
    parts = [ref[...] for ref in refs[:-1]]
    for i, row in enumerate(merged(parts)):
        out_ref[i : i + 1, :] = row
    out_ref[5:8, :] = parts[0][5:8]


def last_merge_kernel(scale_ref, ids_ref, a, b, c, d, sum_ref, coef_ref, misc_ref):
    parts = [ref[...] for ref in (a, b, c, d)]
    t_top, t_sum, cross, s_top, s_sum = merged(parts)
    weight = parts[0][5:6]
    live = weight > 0.0
    s_lse = s_top + jnp.log2(s_sum)
    ce = (s_lse - cross / t_sum) * ln2
    factor = jnp.log2(jnp.where(live, weight * (scale_ref[0] * inverse_temp), 1.0))
    coef_ref[0:1, :] = jnp.where(live, factor - s_lse, low)
    coef_ref[1:2, :] = jnp.where(live, factor - t_top - jnp.log2(t_sum), low)
    coef_ref[2:8, :] = jnp.zeros((6, BOTH), f32)
    part = jnp.where(live, weight * ce, 0.0)
    first = jnp.sum(part[:, :ROWS], axis=1, keepdims=True)
    second = jnp.sum(part[:, ROWS:], axis=1, keepdims=True)
    slot = lax.broadcasted_iota(jnp.int32, (EXTRA, D), 0)
    mine = jnp.bitwise_and(slot, Z - 1) == ids_ref[0]
    row_sum = split3(sum_ref[0:1, :])
    losses = split3(jnp.broadcast_to(first + second, (1, D)))
    block = jnp.zeros((EXTRA, D), f32)
    for i in range(3):
        block = jnp.where(slot // Z == i, row_sum[i].astype(f32), block)
        block = jnp.where(slot // Z == 3 + i, losses[i].astype(f32), block)
    misc_ref[...] = jnp.where(mine, block, 0.0).astype(bf16)


def small_call(kernel, out_shape, *args, smem=()):
    specs = [
        pl.BlockSpec(memory_space=pltpu.SMEM if i in smem else pltpu.VMEM) for i in range(len(args))
    ]
    vmem = pl.BlockSpec(memory_space=pltpu.VMEM)
    return pl.pallas_call(
        kernel,
        out_shape=out_shape,
        in_specs=specs,
        out_specs=jax.tree.map(lambda _: vmem, out_shape),
        compiler_params=params(),
        cost_estimate=cost(1 << 20, 1 << 18),
    )(*args)


def swapped(axis, size, bit):
    return [(i, i ^ bit) for i in range(size)]


def swap(value, axis, size, bit):
    return lax.ppermute(value, axis, swapped(axis, size, bit))


def grad_kernel(n, split, ids_ref, order_ref, pt_ref, cb_ref, p_ref, mine_ref, other_ref, coef_ref, misc_ref, *refs):
    out_refs, du_ref = refs[:-1], refs[-1]
    step = pl.program_id(0)
    protos = pt_ref[0]
    shift = wide(cb_ref[0], TILE // 128)
    wide_p = p_ref[...]
    total = None

    @pl.when(step == 0)
    def _():
        du_ref[...] = jnp.zeros((D, BOTH), f32)

    for half, ref in enumerate((mine_ref, other_ref)):
        for j in range(ROWS // TILE):
            rows = slice(j * TILE, (j + 1) * TILE)
            at = slice(half * ROWS + j * TILE, half * ROWS + (j + 1) * TILE)
            s_rows = ref[0, rows, :]
            t_arg = dot(protos, ref[1, rows, :], NT) * t_scale + shift + coef_ref[1:2, at]
            s_arg = dot(protos, s_rows, NT) * s_scale + coef_ref[0:1, at]
            dlogit = (jnp.exp2(s_arg) - jnp.exp2(t_arg)).astype(bf16)
            part = dot(dlogit, s_rows)
            total = part if total is None else total + part
            du_ref[:, at] += dot(wide_p, dlogit)

    if split:
        half = CHUNK // 2
        out_refs[0][:half, :] = total[:half].astype(bf16)
        out_refs[0][half:, :] = misc_ref[...]
        out_refs[1][...] = total[half:].astype(bf16)
    else:
        for i in range(n):

            @pl.when(step == i)
            def _(i=i):
                out_refs[i][...] = total


def grads(ids, offsets, split, turned, shifts, prototypes, mine, other, coef, misc):
    n = len(offsets)
    order = lax.rem(ids[0] + jnp.array([d % Z for d in offsets], jnp.int32), Z)
    whole = pl.BlockSpec((2, ROWS, D), lambda i, ids, order: (0, 0, 0))
    if split:
        shapes = [(CHUNK // 2 + EXTRA, D), (CHUNK // 2, D)]
        outs = [jax.ShapeDtypeStruct(shape, bf16) for shape in shapes]
    else:
        outs = [jax.ShapeDtypeStruct((CHUNK, D), f32)] * n
    specs = [pl.BlockSpec(out.shape, lambda i, ids, order: (0, 0)) for out in outs]
    grid = pltpu.PrefetchScalarGridSpec(
        num_scalar_prefetch=2,
        grid=(n,),
        in_specs=[
            pl.BlockSpec((1, CHUNK, D), lambda i, ids, order: (order[i], 0, 0)),
            pl.BlockSpec((1, CHUNK, 128), lambda i, ids, order: (order[i], 0, 0)),
            pl.BlockSpec((D, CHUNK), lambda i, ids, order: (0, 2 * order[i] + ids[1])),
            whole,
            whole,
            pl.BlockSpec((8, BOTH), lambda i, ids, order: (0, 0)),
            pl.BlockSpec((EXTRA, D), lambda i, ids, order: (0, 0)),
        ],
        out_specs=specs + [pl.BlockSpec((D, BOTH), lambda i, ids, order: (0, 0))],
    )
    return pl.pallas_call(
        functools.partial(grad_kernel, n, split),
        grid_spec=grid,
        out_shape=outs + [jax.ShapeDtypeStruct((D, BOTH), f32)],
        compiler_params=params(),
        cost_estimate=cost(8 * BOTH * n * CHUNK * D, 3 << 20, 2 * BOTH * n * CHUNK),
    )(ids, order, turned, shifts, prototypes, mine, other, coef, misc)


def du_send_kernel(ids_ref, a, b, c, out_ref):
    total = (a[...] + b[...] + c[...]).astype(bf16)
    core = ids_ref[1]
    out_ref[core] = total[:, :ROWS]
    out_ref[1 - core] = total[:, ROWS:]


def du_sum_kernel(got_ref, out_ref):
    total = jnp.sum(got_ref[...].astype(f32), axis=0).astype(bf16)
    out_ref[...] = jnp.broadcast_to(total[None], (X * Y,) + total.shape)


def halves_kernel(offset, with_extra, far_ref, got_ref, misc_ref, out_ref):
    half = CHUNK // 2
    own = far_ref[...]
    for i in range(2):
        rows = slice(i * half, (i + 1) * half)
        part = own[rows]
        if i == offset:
            part = part + got_ref[:half, :].astype(f32)
        out_ref[rows, :] = part.astype(bf16)
    extra = misc_ref[...]
    if with_extra:
        extra = extra + got_ref[half:, :]
    out_ref[CHUNK:, :] = extra


def step_kernel(near_ref, got_ref, misc_ref, out_ref):
    out_ref[:CHUNK, :] = (near_ref[...] + got_ref[:CHUNK, :].astype(f32)).astype(bf16)
    out_ref[CHUNK:, :] = misc_ref[...] + got_ref[CHUNK:, :]


def finish_kernel(near_ref, up_ref, down_ref, misc_ref, p_ref, grad_ref, center_ref, loss_ref):
    @pl.when(pl.program_id(0) == 0)
    def _():
        grad_ref[...] = near_ref[...] + up_ref[:CHUNK, :].astype(f32) + down_ref[:CHUNK, :].astype(f32)

    extra = (misc_ref[...] + up_ref[CHUNK:, :] + down_ref[CHUNK:, :]).astype(f32)
    first = extra[0:8] + extra[8:16] + extra[16:24]
    loss = extra[24:32] + extra[32:40] + extra[40:48]
    total = jnp.broadcast_to(jnp.sum(first, axis=0, keepdims=True), (16, D))
    loss_ref[...] = jnp.broadcast_to(jnp.sum(loss, axis=0, keepdims=True), (8, D))
    stacked = jnp.concatenate(split3(total), axis=0)
    three = dot(stacked, p_ref[...])
    center_ref[...] = (three[0:1] + three[16:17] + three[32:33]) * (1.0 / TOTAL)


def finish(near, up, down, misc, prototypes):
    width = prototypes.shape[1]
    block = 2048
    rows = CHUNK + EXTRA
    return pl.pallas_call(
        finish_kernel,
        grid=(width // block,),
        in_specs=[
            pl.BlockSpec((CHUNK, D), lambda i: (0, 0)),
            pl.BlockSpec((rows, D), lambda i: (0, 0)),
            pl.BlockSpec((rows, D), lambda i: (0, 0)),
            pl.BlockSpec((EXTRA, D), lambda i: (0, 0)),
            pl.BlockSpec((D, block), lambda i: (0, i)),
        ],
        out_specs=[
            pl.BlockSpec((CHUNK, D), lambda i: (0, 0)),
            pl.BlockSpec((1, block), lambda i: (0, i)),
            pl.BlockSpec((8, D), lambda i: (0, 0)),
        ],
        out_shape=[
            jax.ShapeDtypeStruct((CHUNK, D), f32),
            jax.ShapeDtypeStruct((1, width), f32),
            jax.ShapeDtypeStruct((8, D), f32),
        ],
        compiler_params=params(),
        cost_estimate=cost(6 * 8 * D * width, 5 << 20),
    )(near, up, down, misc, prototypes)


def final_kernel(count_ref, index_ref, s_ref, du_ref, out_ref):
    for i in range(LOCAL):
        pick = picks(index_ref, count_ref[i], i)
        unit, length = unit_rows(dot(pick, s_ref[i], TN))
        d_unit = du_ref[:, i * SLOTS : (i + 1) * SLOTS].astype(f32).T
        row = (d_unit - unit * jnp.sum(unit * d_unit, axis=1, keepdims=True)) / length
        top = row.astype(bf16)
        rest = (row - top.astype(f32)).astype(bf16)
        out_ref[i] = dot(pick, top) + dot(pick, rest)


def shards(student_rows, teacher_rows, prototypes, center, mask_index, mask_count, loss_scale):
    z, core, x, y = (lax.axis_index(a) for a in ("z", "core", "x", "y"))
    ids = jnp.concatenate([jnp.stack([z, core, x, y]).astype(jnp.int32), mask_count])
    down = [(i, (i - 1) % Z) for i in range(Z)]
    up = [(i, (i + 1) % Z) for i in range(Z)]

    mine = prep(mask_count, mask_index, student_rows, teacher_rows)
    other = swap(mine, "core", CORES, 1)
    stats, row_sum, turned, shifts = local_stats(ids, prototypes, center, mine, other)

    shape = jax.ShapeDtypeStruct((8, BOTH), f32)
    stats = small_call(core_merge_kernel, shape, stats, swap(stats, "core", CORES, 1))
    stats = small_call(merge_kernel, shape, stats, *[swap(stats, "y", Y, k) for k in (1, 2, 3)])
    coef, misc = small_call(
        last_merge_kernel,
        [shape, jax.ShapeDtypeStruct((EXTRA, D), bf16)],
        loss_scale.reshape(1),
        ids,
        stats,
        *[swap(stats, "x", X, k) for k in (1, 2, 3)],
        row_sum,
        smem=(0, 1),
    )

    common = (turned, shifts, prototypes, mine, other, coef, misc)
    step_shape = jax.ShapeDtypeStruct((CHUNK + EXTRA, D), bf16)
    half_a, half_b, du_a = grads(ids, [4], True, *common)
    from_up = lax.ppermute(half_a, "z", down)
    from_down = lax.ppermute(half_b, "z", up)
    far_down, far_up, du_b = grads(ids, [-3, 3], False, *common)
    send_down = small_call(functools.partial(halves_kernel, 0, True), step_shape, far_down, from_up, misc)
    send_up = small_call(functools.partial(halves_kernel, 1, False), step_shape, far_up, from_down, misc)
    from_up = lax.ppermute(send_down, "z", down)
    from_down = lax.ppermute(send_up, "z", up)
    *near, du_c = grads(ids, [-2, 2, -1, 1, 0], False, *common)
    for i in (0, 2):
        send_down = small_call(step_kernel, step_shape, near[i], from_up, misc)
        send_up = small_call(step_kernel, step_shape, near[i + 1], from_down, misc)
        from_up = lax.ppermute(send_down, "z", down)
        from_down = lax.ppermute(send_up, "z", up)
    proto_grad, patch_center, loss = finish(near[4], from_up, from_down, misc, prototypes)

    send = small_call(
        du_send_kernel, jax.ShapeDtypeStruct((CORES, D, ROWS), bf16), ids, du_a, du_b, du_c, smem=(0,)
    )
    part = D // (X * Y)
    got = lax.all_to_all(send.reshape(CORES * X * Y, part, ROWS), ("core", "x", "y"), 0, 0)
    own = small_call(du_sum_kernel, jax.ShapeDtypeStruct((X * Y, part, ROWS), bf16), got)
    du = lax.all_to_all(own, ("x", "y"), 0, 0).reshape(D, ROWS)
    student_grad = small_call(
        final_kernel,
        jax.ShapeDtypeStruct(student_rows.shape, f32),
        mask_count, mask_index, student_rows, du,
        smem=(0,),
    )
    return (loss[0, 0], student_grad, proto_grad, patch_center.reshape(-1))


def solution(mesh):
    fine = Mesh(mesh.devices.reshape(Z, CORES, X, Y), ("z", "core", "x", "y"))
    dp, proto = ("z", "core"), ("x", "y")
    in_specs = (
        P(dp, None, None),
        P(dp, None, None),
        P(None, proto),
        P(proto),
        P(dp, None),
        P(dp),
        P(),
    )
    out_specs = (P(), P(dp, None, None), P(proto + dp, None), P(proto))
    return jax.shard_map(shards, mesh=fine, in_specs=in_specs, out_specs=out_specs, check_vma=False)
```

```python
import functools
import math

import jax
import jax.numpy as jnp
from jax import lax
from jax.experimental import pallas as pl
from jax.experimental.pallas import tpu as pltpu
from jax.sharding import Mesh, PartitionSpec as P

bf16 = jnp.bfloat16
f32 = jnp.float32
log2e = math.log2(math.e)
ln2 = math.log(2.0)
t_scale = log2e / 0.04
s_scale = log2e / 0.1
inverse_temp = 10.0
norm_epsilon = 1e-06
low = -1e30

Z, CORES, X, Y = 8, 2, 4, 4
D = 256
SLOTS = 128
IMAGES = 64
TOTAL = 4096
LOCAL = 4
ROWS = LOCAL * SLOTS
BOTH = 2 * ROWS
CHUNK = 512
TILE = 512
STAT_TILE = 256
EXTRA = 48
HELD = ROWS + 16
STATS = 5
PEERS = CORES * X * Y

NT = (((1,), (1,)), ((), ()))
TN = (((0,), (0,)), ((), ()))


def dot(a, b, dims=(((1,), (0,)), ((), ()))):
    return lax.dot_general(a, b, dims, preferred_element_type=f32)


def params():
    return pltpu.CompilerParams(vmem_limit_bytes=32 * 1024 * 1024)


def cost(flops, nbytes, trans=0):
    return pl.CostEstimate(flops=flops, bytes_accessed=nbytes, transcendentals=trans)


def picks(index_ref, count, i):
    patch = lax.broadcasted_iota(jnp.int32, (D, SLOTS), 0)
    slot = lax.broadcasted_iota(jnp.int32, (D, SLOTS), 1)
    hit = (patch == index_ref[i : i + 1, :]) & (slot < count)
    return jnp.where(hit, 1.0, 0.0).astype(bf16)


def unit_rows(values):
    length = jnp.sqrt(jnp.sum(values * values, axis=1, keepdims=True) + norm_epsilon)
    return values / length, length


def prep_kernel(count_ref, index_ref, s_ref, t_ref, out_ref):
    for i in range(LOCAL):
        pick = picks(index_ref, count_ref[i], i)
        for which, ref in enumerate((s_ref, t_ref)):
            unit, _ = unit_rows(dot(pick, ref[i], TN))
            out_ref[which, i * SLOTS : (i + 1) * SLOTS, :] = unit.astype(bf16)
    row = lax.broadcasted_iota(jnp.int32, (HELD - ROWS, D), 0)
    counts = jnp.zeros((HELD - ROWS, D), jnp.int32)
    for i in range(LOCAL):
        counts = jnp.where(row == i, count_ref[i], counts)
    for which in range(2):
        out_ref[which, ROWS:, :] = counts.astype(f32).astype(bf16)


def prep(count, index, student, teacher):
    smem = pl.BlockSpec(memory_space=pltpu.SMEM)
    vmem = pl.BlockSpec(memory_space=pltpu.VMEM)
    return pl.pallas_call(
        prep_kernel,
        out_shape=jax.ShapeDtypeStruct((2, HELD, D), bf16),
        in_specs=[smem, vmem, vmem, vmem],
        out_specs=vmem,
        compiler_params=params(),
        cost_estimate=cost(2 * 2 * ROWS * D * D, 1 << 21),
    )(count, index, student, teacher)


def wide(block, times):
    return jnp.concatenate([block] * times, axis=1)


def chunk_columns(i, core):
    return pl.ds(pl.multiple_of((CORES * i + core) * CHUNK, CHUNK), CHUNK)


def stats_kernel(ids_ref, p_ref, c_ref, mine_ref, other_ref, send_ref, sum_ref, pt_ref, cb_ref, acc, block):
    core = ids_ref[1]
    groups = (CHUNK // 8, 8, STAT_TILE)
    for i in range(Z):
        columns = chunk_columns(i, core)
        protos = p_ref[:, columns].T
        pt_ref[i] = protos
        column = jnp.broadcast_to(c_ref[:, columns] * -t_scale, (128, CHUNK)).T
        cb_ref[i] = column
        shift = wide(column, STAT_TILE // 128)
        for half, ref in enumerate((mine_ref, other_ref)):
            for j in range(ROWS // STAT_TILE):
                rows = slice(j * STAT_TILE, (j + 1) * STAT_TILE)
                at = slice(half * ROWS + j * STAT_TILE, half * ROWS + (j + 1) * STAT_TILE)
                t_arg = (dot(protos, ref[1, rows, :], NT) * t_scale + shift).reshape(groups)
                s_arg = (dot(protos, ref[0, rows, :], NT) * s_scale).reshape(groups)
                t_top = jnp.max(t_arg, axis=0)
                s_top = jnp.max(s_arg, axis=0)
                t_exp = jnp.exp2(t_arg - t_top[None])
                s_exp = jnp.exp2(s_arg - s_top[None])
                acc[0, i, :, at] = t_top
                acc[1, i, :, at] = jnp.sum(t_exp, axis=0)
                acc[2, i, :, at] = jnp.sum(t_exp * s_arg, axis=0)
                acc[3, i, :, at] = s_top
                acc[4, i, :, at] = jnp.sum(s_exp, axis=0)
    for g in range(BOTH // 128):
        at = slice(g * 128, (g + 1) * 128)
        parts = [acc[q, :, :, at].reshape(Z * 8, 128) for q in range(STATS)]
        t_top = jnp.max(parts[0], axis=0, keepdims=True)
        s_top = jnp.max(parts[3], axis=0, keepdims=True)
        t_keep = jnp.exp2(parts[0] - t_top)
        s_keep = jnp.exp2(parts[3] - s_top)
        merged_rows = (
            t_top,
            jnp.sum(parts[1] * t_keep, axis=0, keepdims=True),
            jnp.sum(parts[2] * t_keep, axis=0, keepdims=True),
            s_top,
            jnp.sum(parts[4] * s_keep, axis=0, keepdims=True),
        )
        for q in range(STATS):
            block[q * 8 + g : q * 8 + g + 1, :] = merged_rows[q]
    whole = block[...]
    for peer in range(PEERS):
        send_ref[peer] = whole
    first = jnp.sum(mine_ref[1, :ROWS, :].astype(f32), axis=0, keepdims=True)
    second = jnp.sum(other_ref[1, :ROWS, :].astype(f32), axis=0, keepdims=True)
    sum_ref[...] = jnp.broadcast_to(first + second, (8, D))


def local_stats(ids, prototypes, center, mine, other):
    smem = pl.BlockSpec(memory_space=pltpu.SMEM)
    vmem = pl.BlockSpec(memory_space=pltpu.VMEM)
    return pl.pallas_call(
        stats_kernel,
        in_specs=[smem, vmem, vmem, vmem, vmem],
        out_specs=[vmem] * 4,
        out_shape=[
            jax.ShapeDtypeStruct((PEERS, STATS * 8, 128), f32),
            jax.ShapeDtypeStruct((8, D), f32),
            jax.ShapeDtypeStruct((Z, CHUNK, D), bf16),
            jax.ShapeDtypeStruct((Z, CHUNK, 128), f32),
        ],
        scratch_shapes=[pltpu.VMEM((STATS, Z, 8, BOTH), f32), pltpu.VMEM((STATS * 8, 128), f32)],
        compiler_params=params(),
        cost_estimate=cost(4 * BOTH * Z * CHUNK * D, 6 << 20, 2 * BOTH * Z * CHUNK),
    )(ids, prototypes, center.reshape(1, -1), mine, other)


def split3(value):
    top = value.astype(bf16)
    rest = value - top.astype(f32)
    middle = rest.astype(bf16)
    return top, middle, (rest - middle.astype(f32)).astype(bf16)


def merge(parts):
    t_top = functools.reduce(jnp.maximum, [p[0] for p in parts])
    s_top = functools.reduce(jnp.maximum, [p[3] for p in parts])
    t_sum = cross = s_sum = 0.0
    for p in parts:
        t_keep = jnp.exp2(p[0] - t_top)
        t_sum = t_sum + p[1] * t_keep
        cross = cross + p[2] * t_keep
        s_sum = s_sum + p[4] * jnp.exp2(p[3] - s_top)
    return t_top, t_sum, cross, s_top, s_sum


def flip(value):
    return jnp.concatenate([value[LOCAL:], value[:LOCAL]], axis=0)


def merge_kernel(ids_ref, scale_ref, got_ref, mine_ref, other_ref, sum_ref, coef_ref, misc_ref):
    halves = []
    for core in range(CORES):
        parts = []
        for peer in range(core * X * Y, (core + 1) * X * Y):
            parts.append([got_ref[peer, q * 8 : (q + 1) * 8, :] for q in range(STATS)])
        halves.append(merge(parts))
    halves[1] = [flip(value) for value in halves[1]]
    here = ids_ref[1] == 0
    t_top, t_sum, cross, s_top, s_sum = [jnp.where(here, v, flip(v)) for v in merge(halves)]
    counts = [ref[0, ROWS:, :128].astype(f32)[:LOCAL] for ref in (mine_ref, other_ref)]
    count = jnp.concatenate(counts, axis=0)
    slot = lax.broadcasted_iota(jnp.int32, (8, 128), 1).astype(f32)
    live = slot < count
    weight = 1.0 / (IMAGES * jnp.maximum(count, 1.0))
    s_lse = s_top + jnp.log2(s_sum)
    ce = (s_lse - cross / t_sum) * ln2
    factor = jnp.log2(weight * (scale_ref[0] * inverse_temp))
    s_coef = jnp.where(live, factor - s_lse, low)
    t_coef = jnp.where(live, factor - t_top - jnp.log2(t_sum), low)
    for g in range(8):
        coef_ref[0:1, g * 128 : (g + 1) * 128] = s_coef[g : g + 1]
        coef_ref[1:2, g * 128 : (g + 1) * 128] = t_coef[g : g + 1]
    coef_ref[2:8, :] = jnp.zeros((6, BOTH), f32)
    part = jnp.sum(jnp.where(live, weight * ce, 0.0), axis=1, keepdims=True)
    first = jnp.sum(part[:LOCAL], axis=0, keepdims=True)
    second = jnp.sum(part[LOCAL:], axis=0, keepdims=True)
    row = lax.broadcasted_iota(jnp.int32, (EXTRA, D), 0)
    mine = jnp.bitwise_and(row, Z - 1) == ids_ref[0]
    row_sum = split3(sum_ref[0:1, :])
    losses = split3(jnp.broadcast_to(first + second, (1, D)))
    block = jnp.zeros((EXTRA, D), f32)
    for i in range(3):
        block = jnp.where(row // Z == i, row_sum[i].astype(f32), block)
        block = jnp.where(row // Z == 3 + i, losses[i].astype(f32), block)
    misc_ref[...] = jnp.where(mine, block, 0.0).astype(bf16)


def small_call(kernel, out_shape, *args, smem=()):
    specs = [
        pl.BlockSpec(memory_space=pltpu.SMEM if i in smem else pltpu.VMEM) for i in range(len(args))
    ]
    vmem = pl.BlockSpec(memory_space=pltpu.VMEM)
    return pl.pallas_call(
        kernel,
        out_shape=out_shape,
        in_specs=specs,
        out_specs=jax.tree.map(lambda _: vmem, out_shape),
        compiler_params=params(),
        cost_estimate=cost(1 << 20, 1 << 18),
    )(*args)


def grad_kernel(ids_ref, pt_ref, cb_ref, p_ref, mine_ref, other_ref, coef_ref, misc_ref, out_ref, send_ref, du_ref):
    core = ids_ref[1]
    for i in range(Z):
        protos = pt_ref[i]
        shift = wide(cb_ref[i], TILE // 128)
        wide_p = p_ref[:, chunk_columns(i, core)]
        total = None
        for half, ref in enumerate((mine_ref, other_ref)):
            for j in range(ROWS // TILE):
                rows = slice(j * TILE, (j + 1) * TILE)
                at = slice(half * ROWS + j * TILE, half * ROWS + (j + 1) * TILE)
                s_rows = ref[0, rows, :]
                t_arg = dot(protos, ref[1, rows, :], NT) * t_scale + shift + coef_ref[1:2, at]
                s_arg = dot(protos, s_rows, NT) * s_scale + coef_ref[0:1, at]
                dlogit = (jnp.exp2(s_arg) - jnp.exp2(t_arg)).astype(bf16)
                part = dot(dlogit, s_rows)
                total = part if total is None else total + part
                du = dot(wide_p, dlogit)
                if i == 0:
                    du_ref[:, at] = du
                else:
                    du_ref[:, at] += du
        out_ref[i, :CHUNK, :] = total.astype(bf16)
        out_ref[i, CHUNK:, :] = misc_ref[...]
    send_ref[core] = du_ref[:, :ROWS].astype(bf16)
    send_ref[1 - core] = du_ref[:, ROWS:].astype(bf16)


def grads(ids, turned, shifts, prototypes, mine, other, coef, misc):
    smem = pl.BlockSpec(memory_space=pltpu.SMEM)
    vmem = pl.BlockSpec(memory_space=pltpu.VMEM)
    return pl.pallas_call(
        grad_kernel,
        in_specs=[smem] + [vmem] * 7,
        out_specs=[vmem] * 2,
        out_shape=[
            jax.ShapeDtypeStruct((Z, CHUNK + EXTRA, D), bf16),
            jax.ShapeDtypeStruct((CORES, D, ROWS), bf16),
        ],
        scratch_shapes=[pltpu.VMEM((D, BOTH), f32)],
        compiler_params=params(),
        cost_estimate=cost(8 * BOTH * Z * CHUNK * D, 8 << 20, 2 * BOTH * Z * CHUNK),
    )(ids, turned, shifts, prototypes, mine, other, coef, misc)


def du_sum_kernel(got_ref, out_ref):
    total = jnp.sum(got_ref[...].astype(f32), axis=0).astype(bf16)
    out_ref[...] = jnp.broadcast_to(total[None], (X * Y,) + total.shape)


def finish_kernel(sum_ref, p_ref, grad_ref, center_ref, loss_ref):
    @pl.when(pl.program_id(0) == 0)
    def _():
        grad_ref[...] = sum_ref[:CHUNK, :].astype(f32)

    extra = sum_ref[CHUNK:, :].astype(f32)
    first = extra[0:8] + extra[8:16] + extra[16:24]
    loss = extra[24:32] + extra[32:40] + extra[40:48]
    total = jnp.broadcast_to(jnp.sum(first, axis=0, keepdims=True), (16, D))
    loss_ref[...] = jnp.broadcast_to(jnp.sum(loss, axis=0, keepdims=True), (8, D))
    stacked = jnp.concatenate(split3(total), axis=0)
    three = dot(stacked, p_ref[...])
    center_ref[...] = (three[0:1] + three[16:17] + three[32:33]) * (1.0 / TOTAL)


def finish(summed, prototypes):
    width = prototypes.shape[1]
    block = 2048
    return pl.pallas_call(
        finish_kernel,
        grid=(width // block,),
        in_specs=[
            pl.BlockSpec((CHUNK + EXTRA, D), lambda i: (0, 0)),
            pl.BlockSpec((D, block), lambda i: (0, i)),
        ],
        out_specs=[
            pl.BlockSpec((CHUNK, D), lambda i: (0, 0)),
            pl.BlockSpec((1, block), lambda i: (0, i)),
            pl.BlockSpec((8, D), lambda i: (0, 0)),
        ],
        out_shape=[
            jax.ShapeDtypeStruct((CHUNK, D), f32),
            jax.ShapeDtypeStruct((1, width), f32),
            jax.ShapeDtypeStruct((8, D), f32),
        ],
        compiler_params=params(),
        cost_estimate=cost(6 * 8 * D * width, 5 << 20),
    )(summed, prototypes)


def final_kernel(count_ref, index_ref, s_ref, du_ref, out_ref):
    for i in range(LOCAL):
        pick = picks(index_ref, count_ref[i], i)
        unit, length = unit_rows(dot(pick, s_ref[i], TN))
        d_unit = du_ref[:, i * SLOTS : (i + 1) * SLOTS].astype(f32).T
        row = (d_unit - unit * jnp.sum(unit * d_unit, axis=1, keepdims=True)) / length
        top = row.astype(bf16)
        rest = (row - top.astype(f32)).astype(bf16)
        out_ref[i] = dot(pick, top) + dot(pick, rest)


def shards(student_rows, teacher_rows, prototypes, center, mask_index, mask_count, loss_scale):
    z, core, x, y = (lax.axis_index(a) for a in ("z", "core", "x", "y"))
    ids = jnp.stack([z, core, x, y]).astype(jnp.int32)
    peers = ("core", "x", "y")

    mine = prep(mask_count, mask_index, student_rows, teacher_rows)
    other = lax.ppermute(mine, "core", [(0, 1), (1, 0)])
    stats, row_sum, turned, shifts = local_stats(ids, prototypes, center, mine, other)
    stats = lax.all_to_all(stats, peers, 0, 0)
    coef, misc = small_call(
        merge_kernel,
        [jax.ShapeDtypeStruct((8, BOTH), f32), jax.ShapeDtypeStruct((EXTRA, D), bf16)],
        ids, loss_scale.reshape(1), stats, mine, other, row_sum,
        smem=(0, 1),
    )
    parts, send = grads(ids, turned, shifts, prototypes, mine, other, coef, misc)
    summed = lax.psum_scatter(parts.reshape(-1, D), "z", scatter_dimension=0, tiled=True)
    proto_grad, patch_center, loss = finish(summed, prototypes)

    part = D // (X * Y)
    got = lax.all_to_all(send.reshape(PEERS, part, ROWS), peers, 0, 0)
    own = small_call(du_sum_kernel, jax.ShapeDtypeStruct((X * Y, part, ROWS), bf16), got)
    du = lax.all_to_all(own, ("x", "y"), 0, 0).reshape(D, ROWS)
    student_grad = small_call(
        final_kernel,
        jax.ShapeDtypeStruct(student_rows.shape, f32),
        mask_count, mask_index, student_rows, du,
        smem=(0,),
    )
    return (loss[0, 0], student_grad, proto_grad, patch_center.reshape(-1))


def solution(mesh):
    fine = Mesh(mesh.devices.reshape(Z, CORES, X, Y), ("z", "core", "x", "y"))
    dp, proto = ("z", "core"), ("x", "y")
    in_specs = (
        P(dp, None, None),
        P(dp, None, None),
        P(None, proto),
        P(proto),
        P(dp, None),
        P(dp),
        P(),
    )
    out_specs = (P(), P(dp, None, None), P(proto + dp, None), P(proto))
    return jax.shard_map(shards, mesh=fine, in_specs=in_specs, out_specs=out_specs, check_vma=False)
```

```python
import functools
import math

import jax
import jax.numpy as jnp
from jax import lax
from jax.experimental import pallas as pl
from jax.experimental.pallas import tpu as pltpu
from jax.sharding import Mesh, PartitionSpec as P

bf16 = jnp.bfloat16
f32 = jnp.float32
log2e = math.log2(math.e)
ln2 = math.log(2.0)
t_scale = log2e / 0.04
s_scale = log2e / 0.1
inverse_temp = 10.0
norm_epsilon = 1e-06
low = -1e30

Z, CORES, X, Y = 8, 2, 4, 4
D = 256
SLOTS = 128
IMAGES = 64
TOTAL = 4096
LOCAL = 4
ROWS = LOCAL * SLOTS
BOTH = 2 * ROWS
CHUNK = 512
TILE = 512
STAT_TILE = 256
EXTRA = 48
HELD = ROWS + 16
STATS = 5
PEERS = CORES * X * Y

NT = (((1,), (1,)), ((), ()))
TN = (((0,), (0,)), ((), ()))


def dot(a, b, dims=(((1,), (0,)), ((), ()))):
    return lax.dot_general(a, b, dims, preferred_element_type=f32)


def params(mebibytes=32):
    return pltpu.CompilerParams(vmem_limit_bytes=mebibytes * 1024 * 1024)


def cost(flops, nbytes, trans=0):
    return pl.CostEstimate(flops=flops, bytes_accessed=nbytes, transcendentals=trans)


def picks(index_ref, count, i):
    patch = lax.broadcasted_iota(jnp.int32, (D, SLOTS), 0)
    slot = lax.broadcasted_iota(jnp.int32, (D, SLOTS), 1)
    hit = (patch == index_ref[i : i + 1, :]) & (slot < count)
    return jnp.where(hit, 1.0, 0.0).astype(bf16)


def unit_rows(values):
    length = jnp.sqrt(jnp.sum(values * values, axis=1, keepdims=True) + norm_epsilon)
    return values / length, length


def prep_kernel(count_ref, index_ref, s_ref, t_ref, out_ref):
    for i in range(LOCAL):
        pick = picks(index_ref, count_ref[i], i)
        for which, ref in enumerate((s_ref, t_ref)):
            unit, _ = unit_rows(dot(pick, ref[i], TN))
            out_ref[which, i * SLOTS : (i + 1) * SLOTS, :] = unit.astype(bf16)
    row = lax.broadcasted_iota(jnp.int32, (HELD - ROWS, D), 0)
    counts = jnp.zeros((HELD - ROWS, D), jnp.int32)
    for i in range(LOCAL):
        counts = jnp.where(row == i, count_ref[i], counts)
    for which in range(2):
        out_ref[which, ROWS:, :] = counts.astype(f32).astype(bf16)


def prep(count, index, student, teacher):
    smem = pl.BlockSpec(memory_space=pltpu.SMEM)
    vmem = pl.BlockSpec(memory_space=pltpu.VMEM)
    return pl.pallas_call(
        prep_kernel,
        out_shape=jax.ShapeDtypeStruct((2, HELD, D), bf16),
        in_specs=[smem, vmem, vmem, vmem],
        out_specs=vmem,
        compiler_params=params(),
        cost_estimate=cost(2 * 2 * ROWS * D * D, 1 << 21),
    )(count, index, student, teacher)


def wide(block, times):
    return jnp.concatenate([block] * times, axis=1)


def chunk_columns(i, core):
    return pl.ds(pl.multiple_of((CORES * i + core) * CHUNK, CHUNK), CHUNK)


def fetch(order, core, p_ref, c_ref, p_held, c_held, p_sem, c_sem):
    copies = []
    for i, chunk in enumerate(order):
        columns = chunk_columns(chunk, core)
        pair = (
            pltpu.make_async_copy(p_ref.at[:, columns], p_held.at[i], p_sem.at[i]),
            pltpu.make_async_copy(c_ref.at[:, columns], c_held.at[i], c_sem.at[i]),
        )
        for copy in pair:
            copy.start()
        copies.append(pair)
    return copies


def fetch_scratch(n):
    return [
        pltpu.VMEM((n, D, CHUNK), bf16),
        pltpu.VMEM((n, 1, CHUNK), f32),
        pltpu.SemaphoreType.DMA((n,)),
        pltpu.SemaphoreType.DMA((n,)),
    ]


def turned(held):
    return jnp.broadcast_to(held * -t_scale, (128, CHUNK)).T


def stats_kernel(ids_ref, p_ref, c_ref, mine_ref, other_ref, block, sum_ref, acc, p_held, c_held, p_sem, c_sem):
    groups = (CHUNK // 8, 8, STAT_TILE)
    copies = fetch(range(Z), ids_ref[1], p_ref, c_ref, p_held, c_held, p_sem, c_sem)
    for i in range(Z):
        for copy in copies[i]:
            copy.wait()
        protos = p_held[i].T
        shift = wide(turned(c_held[i]), STAT_TILE // 128)
        for half, ref in enumerate((mine_ref, other_ref)):
            for j in range(ROWS // STAT_TILE):
                rows = slice(j * STAT_TILE, (j + 1) * STAT_TILE)
                at = slice(half * ROWS + j * STAT_TILE, half * ROWS + (j + 1) * STAT_TILE)
                t_arg = (dot(protos, ref[1, rows, :], NT) * t_scale + shift).reshape(groups)
                s_arg = (dot(protos, ref[0, rows, :], NT) * s_scale).reshape(groups)
                t_top = jnp.max(t_arg, axis=0)
                s_top = jnp.max(s_arg, axis=0)
                t_exp = jnp.exp2(t_arg - t_top[None])
                s_exp = jnp.exp2(s_arg - s_top[None])
                acc[0, i, :, at] = t_top
                acc[1, i, :, at] = jnp.sum(t_exp, axis=0)
                acc[2, i, :, at] = jnp.sum(t_exp * s_arg, axis=0)
                acc[3, i, :, at] = s_top
                acc[4, i, :, at] = jnp.sum(s_exp, axis=0)
    for g in range(BOTH // 128):
        at = slice(g * 128, (g + 1) * 128)
        parts = [acc[q, :, :, at].reshape(Z * 8, 128) for q in range(STATS)]
        t_top = jnp.max(parts[0], axis=0, keepdims=True)
        s_top = jnp.max(parts[3], axis=0, keepdims=True)
        t_keep = jnp.exp2(parts[0] - t_top)
        s_keep = jnp.exp2(parts[3] - s_top)
        merged_rows = (
            t_top,
            jnp.sum(parts[1] * t_keep, axis=0, keepdims=True),
            jnp.sum(parts[2] * t_keep, axis=0, keepdims=True),
            s_top,
            jnp.sum(parts[4] * s_keep, axis=0, keepdims=True),
        )
        for q in range(STATS):
            block[q * 8 + g : q * 8 + g + 1, :] = merged_rows[q]
    first = jnp.sum(mine_ref[1, :ROWS, :].astype(f32), axis=0, keepdims=True)
    second = jnp.sum(other_ref[1, :ROWS, :].astype(f32), axis=0, keepdims=True)
    sum_ref[...] = jnp.broadcast_to(first + second, (8, D))


def local_stats(ids, prototypes, center, mine, other):
    smem = pl.BlockSpec(memory_space=pltpu.SMEM)
    vmem = pl.BlockSpec(memory_space=pltpu.VMEM)
    anywhere = pl.BlockSpec(memory_space=pl.ANY)
    return pl.pallas_call(
        stats_kernel,
        in_specs=[smem, anywhere, anywhere, vmem, vmem],
        out_specs=[vmem] * 2,
        out_shape=[jax.ShapeDtypeStruct((STATS * 8, 128), f32), jax.ShapeDtypeStruct((8, D), f32)],
        scratch_shapes=[pltpu.VMEM((STATS, Z, 8, BOTH), f32)] + fetch_scratch(Z),
        compiler_params=params(58),
        cost_estimate=cost(4 * BOTH * Z * CHUNK * D, 6 << 20, 2 * BOTH * Z * CHUNK),
    )(ids, prototypes, center, mine, other)


def split3(value):
    top = value.astype(bf16)
    rest = value - top.astype(f32)
    middle = rest.astype(bf16)
    return top, middle, (rest - middle.astype(f32)).astype(bf16)


def tree(parts):
    while len(parts) > 1:
        parts = [parts[i] + parts[i + 1] for i in range(0, len(parts), 2)]
    return parts[0]


def merge(parts):
    t_top = functools.reduce(jnp.maximum, [p[0] for p in parts])
    s_top = functools.reduce(jnp.maximum, [p[3] for p in parts])
    t_keep = [jnp.exp2(p[0] - t_top) for p in parts]
    s_keep = [jnp.exp2(p[3] - s_top) for p in parts]
    t_sum = tree([p[1] * k for p, k in zip(parts, t_keep)])
    cross = tree([p[2] * k for p, k in zip(parts, t_keep)])
    s_sum = tree([p[4] * k for p, k in zip(parts, s_keep)])
    return t_top, t_sum, cross, s_top, s_sum


def flip(value):
    return jnp.concatenate([value[LOCAL:], value[:LOCAL]], axis=0)


def rows_of(ref):
    return [ref[q * 8 : (q + 1) * 8, :] for q in range(STATS)]


def core_merge_kernel(mine_ref, got_ref, out_ref):
    parts = [rows_of(mine_ref), [flip(value) for value in rows_of(got_ref)]]
    for q, value in enumerate(merge(parts)):
        out_ref[q * 8 : (q + 1) * 8, :] = value


def y_merge_kernel(a, b, c, d, out_ref):
    for q, value in enumerate(merge([rows_of(ref) for ref in (a, b, c, d)])):
        out_ref[q * 8 : (q + 1) * 8, :] = value


def x_merge_kernel(ids_ref, scale_ref, a, b, c, d, mine_ref, other_ref, sum_ref, coef_ref, misc_ref):
    t_top, t_sum, cross, s_top, s_sum = merge([rows_of(ref) for ref in (a, b, c, d)])
    counts = [ref[0, ROWS:, :128].astype(f32)[:LOCAL] for ref in (mine_ref, other_ref)]
    count = jnp.concatenate(counts, axis=0)
    slot = lax.broadcasted_iota(jnp.int32, (8, 128), 1).astype(f32)
    live = slot < count
    weight = 1.0 / (IMAGES * jnp.maximum(count, 1.0))
    s_lse = s_top + jnp.log2(s_sum)
    ce = (s_lse - cross / t_sum) * ln2
    factor = jnp.log2(weight * (scale_ref[0] * inverse_temp))
    s_coef = jnp.where(live, factor - s_lse, low)
    t_coef = jnp.where(live, factor - t_top - jnp.log2(t_sum), low)
    for g in range(8):
        coef_ref[0:1, g * 128 : (g + 1) * 128] = s_coef[g : g + 1]
        coef_ref[1:2, g * 128 : (g + 1) * 128] = t_coef[g : g + 1]
    coef_ref[2:8, :] = jnp.zeros((6, BOTH), f32)
    part = jnp.sum(jnp.where(live, weight * ce, 0.0), axis=1, keepdims=True)
    first = jnp.sum(part[:LOCAL], axis=0, keepdims=True)
    second = jnp.sum(part[LOCAL:], axis=0, keepdims=True)
    row = lax.broadcasted_iota(jnp.int32, (EXTRA, D), 0)
    mine = jnp.bitwise_and(row, Z - 1) == ids_ref[0]
    row_sum = split3(sum_ref[0:1, :])
    losses = split3(jnp.broadcast_to(first + second, (1, D)))
    block = jnp.zeros((EXTRA, D), f32)
    for i in range(3):
        block = jnp.where(row // Z == i, row_sum[i].astype(f32), block)
        block = jnp.where(row // Z == 3 + i, losses[i].astype(f32), block)
    misc_ref[...] = jnp.where(mine, block, 0.0).astype(bf16)


def small_call(kernel, out_shape, *args, smem=()):
    specs = [
        pl.BlockSpec(memory_space=pltpu.SMEM if i in smem else pltpu.VMEM) for i in range(len(args))
    ]
    vmem = pl.BlockSpec(memory_space=pltpu.VMEM)
    return pl.pallas_call(
        kernel,
        out_shape=out_shape,
        in_specs=specs,
        out_specs=jax.tree.map(lambda _: vmem, out_shape),
        compiler_params=params(),
        cost_estimate=cost(1 << 20, 1 << 18),
    )(*args)


def grad_kernel(n, first, last, *refs):
    ids_ref, order_ref, p_ref, c_ref, mine_ref, other_ref, coef_ref, misc_ref = refs[:8]
    refs = refs[8:]
    if not first:
        given_ref, refs = refs[0], refs[1:]
    outs, refs = refs[: 2 if first else n], refs[2 if first else n :]
    out_du, refs = refs[0], refs[1:]
    if last:
        du_ref, refs = refs[0], refs[1:]
    else:
        du_ref = out_du
    core = ids_ref[1]
    copies = fetch([order_ref[i] for i in range(n)], core, p_ref, c_ref, *refs)
    p_held, c_held = refs[:2]
    for i in range(n):
        for copy in copies[i]:
            copy.wait()
        wide_p = p_held[i]
        protos = wide_p.T
        shift = wide(turned(c_held[i]), TILE // 128)
        total = None
        for half, ref in enumerate((mine_ref, other_ref)):
            for j in range(ROWS // TILE):
                rows = slice(j * TILE, (j + 1) * TILE)
                at = slice(half * ROWS + j * TILE, half * ROWS + (j + 1) * TILE)
                s_rows = ref[0, rows, :]
                t_arg = dot(protos, ref[1, rows, :], NT) * t_scale + shift + coef_ref[1:2, at]
                s_arg = dot(protos, s_rows, NT) * s_scale + coef_ref[0:1, at]
                dlogit = (jnp.exp2(s_arg) - jnp.exp2(t_arg)).astype(bf16)
                part = dot(dlogit, s_rows)
                total = part if total is None else total + part
                du = dot(wide_p, dlogit)
                if i > 0:
                    du_ref[:, at] += du
                elif first:
                    du_ref[:, at] = du
                else:
                    du_ref[:, at] = given_ref[:, at] + du
        if first:
            half = CHUNK // 2
            outs[0][:half, :] = total[:half].astype(bf16)
            outs[0][half:, :] = misc_ref[...]
            outs[1][...] = total[half:].astype(bf16)
        else:
            outs[i][...] = total
    if last:
        out_du[core] = du_ref[:, :ROWS].astype(bf16)
        out_du[1 - core] = du_ref[:, ROWS:].astype(bf16)


def grads(ids, order, first, last, prototypes, center, mine, other, coef, misc, given=None):
    smem = pl.BlockSpec(memory_space=pltpu.SMEM)
    vmem = pl.BlockSpec(memory_space=pltpu.VMEM)
    anywhere = pl.BlockSpec(memory_space=pl.ANY)
    n = order.shape[0]
    if first:
        shapes = [(CHUNK // 2 + EXTRA, D), (CHUNK // 2, D)]
        outs = [jax.ShapeDtypeStruct(shape, bf16) for shape in shapes]
    else:
        outs = [jax.ShapeDtypeStruct((CHUNK, D), f32)] * n
    if last:
        outs.append(jax.ShapeDtypeStruct((CORES, D, ROWS), bf16))
    else:
        outs.append(jax.ShapeDtypeStruct((D, BOTH), f32))
    args = [ids, order, prototypes, center, mine, other, coef, misc]
    args += [] if first else [given]
    return pl.pallas_call(
        functools.partial(grad_kernel, n, first, last),
        in_specs=[smem, smem, anywhere, anywhere] + [vmem] * (len(args) - 4),
        out_specs=[vmem] * len(outs),
        out_shape=outs,
        scratch_shapes=([pltpu.VMEM((D, BOTH), f32)] if last else []) + fetch_scratch(n),
        compiler_params=params(58),
        cost_estimate=cost(8 * BOTH * n * CHUNK * D, n << 20, 2 * BOTH * n * CHUNK),
    )(*args)


def du_sum_kernel(got_ref, out_ref):
    total = jnp.sum(got_ref[...].astype(f32), axis=0).astype(bf16)
    out_ref[...] = jnp.broadcast_to(total[None], (X * Y,) + total.shape)


def halves_kernel(offset, with_extra, far_ref, got_ref, misc_ref, out_ref):
    half = CHUNK // 2
    for i in range(2):
        rows = slice(i * half, (i + 1) * half)
        part = far_ref[rows, :]
        if i == offset:
            part = part + got_ref[:half, :].astype(f32)
        out_ref[rows, :] = part.astype(bf16)
    extra = misc_ref[...]
    if with_extra:
        extra = extra + got_ref[half:, :]
    out_ref[CHUNK:, :] = extra


def step_kernel(near_ref, got_ref, misc_ref, out_ref):
    out_ref[:CHUNK, :] = (near_ref[...] + got_ref[:CHUNK, :].astype(f32)).astype(bf16)
    out_ref[CHUNK:, :] = misc_ref[...] + got_ref[CHUNK:, :]


def finish_kernel(near_ref, a_ref, b_ref, misc_ref, p_ref, grad_ref, center_ref, loss_ref):
    @pl.when(pl.program_id(0) == 0)
    def _():
        grad_ref[...] = near_ref[...] + a_ref[:CHUNK, :].astype(f32) + b_ref[:CHUNK, :].astype(f32)

    extra = (misc_ref[...] + a_ref[CHUNK:, :] + b_ref[CHUNK:, :]).astype(f32)
    first = extra[0:8] + extra[8:16] + extra[16:24]
    loss = extra[24:32] + extra[32:40] + extra[40:48]
    total = jnp.broadcast_to(jnp.sum(first, axis=0, keepdims=True), (16, D))
    loss_ref[...] = jnp.broadcast_to(jnp.sum(loss, axis=0, keepdims=True), (8, D))
    stacked = jnp.concatenate(split3(total), axis=0)
    three = dot(stacked, p_ref[...])
    center_ref[...] = (three[0:1] + three[16:17] + three[32:33]) * (1.0 / TOTAL)


def finish(near, a, b, misc, prototypes):
    width = prototypes.shape[1]
    block = 2048
    return pl.pallas_call(
        finish_kernel,
        grid=(width // block,),
        in_specs=[
            pl.BlockSpec((CHUNK, D), lambda i: (0, 0)),
            pl.BlockSpec((CHUNK + EXTRA, D), lambda i: (0, 0)),
            pl.BlockSpec((CHUNK + EXTRA, D), lambda i: (0, 0)),
            pl.BlockSpec((EXTRA, D), lambda i: (0, 0)),
            pl.BlockSpec((D, block), lambda i: (0, i)),
        ],
        out_specs=[
            pl.BlockSpec((CHUNK, D), lambda i: (0, 0)),
            pl.BlockSpec((1, block), lambda i: (0, i)),
            pl.BlockSpec((8, D), lambda i: (0, 0)),
        ],
        out_shape=[
            jax.ShapeDtypeStruct((CHUNK, D), f32),
            jax.ShapeDtypeStruct((1, width), f32),
            jax.ShapeDtypeStruct((8, D), f32),
        ],
        compiler_params=params(58),
        cost_estimate=cost(6 * 8 * D * width, 5 << 20),
    )(near, a, b, misc, prototypes)


def final_kernel(count_ref, index_ref, s_ref, du_ref, out_ref):
    for i in range(LOCAL):
        pick = picks(index_ref, count_ref[i], i)
        unit, length = unit_rows(dot(pick, s_ref[i], TN))
        d_unit = du_ref[:, i * SLOTS : (i + 1) * SLOTS].astype(f32).T
        row = (d_unit - unit * jnp.sum(unit * d_unit, axis=1, keepdims=True)) / length
        top = row.astype(bf16)
        rest = (row - top.astype(f32)).astype(bf16)
        out_ref[i] = dot(pick, top) + dot(pick, rest)


def shards(student_rows, teacher_rows, prototypes, center, mask_index, mask_count, loss_scale):
    z, core, x, y = (lax.axis_index(a) for a in ("z", "core", "x", "y"))
    ids = jnp.stack([z, core, x, y]).astype(jnp.int32)
    peers = ("core", "x", "y")
    ahead = 1 - 2 * core
    one_way, other_way = [], []
    for i in range(Z):
        below, above, here = (i - 1) % Z * CORES, (i + 1) % Z * CORES, i * CORES
        one_way += [(here, below), (here + 1, above + 1)]
        other_way += [(here, above), (here + 1, below + 1)]

    def swaps(value, axis):
        return [lax.ppermute(value, axis, [(i, i ^ k) for i in range(4)]) for k in (1, 2, 3)]

    def chunks(offsets):
        return lax.rem(z + Z + jnp.stack([d * ahead for d in offsets]), Z).astype(jnp.int32)

    def ring(value, pairs):
        return lax.ppermute(value, ("z", "core"), pairs)

    mine = prep(mask_count, mask_index, student_rows, teacher_rows)
    other = lax.ppermute(mine, "core", [(0, 1), (1, 0)])
    center = center.reshape(1, -1)
    stats, row_sum = local_stats(ids, prototypes, center, mine, other)
    shape = jax.ShapeDtypeStruct((STATS * 8, 128), f32)
    stats = small_call(core_merge_kernel, shape, stats, lax.ppermute(stats, "core", [(0, 1), (1, 0)]))
    stats = small_call(y_merge_kernel, shape, stats, *swaps(stats, "y"))
    coef, misc = small_call(
        x_merge_kernel,
        [jax.ShapeDtypeStruct((8, BOTH), f32), jax.ShapeDtypeStruct((EXTRA, D), bf16)],
        ids, loss_scale.reshape(1), stats, *swaps(stats, "x"), mine, other, row_sum,
        smem=(0, 1),
    )

    common = (prototypes, center, mine, other, coef, misc)
    step_shape = jax.ShapeDtypeStruct((CHUNK + EXTRA, D), bf16)
    half_a, half_b, du = grads(ids, chunks([4]), True, False, *common)
    got_a, got_b = ring(half_a, one_way), ring(half_b, other_way)
    far_a, far_b, du = grads(ids, chunks([-3, 3]), False, False, *common, du)
    send_a = small_call(functools.partial(halves_kernel, 0, True), step_shape, far_a, got_a, misc)
    send_b = small_call(functools.partial(halves_kernel, 1, False), step_shape, far_b, got_b, misc)
    got_a, got_b = ring(send_a, one_way), ring(send_b, other_way)
    *near, send = grads(ids, chunks([-2, 2, -1, 1, 0]), False, True, *common, du)
    send_a = small_call(step_kernel, step_shape, near[0], got_a, misc)
    send_b = small_call(step_kernel, step_shape, near[1], got_b, misc)
    send_a, send_b, send = lax.optimization_barrier((send_a, send_b, send))
    got_a, got_b = ring(send_a, one_way), ring(send_b, other_way)
    send_a = small_call(step_kernel, step_shape, near[2], got_a, misc)
    send_b = small_call(step_kernel, step_shape, near[3], got_b, misc)
    got_a, got_b = ring(send_a, one_way), ring(send_b, other_way)
    proto_grad, patch_center, loss = finish(near[4], got_a, got_b, misc, prototypes)

    part = D // (X * Y)
    got = lax.all_to_all(send.reshape(PEERS, part, ROWS), peers, 0, 0)
    own = small_call(du_sum_kernel, jax.ShapeDtypeStruct((X * Y, part, ROWS), bf16), got)
    du = lax.all_to_all(own, ("x", "y"), 0, 0).reshape(D, ROWS)
    student_grad = small_call(
        final_kernel,
        jax.ShapeDtypeStruct(student_rows.shape, f32),
        mask_count, mask_index, student_rows, du,
        smem=(0,),
    )
    return (loss[0, 0], student_grad, proto_grad, patch_center.reshape(-1))


def solution(mesh):
    fine = Mesh(mesh.devices.reshape(Z, CORES, X, Y), ("z", "core", "x", "y"))
    dp, proto = ("z", "core"), ("x", "y")
    in_specs = (
        P(dp, None, None),
        P(dp, None, None),
        P(None, proto),
        P(proto),
        P(dp, None),
        P(dp),
        P(),
    )
    out_specs = (P(), P(dp, None, None), P(proto + dp, None), P(proto))
    return jax.shard_map(shards, mesh=fine, in_specs=in_specs, out_specs=out_specs, check_vma=False)
```

```python
import functools
import math

import jax
import jax.numpy as jnp
from jax import lax
from jax.experimental import pallas as pl
from jax.experimental.pallas import tpu as pltpu
from jax.sharding import Mesh, PartitionSpec as P

bf16 = jnp.bfloat16
f32 = jnp.float32
log2e = math.log2(math.e)
ln2 = math.log(2.0)
t_scale = log2e / 0.04
s_scale = log2e / 0.1
inverse_temp = 10.0
norm_epsilon = 1e-06
low = -1e30

Z, CORES, X, Y = 8, 2, 4, 4
D = 256
SLOTS = 128
IMAGES = 64
TOTAL = 4096
LOCAL = 4
ROWS = LOCAL * SLOTS
BOTH = 2 * ROWS
CHUNK = 512
TILE = 512
STAT_TILE = 256
EXTRA = 48
HELD = ROWS + 16
STATS = 5
PEERS = CORES * X * Y
OFFSETS = (4, -3, 3, -2, 2, -1, 1, 0)
PIECES = 4

NT = (((1,), (1,)), ((), ()))
TN = (((0,), (0,)), ((), ()))


def dot(a, b, dims=(((1,), (0,)), ((), ()))):
    return lax.dot_general(a, b, dims, preferred_element_type=f32)


def params(mebibytes=32):
    return pltpu.CompilerParams(vmem_limit_bytes=mebibytes * 1024 * 1024)


def cost(flops, nbytes, trans=0):
    return pl.CostEstimate(flops=flops, bytes_accessed=nbytes, transcendentals=trans)


def picks(index_ref, count, i):
    patch = lax.broadcasted_iota(jnp.int32, (D, SLOTS), 0)
    slot = lax.broadcasted_iota(jnp.int32, (D, SLOTS), 1)
    hit = (patch == index_ref[i : i + 1, :]) & (slot < count)
    return jnp.where(hit, 1.0, 0.0).astype(bf16)


def unit_rows(values):
    length = jnp.sqrt(jnp.sum(values * values, axis=1, keepdims=True) + norm_epsilon)
    return values / length, length


def prep_kernel(count_ref, index_ref, s_ref, t_ref, out_ref, held, sems):
    copies = []
    for i in range(LOCAL):
        for which, ref in enumerate((s_ref, t_ref)):
            copy = pltpu.make_async_copy(ref.at[i], held.at[which, i], sems.at[which, i])
            copy.start()
            copies.append(copy)
    row = lax.broadcasted_iota(jnp.int32, (HELD - ROWS, D), 0)
    counts = jnp.zeros((HELD - ROWS, D), jnp.int32)
    for i in range(LOCAL):
        counts = jnp.where(row == i, count_ref[i], counts)
    for which in range(2):
        out_ref[which, ROWS:, :] = counts.astype(f32).astype(bf16)
    for i in range(LOCAL):
        pick = picks(index_ref, count_ref[i], i)
        for which in range(2):
            copies[2 * i + which].wait()
            unit, _ = unit_rows(dot(pick, held[which, i], TN))
            out_ref[which, i * SLOTS : (i + 1) * SLOTS, :] = unit.astype(bf16)


def prep(count, index, student, teacher):
    smem = pl.BlockSpec(memory_space=pltpu.SMEM)
    vmem = pl.BlockSpec(memory_space=pltpu.VMEM)
    anywhere = pl.BlockSpec(memory_space=pl.ANY)
    return pl.pallas_call(
        prep_kernel,
        out_shape=jax.ShapeDtypeStruct((2, HELD, D), bf16),
        in_specs=[smem, vmem, anywhere, anywhere],
        out_specs=vmem,
        scratch_shapes=[pltpu.VMEM((2, LOCAL, D, D), bf16), pltpu.SemaphoreType.DMA((2, LOCAL))],
        compiler_params=params(58),
        cost_estimate=cost(2 * 2 * ROWS * D * D, 1 << 21),
    )(count, index, student, teacher)


def wide(block, times):
    return jnp.concatenate([block] * times, axis=1)


def chunk_columns(i, core):
    return pl.ds(pl.multiple_of((CORES * i + core) * CHUNK, CHUNK), CHUNK)


def fetch(order, core, p_ref, c_ref, p_held, c_held, p_sem, c_sem):
    copies = []
    for i, chunk in enumerate(order):
        columns = chunk_columns(chunk, core)
        pair = (
            pltpu.make_async_copy(p_ref.at[:, columns], p_held.at[i], p_sem.at[i]),
            pltpu.make_async_copy(c_ref.at[:, columns], c_held.at[i], c_sem.at[i]),
        )
        for copy in pair:
            copy.start()
        copies.append(pair)
    return copies


def fetch_scratch(n):
    return [
        pltpu.VMEM((n, D, CHUNK), bf16),
        pltpu.VMEM((n, 1, CHUNK), f32),
        pltpu.SemaphoreType.DMA((n,)),
        pltpu.SemaphoreType.DMA((n,)),
    ]


def turned(held):
    return jnp.broadcast_to(held * -t_scale, (128, CHUNK)).T


def stats_kernel(ids_ref, p_ref, c_ref, mine_ref, other_ref, block, sum_ref, acc, p_held, c_held, p_sem, c_sem):
    groups = (CHUNK // 8, 8, STAT_TILE)
    copies = fetch(range(Z), ids_ref[1], p_ref, c_ref, p_held, c_held, p_sem, c_sem)
    for i in range(Z):
        for copy in copies[i]:
            copy.wait()
        protos = p_held[i].T
        shift = wide(turned(c_held[i]), STAT_TILE // 128)
        for half, ref in enumerate((mine_ref, other_ref)):
            for j in range(ROWS // STAT_TILE):
                rows = slice(j * STAT_TILE, (j + 1) * STAT_TILE)
                at = slice(half * ROWS + j * STAT_TILE, half * ROWS + (j + 1) * STAT_TILE)
                t_arg = (dot(protos, ref[1, rows, :], NT) * t_scale + shift).reshape(groups)
                s_arg = (dot(protos, ref[0, rows, :], NT) * s_scale).reshape(groups)
                t_top = jnp.max(t_arg, axis=0)
                s_top = jnp.max(s_arg, axis=0)
                t_exp = jnp.exp2(t_arg - t_top[None])
                s_exp = jnp.exp2(s_arg - s_top[None])
                acc[0, i, :, at] = t_top
                acc[1, i, :, at] = jnp.sum(t_exp, axis=0)
                acc[2, i, :, at] = jnp.sum(t_exp * s_arg, axis=0)
                acc[3, i, :, at] = s_top
                acc[4, i, :, at] = jnp.sum(s_exp, axis=0)
    for g in range(BOTH // 128):
        at = slice(g * 128, (g + 1) * 128)
        parts = [acc[q, :, :, at].reshape(Z * 8, 128) for q in range(STATS)]
        t_top = jnp.max(parts[0], axis=0, keepdims=True)
        s_top = jnp.max(parts[3], axis=0, keepdims=True)
        t_keep = jnp.exp2(parts[0] - t_top)
        s_keep = jnp.exp2(parts[3] - s_top)
        merged_rows = (
            t_top,
            jnp.sum(parts[1] * t_keep, axis=0, keepdims=True),
            jnp.sum(parts[2] * t_keep, axis=0, keepdims=True),
            s_top,
            jnp.sum(parts[4] * s_keep, axis=0, keepdims=True),
        )
        for q in range(STATS):
            block[q * 8 + g : q * 8 + g + 1, :] = merged_rows[q]
    first = jnp.sum(mine_ref[1, :ROWS, :].astype(f32), axis=0, keepdims=True)
    second = jnp.sum(other_ref[1, :ROWS, :].astype(f32), axis=0, keepdims=True)
    sum_ref[...] = jnp.broadcast_to(first + second, (8, D))


def local_stats(ids, prototypes, center, mine, other):
    smem = pl.BlockSpec(memory_space=pltpu.SMEM)
    vmem = pl.BlockSpec(memory_space=pltpu.VMEM)
    anywhere = pl.BlockSpec(memory_space=pl.ANY)
    return pl.pallas_call(
        stats_kernel,
        in_specs=[smem, anywhere, anywhere, vmem, vmem],
        out_specs=[vmem] * 2,
        out_shape=[jax.ShapeDtypeStruct((STATS * 8, 128), f32), jax.ShapeDtypeStruct((8, D), f32)],
        scratch_shapes=[pltpu.VMEM((STATS, Z, 8, BOTH), f32)] + fetch_scratch(Z),
        compiler_params=params(),
        cost_estimate=cost(4 * BOTH * Z * CHUNK * D, 6 << 20, 2 * BOTH * Z * CHUNK),
    )(ids, prototypes, center, mine, other)


def split3(value):
    top = value.astype(bf16)
    rest = value - top.astype(f32)
    middle = rest.astype(bf16)
    return top, middle, (rest - middle.astype(f32)).astype(bf16)


def tree(parts):
    while len(parts) > 1:
        parts = [parts[i] + parts[i + 1] for i in range(0, len(parts), 2)]
    return parts[0]


def merge(parts):
    t_top = functools.reduce(jnp.maximum, [p[0] for p in parts])
    s_top = functools.reduce(jnp.maximum, [p[3] for p in parts])
    t_keep = [jnp.exp2(p[0] - t_top) for p in parts]
    s_keep = [jnp.exp2(p[3] - s_top) for p in parts]
    t_sum = tree([p[1] * k for p, k in zip(parts, t_keep)])
    cross = tree([p[2] * k for p, k in zip(parts, t_keep)])
    s_sum = tree([p[4] * k for p, k in zip(parts, s_keep)])
    return t_top, t_sum, cross, s_top, s_sum


def flip(value):
    return jnp.concatenate([value[LOCAL:], value[:LOCAL]], axis=0)


def rows_of(ref):
    return [ref[q * 8 : (q + 1) * 8, :] for q in range(STATS)]


def core_merge_kernel(mine_ref, got_ref, out_ref):
    parts = [rows_of(mine_ref), [flip(value) for value in rows_of(got_ref)]]
    for q, value in enumerate(merge(parts)):
        out_ref[q * 8 : (q + 1) * 8, :] = value


def y_merge_kernel(a, b, c, d, out_ref):
    for q, value in enumerate(merge([rows_of(ref) for ref in (a, b, c, d)])):
        out_ref[q * 8 : (q + 1) * 8, :] = value


def x_merge_kernel(ids_ref, scale_ref, a, b, c, d, mine_ref, other_ref, sum_ref, coef_ref, misc_ref):
    t_top, t_sum, cross, s_top, s_sum = merge([rows_of(ref) for ref in (a, b, c, d)])
    counts = [ref[0, ROWS:, :128].astype(f32)[:LOCAL] for ref in (mine_ref, other_ref)]
    count = jnp.concatenate(counts, axis=0)
    slot = lax.broadcasted_iota(jnp.int32, (8, 128), 1).astype(f32)
    live = slot < count
    weight = 1.0 / (IMAGES * jnp.maximum(count, 1.0))
    s_lse = s_top + jnp.log2(s_sum)
    ce = (s_lse - cross / t_sum) * ln2
    factor = jnp.log2(weight * (scale_ref[0] * inverse_temp))
    s_coef = jnp.where(live, factor - s_lse, low)
    t_coef = jnp.where(live, factor - t_top - jnp.log2(t_sum), low)
    for g in range(8):
        coef_ref[0:1, g * 128 : (g + 1) * 128] = s_coef[g : g + 1]
        coef_ref[1:2, g * 128 : (g + 1) * 128] = t_coef[g : g + 1]
    coef_ref[2:8, :] = jnp.zeros((6, BOTH), f32)
    part = jnp.sum(jnp.where(live, weight * ce, 0.0), axis=1, keepdims=True)
    first = jnp.sum(part[:LOCAL], axis=0, keepdims=True)
    second = jnp.sum(part[LOCAL:], axis=0, keepdims=True)
    row = lax.broadcasted_iota(jnp.int32, (EXTRA, D), 0)
    mine = jnp.bitwise_and(row, Z - 1) == ids_ref[0]
    row_sum = split3(sum_ref[0:1, :])
    losses = split3(jnp.broadcast_to(first + second, (1, D)))
    block = jnp.zeros((EXTRA, D), f32)
    for i in range(3):
        block = jnp.where(row // Z == i, row_sum[i].astype(f32), block)
        block = jnp.where(row // Z == 3 + i, losses[i].astype(f32), block)
    misc_ref[...] = jnp.where(mine, block, 0.0).astype(bf16)


def small_call(kernel, out_shape, *args, smem=()):
    specs = [
        pl.BlockSpec(memory_space=pltpu.SMEM if i in smem else pltpu.VMEM) for i in range(len(args))
    ]
    vmem = pl.BlockSpec(memory_space=pltpu.VMEM)
    return pl.pallas_call(
        kernel,
        out_shape=out_shape,
        in_specs=specs,
        out_specs=jax.tree.map(lambda _: vmem, out_shape),
        compiler_params=params(),
        cost_estimate=cost(1 << 20, 1 << 18),
    )(*args)


def grad_kernel(ids_ref, p_ref, c_ref, mine_ref, other_ref, coef_ref, misc_ref, *refs):
    n = len(OFFSETS)
    outs, send_ref, du_ref, refs = refs[: n + 1], refs[n + 1], refs[n + 2], refs[n + 3 :]
    core = ids_ref[1]
    order = [lax.rem(ids_ref[0] + Z + d * (1 - 2 * core), Z) for d in OFFSETS]
    copies = fetch(order, core, p_ref, c_ref, *refs)
    p_held, c_held = refs[:2]
    for i in range(n):
        for copy in copies[i]:
            copy.wait()
        wide_p = p_held[i]
        protos = wide_p.T
        shift = wide(turned(c_held[i]), TILE // 128)
        total = None
        for half, ref in enumerate((mine_ref, other_ref)):
            for j in range(ROWS // TILE):
                rows = slice(j * TILE, (j + 1) * TILE)
                at = slice(half * ROWS + j * TILE, half * ROWS + (j + 1) * TILE)
                s_rows = ref[0, rows, :]
                t_arg = dot(protos, ref[1, rows, :], NT) * t_scale + shift + coef_ref[1:2, at]
                s_arg = dot(protos, s_rows, NT) * s_scale + coef_ref[0:1, at]
                dlogit = (jnp.exp2(s_arg) - jnp.exp2(t_arg)).astype(bf16)
                part = dot(dlogit, s_rows)
                total = part if total is None else total + part
                du = dot(wide_p, dlogit)
                if i == 0:
                    du_ref[:, at] = du
                else:
                    du_ref[:, at] += du
        if i == 0:
            half = CHUNK // 2
            outs[0][:half, :] = total[:half].astype(bf16)
            outs[0][half:, :] = misc_ref[...]
            outs[1][...] = total[half:].astype(bf16)
        else:
            outs[i + 1][...] = total.astype(bf16)
    send_ref[core] = du_ref[:, :ROWS].astype(bf16)
    send_ref[1 - core] = du_ref[:, ROWS:].astype(bf16)


def grads(ids, prototypes, center, mine, other, coef, misc):
    smem = pl.BlockSpec(memory_space=pltpu.SMEM)
    vmem = pl.BlockSpec(memory_space=pltpu.VMEM)
    anywhere = pl.BlockSpec(memory_space=pl.ANY)
    n = len(OFFSETS)
    shapes = [(CHUNK // 2 + EXTRA, D), (CHUNK // 2, D)] + [(CHUNK, D)] * (n - 1) + [(CORES, D, ROWS)]
    return pl.pallas_call(
        grad_kernel,
        in_specs=[smem, anywhere, anywhere] + [vmem] * 4,
        out_specs=[vmem] * len(shapes),
        out_shape=[jax.ShapeDtypeStruct(shape, bf16) for shape in shapes],
        scratch_shapes=[pltpu.VMEM((D, BOTH), f32)] + fetch_scratch(n),
        compiler_params=params(),
        cost_estimate=cost(8 * BOTH * n * CHUNK * D, n << 20, 2 * BOTH * n * CHUNK),
    )(ids, prototypes, center, mine, other, coef, misc)


def du_sum_kernel(got_ref, out_ref):
    total = jnp.sum(got_ref[...].astype(f32), axis=0).astype(bf16)
    out_ref[...] = jnp.broadcast_to(total[None], (X * Y,) + total.shape)


def halves_kernel(offset, with_extra, far_ref, got_ref, misc_ref, out_ref):
    half = CHUNK // 2
    for i in range(2):
        rows = slice(i * half, (i + 1) * half)
        part = far_ref[rows, :].astype(f32)
        if i == offset:
            part = part + got_ref[:half, :].astype(f32)
        out_ref[rows, :] = part.astype(bf16)
    extra = misc_ref[...]
    if with_extra:
        extra = extra + got_ref[half:, :]
    out_ref[CHUNK:, :] = extra


def step_kernel(near_ref, got_ref, misc_ref, out_ref):
    out_ref[:CHUNK, :] = (near_ref[...].astype(f32) + got_ref[:CHUNK, :].astype(f32)).astype(bf16)
    out_ref[CHUNK:, :] = misc_ref[...] + got_ref[CHUNK:, :]


def finish_kernel(near_ref, a_ref, b_ref, misc_ref, p_ref, grad_ref, center_ref, loss_ref, held, sems):
    width = p_ref.shape[1] // PIECES
    pieces = [pl.ds(i * width, width) for i in range(PIECES)]
    copies = [pltpu.make_async_copy(p_ref.at[:, at], held.at[i], sems.at[i]) for i, at in enumerate(pieces)]
    for copy in copies:
        copy.start()
    total = near_ref[...].astype(f32) + a_ref[:CHUNK, :].astype(f32)
    grad_ref[...] = total + b_ref[:CHUNK, :].astype(f32)
    extra = (misc_ref[...] + a_ref[CHUNK:, :] + b_ref[CHUNK:, :]).astype(f32)
    first = extra[0:8] + extra[8:16] + extra[16:24]
    loss = extra[24:32] + extra[32:40] + extra[40:48]
    total = jnp.broadcast_to(jnp.sum(first, axis=0, keepdims=True), (16, D))
    loss_ref[0, 0] = jnp.sum(loss[:, 0:1])
    stacked = jnp.concatenate(split3(total), axis=0)
    for i, at in enumerate(pieces):
        copies[i].wait()
        three = dot(stacked, held[i])
        center_ref[:, at] = (three[0:1] + three[16:17] + three[32:33]) * (1.0 / TOTAL)


def finish(near, a, b, misc, prototypes):
    width = prototypes.shape[1]
    smem = pl.BlockSpec(memory_space=pltpu.SMEM)
    vmem = pl.BlockSpec(memory_space=pltpu.VMEM)
    return pl.pallas_call(
        finish_kernel,
        in_specs=[vmem] * 4 + [pl.BlockSpec(memory_space=pl.ANY)],
        out_specs=[vmem, vmem, smem],
        out_shape=[
            jax.ShapeDtypeStruct((CHUNK, D), f32),
            jax.ShapeDtypeStruct((1, width), f32),
            jax.ShapeDtypeStruct((1, 1), f32),
        ],
        scratch_shapes=[
            pltpu.VMEM((PIECES, D, width // PIECES), bf16),
            pltpu.SemaphoreType.DMA((PIECES,)),
        ],
        compiler_params=params(),
        cost_estimate=cost(6 * 8 * D * width, 5 << 20),
    )(near, a, b, misc, prototypes)


def final_kernel(count_ref, index_ref, s_ref, du_ref, out_ref):
    for i in range(LOCAL):
        pick = picks(index_ref, count_ref[i], i)
        unit, length = unit_rows(dot(pick, s_ref[i], TN))
        d_unit = du_ref[:, i * SLOTS : (i + 1) * SLOTS].astype(f32).T
        row = (d_unit - unit * jnp.sum(unit * d_unit, axis=1, keepdims=True)) / length
        top = row.astype(bf16)
        rest = (row - top.astype(f32)).astype(bf16)
        out_ref[i] = dot(pick, top) + dot(pick, rest)


def shards(student_rows, teacher_rows, prototypes, center, mask_index, mask_count, loss_scale):
    z, core, x, y = (lax.axis_index(a) for a in ("z", "core", "x", "y"))
    ids = jnp.stack([z, core, x, y]).astype(jnp.int32)
    peers = ("core", "x", "y")
    one_way, other_way = [], []
    for i in range(Z):
        below, above, here = (i - 1) % Z * CORES, (i + 1) % Z * CORES, i * CORES
        one_way += [(here, below), (here + 1, above + 1)]
        other_way += [(here, above), (here + 1, below + 1)]

    def swaps(value, axis):
        return [lax.ppermute(value, axis, [(i, i ^ k) for i in range(4)]) for k in (1, 2, 3)]

    def ring(value, pairs):
        return lax.ppermute(value, ("z", "core"), pairs)

    mine = prep(mask_count, mask_index, student_rows, teacher_rows)
    other = lax.ppermute(mine, "core", [(0, 1), (1, 0)])
    center = center.reshape(1, -1)
    stats, row_sum = local_stats(ids, prototypes, center, mine, other)
    shape = jax.ShapeDtypeStruct((STATS * 8, 128), f32)
    stats = small_call(core_merge_kernel, shape, stats, lax.ppermute(stats, "core", [(0, 1), (1, 0)]))
    stats = small_call(y_merge_kernel, shape, stats, *swaps(stats, "y"))
    coef, misc = small_call(
        x_merge_kernel,
        [jax.ShapeDtypeStruct((8, BOTH), f32), jax.ShapeDtypeStruct((EXTRA, D), bf16)],
        ids, loss_scale.reshape(1), stats, *swaps(stats, "x"), mine, other, row_sum,
        smem=(0, 1),
    )

    step_shape = jax.ShapeDtypeStruct((CHUNK + EXTRA, D), bf16)
    half_a, half_b, *near, send = grads(ids, prototypes, center, mine, other, coef, misc)
    got_a, got_b = ring(half_a, one_way), ring(half_b, other_way)
    part = D // (X * Y)
    for i in range(3):
        if i == 0:
            kernel_a = functools.partial(halves_kernel, 0, True)
            kernel_b = functools.partial(halves_kernel, 1, False)
        else:
            kernel_a = kernel_b = step_kernel
        send_a = small_call(kernel_a, step_shape, near[2 * i], got_a, misc)
        send_b = small_call(kernel_b, step_shape, near[2 * i + 1], got_b, misc)
        if i == 0:
            send_a, send_b, send = lax.optimization_barrier((send_a, send_b, send))
            got = lax.all_to_all(send.reshape(PEERS, part, ROWS), peers, 0, 0)
        if i == 2:
            own = small_call(du_sum_kernel, jax.ShapeDtypeStruct((X * Y, part, ROWS), bf16), got)
            send_a, send_b, own = lax.optimization_barrier((send_a, send_b, own))
            du = lax.all_to_all(own, ("x", "y"), 0, 0).reshape(D, ROWS)
        got_a, got_b = ring(send_a, one_way), ring(send_b, other_way)
    proto_grad, patch_center, loss = finish(near[6], got_a, got_b, misc, prototypes)
    student_grad = small_call(
        final_kernel,
        jax.ShapeDtypeStruct(student_rows.shape, f32),
        mask_count, mask_index, student_rows, du,
        smem=(0,),
    )
    return (loss.reshape(()), student_grad, proto_grad, patch_center.reshape(-1))


def solution(mesh):
    fine = Mesh(mesh.devices.reshape(Z, CORES, X, Y), ("z", "core", "x", "y"))
    dp, proto = ("z", "core"), ("x", "y")
    in_specs = (
        P(dp, None, None),
        P(dp, None, None),
        P(None, proto),
        P(proto),
        P(dp, None),
        P(dp),
        P(),
    )
    out_specs = (P(), P(dp, None, None), P(proto + dp, None), P(proto))
    return jax.shard_map(shards, mesh=fine, in_specs=in_specs, out_specs=out_specs, check_vma=False)
```

```python
import functools
import math

import jax
import jax.numpy as jnp
from jax import lax
from jax.experimental import pallas as pl
from jax.experimental.pallas import tpu as pltpu
from jax.sharding import Mesh, PartitionSpec as P

bf16 = jnp.bfloat16
f32 = jnp.float32
log2e = math.log2(math.e)
ln2 = math.log(2.0)
t_scale = log2e / 0.04
s_scale = log2e / 0.1
inverse_temp = 10.0
norm_epsilon = 1e-06
low = -1e30

Z, CORES, X, Y = 8, 2, 4, 4
D = 256
SLOTS = 128
IMAGES = 64
TOTAL = 4096
LOCAL = 4
ROWS = LOCAL * SLOTS
BOTH = 2 * ROWS
CHUNK = 512
TILE = 512
STAT_TILE = 256
EXTRA = 48
HELD = ROWS + 16
STATS = 5
PEERS = CORES * X * Y
OFFSETS = (4, -3, 3, -2, 2, -1, 1, 0)
PIECES = 4

NT = (((1,), (1,)), ((), ()))
TN = (((0,), (0,)), ((), ()))


def dot(a, b, dims=(((1,), (0,)), ((), ()))):
    return lax.dot_general(a, b, dims, preferred_element_type=f32)


def params(mebibytes=16):
    return pltpu.CompilerParams(vmem_limit_bytes=mebibytes * 1024 * 1024)


def cost(flops, nbytes, trans=0):
    return pl.CostEstimate(flops=flops, bytes_accessed=nbytes, transcendentals=trans)


def picks(index_ref, count, i):
    patch = lax.broadcasted_iota(jnp.int32, (D, SLOTS), 0)
    slot = lax.broadcasted_iota(jnp.int32, (D, SLOTS), 1)
    hit = (patch == index_ref[i : i + 1, :]) & (slot < count)
    return jnp.where(hit, 1.0, 0.0).astype(bf16)


def unit_rows(values):
    length = jnp.sqrt(jnp.sum(values * values, axis=1, keepdims=True) + norm_epsilon)
    return values / length, length


def prep_kernel(count_ref, index_ref, s_ref, t_ref, out_ref):
    for i in range(LOCAL):
        pick = picks(index_ref, count_ref[i], i)
        for which, ref in enumerate((s_ref, t_ref)):
            unit, _ = unit_rows(dot(pick, ref[i], TN))
            out_ref[which, i * SLOTS : (i + 1) * SLOTS, :] = unit.astype(bf16)
    row = lax.broadcasted_iota(jnp.int32, (HELD - ROWS, D), 0)
    counts = jnp.zeros((HELD - ROWS, D), jnp.int32)
    for i in range(LOCAL):
        counts = jnp.where(row == i, count_ref[i], counts)
    for which in range(2):
        out_ref[which, ROWS:, :] = counts.astype(f32).astype(bf16)


def prep(count, index, student, teacher):
    smem = pl.BlockSpec(memory_space=pltpu.SMEM)
    vmem = pl.BlockSpec(memory_space=pltpu.VMEM)
    return pl.pallas_call(
        prep_kernel,
        out_shape=jax.ShapeDtypeStruct((2, HELD, D), bf16),
        in_specs=[smem, vmem, vmem, vmem],
        out_specs=vmem,
        compiler_params=params(),
        cost_estimate=cost(2 * 2 * ROWS * D * D, 1 << 21),
    )(count, index, student, teacher)


def wide(block, times):
    return jnp.concatenate([block] * times, axis=1)


def chunk_columns(i, core):
    return pl.ds(pl.multiple_of((CORES * i + core) * CHUNK, CHUNK), CHUNK)


def turned(held):
    return jnp.broadcast_to(held * -t_scale, (128, CHUNK)).T


def stats_kernel(ids_ref, p_ref, c_ref, mine_ref, other_ref, block, sum_ref, acc):
    groups = (CHUNK // 8, 8, STAT_TILE)
    for i in range(Z):
        columns = chunk_columns(i, ids_ref[1])
        protos = p_ref[:, columns].T
        shift = wide(turned(c_ref[:, columns]), STAT_TILE // 128)
        for half, ref in enumerate((mine_ref, other_ref)):
            for j in range(ROWS // STAT_TILE):
                rows = slice(j * STAT_TILE, (j + 1) * STAT_TILE)
                at = slice(half * ROWS + j * STAT_TILE, half * ROWS + (j + 1) * STAT_TILE)
                t_arg = (dot(protos, ref[1, rows, :], NT) * t_scale + shift).reshape(groups)
                s_arg = (dot(protos, ref[0, rows, :], NT) * s_scale).reshape(groups)
                t_top = jnp.max(t_arg, axis=0)
                s_top = jnp.max(s_arg, axis=0)
                t_exp = jnp.exp2(t_arg - t_top[None])
                s_exp = jnp.exp2(s_arg - s_top[None])
                acc[0, i, :, at] = t_top
                acc[1, i, :, at] = jnp.sum(t_exp, axis=0)
                acc[2, i, :, at] = jnp.sum(t_exp * s_arg, axis=0)
                acc[3, i, :, at] = s_top
                acc[4, i, :, at] = jnp.sum(s_exp, axis=0)
    for g in range(BOTH // 128):
        at = slice(g * 128, (g + 1) * 128)
        parts = [acc[q, :, :, at].reshape(Z * 8, 128) for q in range(STATS)]
        t_top = jnp.max(parts[0], axis=0, keepdims=True)
        s_top = jnp.max(parts[3], axis=0, keepdims=True)
        t_keep = jnp.exp2(parts[0] - t_top)
        s_keep = jnp.exp2(parts[3] - s_top)
        merged_rows = (
            t_top,
            jnp.sum(parts[1] * t_keep, axis=0, keepdims=True),
            jnp.sum(parts[2] * t_keep, axis=0, keepdims=True),
            s_top,
            jnp.sum(parts[4] * s_keep, axis=0, keepdims=True),
        )
        for q in range(STATS):
            block[q * 8 + g : q * 8 + g + 1, :] = merged_rows[q]
    first = jnp.sum(mine_ref[1, :ROWS, :].astype(f32), axis=0, keepdims=True)
    second = jnp.sum(other_ref[1, :ROWS, :].astype(f32), axis=0, keepdims=True)
    sum_ref[...] = jnp.broadcast_to(first + second, (8, D))


def local_stats(ids, prototypes, center, mine, other):
    smem = pl.BlockSpec(memory_space=pltpu.SMEM)
    vmem = pl.BlockSpec(memory_space=pltpu.VMEM)
    return pl.pallas_call(
        stats_kernel,
        in_specs=[smem, vmem, vmem, vmem, vmem],
        out_specs=[vmem] * 2,
        out_shape=[jax.ShapeDtypeStruct((STATS * 8, 128), f32), jax.ShapeDtypeStruct((8, D), f32)],
        scratch_shapes=[pltpu.VMEM((STATS, Z, 8, BOTH), f32)],
        compiler_params=params(24),
        cost_estimate=cost(4 * BOTH * Z * CHUNK * D, 6 << 20, 2 * BOTH * Z * CHUNK),
    )(ids, prototypes, center, mine, other)


def split3(value):
    top = value.astype(bf16)
    rest = value - top.astype(f32)
    middle = rest.astype(bf16)
    return top, middle, (rest - middle.astype(f32)).astype(bf16)


def tree(parts):
    while len(parts) > 1:
        parts = [parts[i] + parts[i + 1] for i in range(0, len(parts), 2)]
    return parts[0]


def merge(parts):
    t_top = functools.reduce(jnp.maximum, [p[0] for p in parts])
    s_top = functools.reduce(jnp.maximum, [p[3] for p in parts])
    t_keep = [jnp.exp2(p[0] - t_top) for p in parts]
    s_keep = [jnp.exp2(p[3] - s_top) for p in parts]
    t_sum = tree([p[1] * k for p, k in zip(parts, t_keep)])
    cross = tree([p[2] * k for p, k in zip(parts, t_keep)])
    s_sum = tree([p[4] * k for p, k in zip(parts, s_keep)])
    return t_top, t_sum, cross, s_top, s_sum


def flip(value):
    return jnp.concatenate([value[LOCAL:], value[:LOCAL]], axis=0)


def rows_of(ref):
    return [ref[q * 8 : (q + 1) * 8, :] for q in range(STATS)]


def core_merge_kernel(mine_ref, got_ref, out_ref):
    parts = [rows_of(mine_ref), [flip(value) for value in rows_of(got_ref)]]
    for q, value in enumerate(merge(parts)):
        out_ref[q * 8 : (q + 1) * 8, :] = value


def y_merge_kernel(a, b, c, d, out_ref):
    for q, value in enumerate(merge([rows_of(ref) for ref in (a, b, c, d)])):
        out_ref[q * 8 : (q + 1) * 8, :] = value


def x_merge_kernel(ids_ref, scale_ref, a, b, c, d, mine_ref, other_ref, sum_ref, coef_ref, misc_ref):
    t_top, t_sum, cross, s_top, s_sum = merge([rows_of(ref) for ref in (a, b, c, d)])
    counts = [ref[0, ROWS:, :128].astype(f32)[:LOCAL] for ref in (mine_ref, other_ref)]
    count = jnp.concatenate(counts, axis=0)
    slot = lax.broadcasted_iota(jnp.int32, (8, 128), 1).astype(f32)
    live = slot < count
    weight = 1.0 / (IMAGES * jnp.maximum(count, 1.0))
    s_lse = s_top + jnp.log2(s_sum)
    ce = (s_lse - cross / t_sum) * ln2
    factor = jnp.log2(weight * (scale_ref[0] * inverse_temp))
    s_coef = jnp.where(live, factor - s_lse, low)
    t_coef = jnp.where(live, factor - t_top - jnp.log2(t_sum), low)
    for g in range(8):
        coef_ref[0:1, g * 128 : (g + 1) * 128] = s_coef[g : g + 1]
        coef_ref[1:2, g * 128 : (g + 1) * 128] = t_coef[g : g + 1]
    coef_ref[2:8, :] = jnp.zeros((6, BOTH), f32)
    part = jnp.sum(jnp.where(live, weight * ce, 0.0), axis=1, keepdims=True)
    first = jnp.sum(part[:LOCAL], axis=0, keepdims=True)
    second = jnp.sum(part[LOCAL:], axis=0, keepdims=True)
    row = lax.broadcasted_iota(jnp.int32, (EXTRA, D), 0)
    mine = jnp.bitwise_and(row, Z - 1) == ids_ref[0]
    row_sum = split3(sum_ref[0:1, :])
    losses = split3(jnp.broadcast_to(first + second, (1, D)))
    block = jnp.zeros((EXTRA, D), f32)
    for i in range(3):
        block = jnp.where(row // Z == i, row_sum[i].astype(f32), block)
        block = jnp.where(row // Z == 3 + i, losses[i].astype(f32), block)
    misc_ref[...] = jnp.where(mine, block, 0.0).astype(bf16)


def small_call(kernel, out_shape, *args, smem=()):
    specs = [
        pl.BlockSpec(memory_space=pltpu.SMEM if i in smem else pltpu.VMEM) for i in range(len(args))
    ]
    vmem = pl.BlockSpec(memory_space=pltpu.VMEM)
    return pl.pallas_call(
        kernel,
        out_shape=out_shape,
        in_specs=specs,
        out_specs=jax.tree.map(lambda _: vmem, out_shape),
        compiler_params=params(),
        cost_estimate=cost(1 << 20, 1 << 18),
    )(*args)


def grad_kernel(ids_ref, p_ref, c_ref, mine_ref, other_ref, coef_ref, misc_ref, *refs):
    n = len(OFFSETS)
    outs, send_ref, du_ref = refs[: n + 1], refs[n + 1], refs[n + 2]
    core = ids_ref[1]
    order = [lax.rem(ids_ref[0] + Z + d * (1 - 2 * core), Z) for d in OFFSETS]
    for i in range(n):
        columns = chunk_columns(order[i], core)
        wide_p = p_ref[:, columns]
        protos = wide_p.T
        shift = wide(turned(c_ref[:, columns]), TILE // 128)
        total = None
        for half, ref in enumerate((mine_ref, other_ref)):
            for j in range(ROWS // TILE):
                rows = slice(j * TILE, (j + 1) * TILE)
                at = slice(half * ROWS + j * TILE, half * ROWS + (j + 1) * TILE)
                s_rows = ref[0, rows, :]
                t_arg = dot(protos, ref[1, rows, :], NT) * t_scale + shift + coef_ref[1:2, at]
                s_arg = dot(protos, s_rows, NT) * s_scale + coef_ref[0:1, at]
                dlogit = (jnp.exp2(s_arg) - jnp.exp2(t_arg)).astype(bf16)
                part = dot(dlogit, s_rows)
                total = part if total is None else total + part
                du = dot(wide_p, dlogit)
                if i == 0:
                    du_ref[:, at] = du
                else:
                    du_ref[:, at] += du
        if i == 0:
            half = CHUNK // 2
            outs[0][:half, :] = total[:half].astype(bf16)
            outs[0][half:, :] = misc_ref[...]
            outs[1][...] = total[half:].astype(bf16)
        else:
            outs[i + 1][...] = total.astype(bf16)
    send_ref[core] = du_ref[:, :ROWS].astype(bf16)
    send_ref[1 - core] = du_ref[:, ROWS:].astype(bf16)


def grads(ids, prototypes, center, mine, other, coef, misc):
    smem = pl.BlockSpec(memory_space=pltpu.SMEM)
    vmem = pl.BlockSpec(memory_space=pltpu.VMEM)
    n = len(OFFSETS)
    shapes = [(CHUNK // 2 + EXTRA, D), (CHUNK // 2, D)] + [(CHUNK, D)] * (n - 1) + [(CORES, D, ROWS)]
    return pl.pallas_call(
        grad_kernel,
        in_specs=[smem] + [vmem] * 6,
        out_specs=[vmem] * len(shapes),
        out_shape=[jax.ShapeDtypeStruct(shape, bf16) for shape in shapes],
        scratch_shapes=[pltpu.VMEM((D, BOTH), f32)],
        compiler_params=params(24),
        cost_estimate=cost(8 * BOTH * n * CHUNK * D, n << 20, 2 * BOTH * n * CHUNK),
    )(ids, prototypes, center, mine, other, coef, misc)


def du_sum_kernel(got_ref, out_ref):
    total = jnp.sum(got_ref[...].astype(f32), axis=0).astype(bf16)
    out_ref[...] = jnp.broadcast_to(total[None], (X * Y,) + total.shape)


def halves_kernel(offset, with_extra, far_ref, got_ref, misc_ref, out_ref):
    half = CHUNK // 2
    for i in range(2):
        rows = slice(i * half, (i + 1) * half)
        part = far_ref[rows, :].astype(f32)
        if i == offset:
            part = part + got_ref[:half, :].astype(f32)
        out_ref[rows, :] = part.astype(bf16)
    extra = misc_ref[...]
    if with_extra:
        extra = extra + got_ref[half:, :]
    out_ref[CHUNK:, :] = extra


def step_kernel(near_ref, got_ref, misc_ref, out_ref):
    out_ref[:CHUNK, :] = (near_ref[...].astype(f32) + got_ref[:CHUNK, :].astype(f32)).astype(bf16)
    out_ref[CHUNK:, :] = misc_ref[...] + got_ref[CHUNK:, :]


def finish_kernel(near_ref, a_ref, b_ref, misc_ref, p_ref, grad_ref, center_ref, loss_ref):
    width = p_ref.shape[1] // PIECES
    pieces = [pl.ds(i * width, width) for i in range(PIECES)]
    total = near_ref[...].astype(f32) + a_ref[:CHUNK, :].astype(f32)
    grad_ref[...] = total + b_ref[:CHUNK, :].astype(f32)
    extra = (misc_ref[...] + a_ref[CHUNK:, :] + b_ref[CHUNK:, :]).astype(f32)
    first = extra[0:8] + extra[8:16] + extra[16:24]
    loss = extra[24:32] + extra[32:40] + extra[40:48]
    total = jnp.broadcast_to(jnp.sum(first, axis=0, keepdims=True), (16, D))
    loss_ref[0, 0] = jnp.sum(loss[:, 0:1])
    stacked = jnp.concatenate(split3(total), axis=0)
    for at in pieces:
        three = dot(stacked, p_ref[:, at])
        center_ref[:, at] = (three[0:1] + three[16:17] + three[32:33]) * (1.0 / TOTAL)


def finish(near, a, b, misc, prototypes):
    width = prototypes.shape[1]
    smem = pl.BlockSpec(memory_space=pltpu.SMEM)
    vmem = pl.BlockSpec(memory_space=pltpu.VMEM)
    return pl.pallas_call(
        finish_kernel,
        in_specs=[vmem] * 5,
        out_specs=[vmem, vmem, smem],
        out_shape=[
            jax.ShapeDtypeStruct((CHUNK, D), f32),
            jax.ShapeDtypeStruct((1, width), f32),
            jax.ShapeDtypeStruct((1, 1), f32),
        ],
        compiler_params=params(),
        cost_estimate=cost(6 * 8 * D * width, 5 << 20),
    )(near, a, b, misc, prototypes)


def final_kernel(count_ref, index_ref, s_ref, du_ref, out_ref):
    for i in range(LOCAL):
        pick = picks(index_ref, count_ref[i], i)
        unit, length = unit_rows(dot(pick, s_ref[i], TN))
        d_unit = du_ref[:, i * SLOTS : (i + 1) * SLOTS].astype(f32).T
        row = (d_unit - unit * jnp.sum(unit * d_unit, axis=1, keepdims=True)) / length
        top = row.astype(bf16)
        rest = (row - top.astype(f32)).astype(bf16)
        out_ref[i] = dot(pick, top) + dot(pick, rest)


def shards(student_rows, teacher_rows, prototypes, center, mask_index, mask_count, loss_scale):
    z, core, x, y = (lax.axis_index(a) for a in ("z", "core", "x", "y"))
    ids = jnp.stack([z, core, x, y]).astype(jnp.int32)
    peers = ("core", "x", "y")
    one_way, other_way = [], []
    for i in range(Z):
        below, above, here = (i - 1) % Z * CORES, (i + 1) % Z * CORES, i * CORES
        one_way += [(here, below), (here + 1, above + 1)]
        other_way += [(here, above), (here + 1, below + 1)]

    def swaps(value, axis):
        return [lax.ppermute(value, axis, [(i, i ^ k) for i in range(4)]) for k in (1, 2, 3)]

    def ring(value, pairs):
        return lax.ppermute(value, ("z", "core"), pairs)

    mine = prep(mask_count, mask_index, student_rows, teacher_rows)
    other = lax.ppermute(mine, "core", [(0, 1), (1, 0)])
    center = center.reshape(1, -1)
    stats, row_sum = local_stats(ids, prototypes, center, mine, other)
    shape = jax.ShapeDtypeStruct((STATS * 8, 128), f32)
    stats = small_call(core_merge_kernel, shape, stats, lax.ppermute(stats, "core", [(0, 1), (1, 0)]))
    stats = small_call(y_merge_kernel, shape, stats, *swaps(stats, "y"))
    coef, misc = small_call(
        x_merge_kernel,
        [jax.ShapeDtypeStruct((8, BOTH), f32), jax.ShapeDtypeStruct((EXTRA, D), bf16)],
        ids, loss_scale.reshape(1), stats, *swaps(stats, "x"), mine, other, row_sum,
        smem=(0, 1),
    )

    step_shape = jax.ShapeDtypeStruct((CHUNK + EXTRA, D), bf16)
    half_a, half_b, *near, send = grads(ids, prototypes, center, mine, other, coef, misc)
    got_a, got_b = ring(half_a, one_way), ring(half_b, other_way)
    part = D // (X * Y)
    got = lax.all_to_all(send.reshape(PEERS, part, ROWS), peers, 0, 0)
    own = small_call(du_sum_kernel, jax.ShapeDtypeStruct((X * Y, part, ROWS), bf16), got)
    for i in range(3):
        if i == 0:
            kernel_a = functools.partial(halves_kernel, 0, True)
            kernel_b = functools.partial(halves_kernel, 1, False)
        else:
            kernel_a = kernel_b = step_kernel
        send_a = small_call(kernel_a, step_shape, near[2 * i], got_a, misc)
        send_b = small_call(kernel_b, step_shape, near[2 * i + 1], got_b, misc)
        if i == 0:
            send_a, send_b, own = lax.optimization_barrier((send_a, send_b, own))
            du = lax.all_to_all(own, ("x", "y"), 0, 0)
        if i == 2:
            send_a, send_b, du = lax.optimization_barrier((send_a, send_b, du))
        got_a, got_b = ring(send_a, one_way), ring(send_b, other_way)
    proto_grad, patch_center, loss = finish(near[6], got_a, got_b, misc, prototypes)
    student_grad = small_call(
        final_kernel,
        jax.ShapeDtypeStruct(student_rows.shape, f32),
        mask_count, mask_index, student_rows, du.reshape(D, ROWS),
        smem=(0,),
    )
    return (loss.reshape(()), student_grad, proto_grad, patch_center.reshape(-1))


def solution(mesh):
    fine = Mesh(mesh.devices.reshape(Z, CORES, X, Y), ("z", "core", "x", "y"))
    dp, proto = ("z", "core"), ("x", "y")
    in_specs = (
        P(dp, None, None),
        P(dp, None, None),
        P(None, proto),
        P(proto),
        P(dp, None),
        P(dp),
        P(),
    )
    out_specs = (P(), P(dp, None, None), P(proto + dp, None), P(proto))
    return jax.shard_map(shards, mesh=fine, in_specs=in_specs, out_specs=out_specs, check_vma=False)
```

```python
import functools
import math

import jax
import jax.numpy as jnp
from jax import lax
from jax.experimental import pallas as pl
from jax.experimental.pallas import tpu as pltpu
from jax.sharding import Mesh, PartitionSpec as P

bf16 = jnp.bfloat16
f32 = jnp.float32
log2e = math.log2(math.e)
ln2 = math.log(2.0)
t_scale = log2e / 0.04
s_scale = log2e / 0.1
inverse_temp = 10.0
norm_epsilon = 1e-06
low = -1e30

Z, CORES, X, Y = 8, 2, 4, 4
D = 256
SLOTS = 128
IMAGES = 64
TOTAL = 4096
LOCAL = 4
ROWS = LOCAL * SLOTS
BOTH = 2 * ROWS
CHUNK = 512
TILE = 512
STAT_TILE = 256
EXTRA = 32
HELD = ROWS + 16
STATS = 5
PEERS = CORES * X * Y
OFFSETS = (4, -3, 3, -2, 2, -1, 1, 0)
PIECES = 4

NT = (((1,), (1,)), ((), ()))
TN = (((0,), (0,)), ((), ()))


def dot(a, b, dims=(((1,), (0,)), ((), ()))):
    return lax.dot_general(a, b, dims, preferred_element_type=f32)


def params(mebibytes=16):
    return pltpu.CompilerParams(vmem_limit_bytes=mebibytes * 1024 * 1024)


def cost(flops, nbytes, trans=0):
    return pl.CostEstimate(flops=flops, bytes_accessed=nbytes, transcendentals=trans)


def picks(index_ref, count, i):
    patch = lax.broadcasted_iota(jnp.int32, (D, SLOTS), 0)
    slot = lax.broadcasted_iota(jnp.int32, (D, SLOTS), 1)
    hit = (patch == index_ref[i : i + 1, :]) & (slot < count)
    return jnp.where(hit, 1.0, 0.0).astype(bf16)


def unit_rows(values):
    length = jnp.sqrt(jnp.sum(values * values, axis=1, keepdims=True) + norm_epsilon)
    return values / length, length


def prep_kernel(count_ref, index_ref, s_ref, t_ref, out_ref):
    for i in range(LOCAL):
        pick = picks(index_ref, count_ref[i], i)
        for which, ref in enumerate((s_ref, t_ref)):
            unit, _ = unit_rows(dot(pick, ref[i], TN))
            out_ref[which, i * SLOTS : (i + 1) * SLOTS, :] = unit.astype(bf16)
    row = lax.broadcasted_iota(jnp.int32, (HELD - ROWS, D), 0)
    counts = jnp.zeros((HELD - ROWS, D), jnp.int32)
    for i in range(LOCAL):
        counts = jnp.where(row == i, count_ref[i], counts)
    for which in range(2):
        out_ref[which, ROWS:, :] = counts.astype(f32).astype(bf16)


def prep(count, index, student, teacher):
    smem = pl.BlockSpec(memory_space=pltpu.SMEM)
    vmem = pl.BlockSpec(memory_space=pltpu.VMEM)
    return pl.pallas_call(
        prep_kernel,
        out_shape=jax.ShapeDtypeStruct((2, HELD, D), bf16),
        in_specs=[smem, vmem, vmem, vmem],
        out_specs=vmem,
        compiler_params=params(),
        cost_estimate=cost(2 * 2 * ROWS * D * D, 1 << 21),
    )(count, index, student, teacher)


def wide(block, times):
    return jnp.concatenate([block] * times, axis=1)


def chunk_columns(i, core):
    return pl.ds(pl.multiple_of((CORES * i + core) * CHUNK, CHUNK), CHUNK)


def turned(held):
    return jnp.broadcast_to(held * -t_scale, (128, CHUNK)).T


def stats_kernel(ids_ref, p_ref, c_ref, mine_ref, other_ref, block, sum_ref, acc):
    groups = (CHUNK // 8, 8, STAT_TILE)
    for i in range(Z):
        columns = chunk_columns(i, ids_ref[1])
        protos = p_ref[:, columns].T
        shift = wide(turned(c_ref[:, columns]), STAT_TILE // 128)
        for half, ref in enumerate((mine_ref, other_ref)):
            for j in range(ROWS // STAT_TILE):
                rows = slice(j * STAT_TILE, (j + 1) * STAT_TILE)
                at = slice(half * ROWS + j * STAT_TILE, half * ROWS + (j + 1) * STAT_TILE)
                t_arg = (dot(protos, ref[1, rows, :], NT) * t_scale + shift).reshape(groups)
                s_arg = (dot(protos, ref[0, rows, :], NT) * s_scale).reshape(groups)
                t_top = jnp.max(t_arg, axis=0)
                s_top = jnp.max(s_arg, axis=0)
                t_exp = jnp.exp2(t_arg - t_top[None])
                s_exp = jnp.exp2(s_arg - s_top[None])
                acc[0, i, :, at] = t_top
                acc[1, i, :, at] = jnp.sum(t_exp, axis=0)
                acc[2, i, :, at] = jnp.sum(t_exp * s_arg, axis=0)
                acc[3, i, :, at] = s_top
                acc[4, i, :, at] = jnp.sum(s_exp, axis=0)
    for g in range(BOTH // 128):
        at = slice(g * 128, (g + 1) * 128)
        parts = [acc[q, :, :, at].reshape(Z * 8, 128) for q in range(STATS)]
        t_top = jnp.max(parts[0], axis=0, keepdims=True)
        s_top = jnp.max(parts[3], axis=0, keepdims=True)
        t_keep = jnp.exp2(parts[0] - t_top)
        s_keep = jnp.exp2(parts[3] - s_top)
        merged_rows = (
            t_top,
            jnp.sum(parts[1] * t_keep, axis=0, keepdims=True),
            jnp.sum(parts[2] * t_keep, axis=0, keepdims=True),
            s_top,
            jnp.sum(parts[4] * s_keep, axis=0, keepdims=True),
        )
        for q in range(STATS):
            block[q * 8 + g : q * 8 + g + 1, :] = merged_rows[q]
    first = jnp.sum(mine_ref[1, :ROWS, :].astype(f32), axis=0, keepdims=True)
    second = jnp.sum(other_ref[1, :ROWS, :].astype(f32), axis=0, keepdims=True)
    sum_ref[...] = jnp.broadcast_to(first + second, (8, D))


def local_stats(ids, prototypes, center, mine, other):
    smem = pl.BlockSpec(memory_space=pltpu.SMEM)
    vmem = pl.BlockSpec(memory_space=pltpu.VMEM)
    return pl.pallas_call(
        stats_kernel,
        in_specs=[smem, vmem, vmem, vmem, vmem],
        out_specs=[vmem] * 2,
        out_shape=[jax.ShapeDtypeStruct((STATS * 8, 128), f32), jax.ShapeDtypeStruct((8, D), f32)],
        scratch_shapes=[pltpu.VMEM((STATS, Z, 8, BOTH), f32)],
        compiler_params=params(24),
        cost_estimate=cost(4 * BOTH * Z * CHUNK * D, 6 << 20, 2 * BOTH * Z * CHUNK),
    )(ids, prototypes, center, mine, other)


def split3(value):
    top = value.astype(bf16)
    rest = value - top.astype(f32)
    middle = rest.astype(bf16)
    return top, middle, (rest - middle.astype(f32)).astype(bf16)


def tree(parts):
    while len(parts) > 1:
        parts = [parts[i] + parts[i + 1] for i in range(0, len(parts), 2)]
    return parts[0]


def merge(parts):
    t_top = functools.reduce(jnp.maximum, [p[0] for p in parts])
    s_top = functools.reduce(jnp.maximum, [p[3] for p in parts])
    t_keep = [jnp.exp2(p[0] - t_top) for p in parts]
    s_keep = [jnp.exp2(p[3] - s_top) for p in parts]
    t_sum = tree([p[1] * k for p, k in zip(parts, t_keep)])
    cross = tree([p[2] * k for p, k in zip(parts, t_keep)])
    s_sum = tree([p[4] * k for p, k in zip(parts, s_keep)])
    return t_top, t_sum, cross, s_top, s_sum


def flip(value):
    return jnp.concatenate([value[LOCAL:], value[:LOCAL]], axis=0)


def rows_of(ref):
    return [ref[q * 8 : (q + 1) * 8, :] for q in range(STATS)]


def core_merge_kernel(mine_ref, got_ref, out_ref):
    parts = [rows_of(mine_ref), [flip(value) for value in rows_of(got_ref)]]
    for q, value in enumerate(merge(parts)):
        out_ref[q * 8 : (q + 1) * 8, :] = value


def y_merge_kernel(a, b, c, d, out_ref):
    for q, value in enumerate(merge([rows_of(ref) for ref in (a, b, c, d)])):
        out_ref[q * 8 : (q + 1) * 8, :] = value


def x_merge_kernel(ids_ref, scale_ref, a, b, c, d, mine_ref, other_ref, sum_ref, coef_ref, misc_ref):
    t_top, t_sum, cross, s_top, s_sum = merge([rows_of(ref) for ref in (a, b, c, d)])
    counts = [ref[0, ROWS:, :128].astype(f32)[:LOCAL] for ref in (mine_ref, other_ref)]
    count = jnp.concatenate(counts, axis=0)
    slot = lax.broadcasted_iota(jnp.int32, (8, 128), 1).astype(f32)
    live = slot < count
    weight = 1.0 / (IMAGES * jnp.maximum(count, 1.0))
    s_lse = s_top + jnp.log2(s_sum)
    ce = (s_lse - cross / t_sum) * ln2
    factor = jnp.log2(weight * (scale_ref[0] * inverse_temp))
    s_coef = jnp.where(live, factor - s_lse, low)
    t_coef = jnp.where(live, factor - t_top - jnp.log2(t_sum), low)
    for g in range(8):
        coef_ref[0:1, g * 128 : (g + 1) * 128] = s_coef[g : g + 1]
        coef_ref[1:2, g * 128 : (g + 1) * 128] = t_coef[g : g + 1]
    coef_ref[2:8, :] = jnp.zeros((6, BOTH), f32)
    part = jnp.sum(jnp.where(live, weight * ce, 0.0), axis=1, keepdims=True)
    first = jnp.sum(part[:LOCAL], axis=0, keepdims=True)
    second = jnp.sum(part[LOCAL:], axis=0, keepdims=True)
    row = lax.broadcasted_iota(jnp.int32, (EXTRA, D), 0)
    mine = jnp.bitwise_and(row, Z - 1) == ids_ref[0]
    row_sum = split3(sum_ref[0:1, :])
    losses = split3(jnp.broadcast_to(first + second, (1, D)))
    block = jnp.zeros((EXTRA, D), f32)
    for i in range(2):
        block = jnp.where(row // Z == i, row_sum[i].astype(f32), block)
        block = jnp.where(row // Z == 2 + i, losses[i].astype(f32), block)
    misc_ref[...] = jnp.where(mine, block, 0.0).astype(bf16)


def small_call(kernel, out_shape, *args, smem=()):
    specs = [
        pl.BlockSpec(memory_space=pltpu.SMEM if i in smem else pltpu.VMEM) for i in range(len(args))
    ]
    vmem = pl.BlockSpec(memory_space=pltpu.VMEM)
    return pl.pallas_call(
        kernel,
        out_shape=out_shape,
        in_specs=specs,
        out_specs=jax.tree.map(lambda _: vmem, out_shape),
        compiler_params=params(),
        cost_estimate=cost(1 << 20, 1 << 18),
    )(*args)


def grad_kernel(ids_ref, p_ref, c_ref, mine_ref, other_ref, coef_ref, misc_ref, *refs):
    n = len(OFFSETS)
    outs, send_ref, du_ref = refs[: n + 1], refs[n + 1], refs[n + 2]
    core = ids_ref[1]
    order = [lax.rem(ids_ref[0] + Z + d * (1 - 2 * core), Z) for d in OFFSETS]
    for i in range(n):
        columns = chunk_columns(order[i], core)
        wide_p = p_ref[:, columns]
        protos = wide_p.T
        shift = wide(turned(c_ref[:, columns]), TILE // 128)
        total = None
        for half, ref in enumerate((mine_ref, other_ref)):
            for j in range(ROWS // TILE):
                rows = slice(j * TILE, (j + 1) * TILE)
                at = slice(half * ROWS + j * TILE, half * ROWS + (j + 1) * TILE)
                s_rows = ref[0, rows, :]
                t_arg = dot(protos, ref[1, rows, :], NT) * t_scale + shift + coef_ref[1:2, at]
                s_arg = dot(protos, s_rows, NT) * s_scale + coef_ref[0:1, at]
                dlogit = (jnp.exp2(s_arg) - jnp.exp2(t_arg)).astype(bf16)
                part = dot(dlogit, s_rows)
                total = part if total is None else total + part
                du = dot(wide_p, dlogit)
                if i == 0:
                    du_ref[:, at] = du
                else:
                    du_ref[:, at] += du
        if i == 0:
            half = CHUNK // 2
            outs[0][:half, :] = total[:half].astype(bf16)
            outs[0][half:, :] = misc_ref[...]
            outs[1][...] = total[half:].astype(bf16)
        else:
            outs[i + 1][...] = total.astype(bf16)
    send_ref[core] = du_ref[:, :ROWS].astype(bf16)
    send_ref[1 - core] = du_ref[:, ROWS:].astype(bf16)


def grads(ids, prototypes, center, mine, other, coef, misc):
    smem = pl.BlockSpec(memory_space=pltpu.SMEM)
    vmem = pl.BlockSpec(memory_space=pltpu.VMEM)
    n = len(OFFSETS)
    shapes = [(CHUNK // 2 + EXTRA, D), (CHUNK // 2, D)] + [(CHUNK, D)] * (n - 1) + [(CORES, D, ROWS)]
    return pl.pallas_call(
        grad_kernel,
        in_specs=[smem] + [vmem] * 6,
        out_specs=[vmem] * len(shapes),
        out_shape=[jax.ShapeDtypeStruct(shape, bf16) for shape in shapes],
        scratch_shapes=[pltpu.VMEM((D, BOTH), f32)],
        compiler_params=params(24),
        cost_estimate=cost(8 * BOTH * n * CHUNK * D, n << 20, 2 * BOTH * n * CHUNK),
    )(ids, prototypes, center, mine, other, coef, misc)


def du_sum_kernel(got_ref, out_ref):
    total = jnp.sum(got_ref[...].astype(f32), axis=0).astype(bf16)
    out_ref[...] = jnp.broadcast_to(total[None], (X * Y,) + total.shape)


def halves_kernel(offset, with_extra, far_ref, got_ref, misc_ref, out_ref):
    half = CHUNK // 2
    for i in range(2):
        rows = slice(i * half, (i + 1) * half)
        part = far_ref[rows, :].astype(f32)
        if i == offset:
            part = part + got_ref[:half, :].astype(f32)
        out_ref[rows, :] = part.astype(bf16)
    extra = misc_ref[...]
    if with_extra:
        extra = extra + got_ref[half:, :]
    out_ref[CHUNK:, :] = extra


def step_kernel(near_ref, got_ref, misc_ref, out_ref):
    out_ref[:CHUNK, :] = (near_ref[...].astype(f32) + got_ref[:CHUNK, :].astype(f32)).astype(bf16)
    out_ref[CHUNK:, :] = misc_ref[...] + got_ref[CHUNK:, :]


def finish_kernel(near_ref, a_ref, b_ref, misc_ref, p_ref, grad_ref, center_ref, loss_ref):
    width = p_ref.shape[1] // PIECES
    pieces = [pl.ds(i * width, width) for i in range(PIECES)]
    total = near_ref[...].astype(f32) + a_ref[:CHUNK, :].astype(f32)
    grad_ref[...] = total + b_ref[:CHUNK, :].astype(f32)
    extra = (misc_ref[...] + a_ref[CHUNK:, :] + b_ref[CHUNK:, :]).astype(f32)
    first = extra[0:8] + extra[8:16]
    loss = extra[16:24] + extra[24:32]
    total = jnp.broadcast_to(jnp.sum(first, axis=0, keepdims=True), (16, D))
    loss_ref[0, 0] = jnp.sum(loss[:, 0:1])
    stacked = jnp.concatenate(split3(total), axis=0)
    for at in pieces:
        three = dot(stacked, p_ref[:, at])
        center_ref[:, at] = (three[0:1] + three[16:17] + three[32:33]) * (1.0 / TOTAL)


def finish(near, a, b, misc, prototypes):
    width = prototypes.shape[1]
    smem = pl.BlockSpec(memory_space=pltpu.SMEM)
    vmem = pl.BlockSpec(memory_space=pltpu.VMEM)
    return pl.pallas_call(
        finish_kernel,
        in_specs=[vmem] * 5,
        out_specs=[vmem, vmem, smem],
        out_shape=[
            jax.ShapeDtypeStruct((CHUNK, D), f32),
            jax.ShapeDtypeStruct((1, width), f32),
            jax.ShapeDtypeStruct((1, 1), f32),
        ],
        compiler_params=params(),
        cost_estimate=cost(6 * 8 * D * width, 5 << 20),
    )(near, a, b, misc, prototypes)


def final_kernel(count_ref, index_ref, s_ref, du_ref, out_ref):
    for i in range(LOCAL):
        pick = picks(index_ref, count_ref[i], i)
        unit, length = unit_rows(dot(pick, s_ref[i], TN))
        d_unit = du_ref[:, i * SLOTS : (i + 1) * SLOTS].astype(f32).T
        row = (d_unit - unit * jnp.sum(unit * d_unit, axis=1, keepdims=True)) / length
        top = row.astype(bf16)
        rest = (row - top.astype(f32)).astype(bf16)
        out_ref[i] = dot(pick, top) + dot(pick, rest)


def shards(student_rows, teacher_rows, prototypes, center, mask_index, mask_count, loss_scale):
    z, core, x, y = (lax.axis_index(a) for a in ("z", "core", "x", "y"))
    ids = jnp.stack([z, core, x, y]).astype(jnp.int32)
    peers = ("core", "x", "y")
    one_way, other_way = [], []
    for i in range(Z):
        below, above, here = (i - 1) % Z * CORES, (i + 1) % Z * CORES, i * CORES
        one_way += [(here, below), (here + 1, above + 1)]
        other_way += [(here, above), (here + 1, below + 1)]

    def swaps(value, axis):
        return [lax.ppermute(value, axis, [(i, i ^ k) for i in range(4)]) for k in (1, 2, 3)]

    def ring(value, pairs):
        return lax.ppermute(value, ("z", "core"), pairs)

    mine = prep(mask_count, mask_index, student_rows, teacher_rows)
    other = lax.ppermute(mine, "core", [(0, 1), (1, 0)])
    center = center.reshape(1, -1)
    stats, row_sum = local_stats(ids, prototypes, center, mine, other)
    shape = jax.ShapeDtypeStruct((STATS * 8, 128), f32)
    stats = small_call(core_merge_kernel, shape, stats, lax.ppermute(stats, "core", [(0, 1), (1, 0)]))
    stats = small_call(y_merge_kernel, shape, stats, *swaps(stats, "y"))
    coef, misc = small_call(
        x_merge_kernel,
        [jax.ShapeDtypeStruct((8, BOTH), f32), jax.ShapeDtypeStruct((EXTRA, D), bf16)],
        ids, loss_scale.reshape(1), stats, *swaps(stats, "x"), mine, other, row_sum,
        smem=(0, 1),
    )

    step_shape = jax.ShapeDtypeStruct((CHUNK + EXTRA, D), bf16)
    half_a, half_b, *near, send = grads(ids, prototypes, center, mine, other, coef, misc)
    got_a, got_b = ring(half_a, one_way), ring(half_b, other_way)
    part = D // (X * Y)
    got = lax.all_to_all(send.reshape(PEERS, part, ROWS), peers, 0, 0)
    own = small_call(du_sum_kernel, jax.ShapeDtypeStruct((X * Y, part, ROWS), bf16), got)
    du = lax.all_to_all(own, ("x", "y"), 0, 0)
    for i in range(3):
        if i == 0:
            kernel_a = functools.partial(halves_kernel, 0, True)
            kernel_b = functools.partial(halves_kernel, 1, False)
        else:
            kernel_a = kernel_b = step_kernel
        send_a = small_call(kernel_a, step_shape, near[2 * i], got_a, misc)
        send_b = small_call(kernel_b, step_shape, near[2 * i + 1], got_b, misc)
        if i == 2:
            send_a, send_b, du = lax.optimization_barrier((send_a, send_b, du))
        got_a, got_b = ring(send_a, one_way), ring(send_b, other_way)
    proto_grad, patch_center, loss = finish(near[6], got_a, got_b, misc, prototypes)
    student_grad = small_call(
        final_kernel,
        jax.ShapeDtypeStruct(student_rows.shape, f32),
        mask_count, mask_index, student_rows, du.reshape(D, ROWS),
        smem=(0,),
    )
    return (loss.reshape(()), student_grad, proto_grad, patch_center.reshape(-1))


def solution(mesh):
    fine = Mesh(mesh.devices.reshape(Z, CORES, X, Y), ("z", "core", "x", "y"))
    dp, proto = ("z", "core"), ("x", "y")
    in_specs = (
        P(dp, None, None),
        P(dp, None, None),
        P(None, proto),
        P(proto),
        P(dp, None),
        P(dp),
        P(),
    )
    out_specs = (P(), P(dp, None, None), P(proto + dp, None), P(proto))
    return jax.shard_map(shards, mesh=fine, in_specs=in_specs, out_specs=out_specs, check_vma=False)
```

```python
import functools
import math

import jax
import jax.numpy as jnp
from jax import lax
from jax.experimental import pallas as pl
from jax.experimental.pallas import tpu as pltpu
from jax.sharding import Mesh, PartitionSpec as P

bf16 = jnp.bfloat16
f32 = jnp.float32
log2e = math.log2(math.e)
ln2 = math.log(2.0)
t_scale = log2e / 0.04
s_scale = log2e / 0.1
inverse_temp = 10.0
norm_epsilon = 1e-06
low = -1e30

Z, CORES, X, Y = 8, 2, 4, 4
D = 256
SLOTS = 128
IMAGES = 64
TOTAL = 4096
LOCAL = 4
ROWS = LOCAL * SLOTS
BOTH = 2 * ROWS
CHUNK = 512
TILE = 512
STAT_TILE = 256
EXTRA = 32
HELD = ROWS + 16
STATS = 5
PEERS = CORES * X * Y
OFFSETS = (4, -3, 3, -2, 2, -1, 1, 0)
PIECES = 4

NT = (((1,), (1,)), ((), ()))
TN = (((0,), (0,)), ((), ()))


def dot(a, b, dims=(((1,), (0,)), ((), ()))):
    return lax.dot_general(a, b, dims, preferred_element_type=f32)


def params(mebibytes=16):
    return pltpu.CompilerParams(vmem_limit_bytes=mebibytes * 1024 * 1024)


def cost(flops, nbytes, trans=0):
    return pl.CostEstimate(flops=flops, bytes_accessed=nbytes, transcendentals=trans)


def picks(index_ref, count, i):
    patch = lax.broadcasted_iota(jnp.int32, (D, SLOTS), 0)
    slot = lax.broadcasted_iota(jnp.int32, (D, SLOTS), 1)
    hit = (patch == index_ref[i : i + 1, :]) & (slot < count)
    return jnp.where(hit, 1.0, 0.0).astype(bf16)


def unit_rows(values):
    length = jnp.sqrt(jnp.sum(values * values, axis=1, keepdims=True) + norm_epsilon)
    return values / length, length


def prep_kernel(count_ref, index_ref, s_ref, t_ref, out_ref, info_ref):
    for i in range(LOCAL):
        pick = picks(index_ref, count_ref[i], i)
        for which, ref in enumerate((s_ref, t_ref)):
            unit, _ = unit_rows(dot(pick, ref[i], TN))
            out_ref[which, i * SLOTS : (i + 1) * SLOTS, :] = unit.astype(bf16)
    row = lax.broadcasted_iota(jnp.int32, (HELD - ROWS, D), 0)
    counts = jnp.zeros((HELD - ROWS, D), jnp.int32)
    for i in range(LOCAL):
        counts = jnp.where(row == i, count_ref[i], counts)
    counts = counts.astype(f32)
    for which in range(2):
        out_ref[which, ROWS:, :] = counts.astype(bf16)
    info_ref[:LOCAL, :] = counts[:LOCAL, :SLOTS]
    info_ref[LOCAL:, :] = index_ref[...].astype(f32)


def prep(count, index, student, teacher):
    smem = pl.BlockSpec(memory_space=pltpu.SMEM)
    vmem = pl.BlockSpec(memory_space=pltpu.VMEM)
    return pl.pallas_call(
        prep_kernel,
        out_shape=[jax.ShapeDtypeStruct((2, HELD, D), bf16), jax.ShapeDtypeStruct((2 * LOCAL, SLOTS), f32)],
        in_specs=[smem, vmem, vmem, vmem],
        out_specs=[vmem, vmem],
        compiler_params=params(),
        cost_estimate=cost(2 * 2 * ROWS * D * D, 1 << 21),
    )(count, index, student, teacher)


def wide(block, times):
    return jnp.concatenate([block] * times, axis=1)


def chunk_columns(i, core):
    return pl.ds(pl.multiple_of((CORES * i + core) * CHUNK, CHUNK), CHUNK)


def turned(held):
    return jnp.broadcast_to(held * -t_scale, (128, CHUNK)).T


def stats_kernel(ids_ref, p_ref, c_ref, mine_ref, other_ref, block, sum_ref, acc):
    groups = (CHUNK // 8, 8, STAT_TILE)
    for i in range(Z):
        columns = chunk_columns(i, ids_ref[1])
        protos = p_ref[:, columns].T
        shift = wide(turned(c_ref[:, columns]), STAT_TILE // 128)
        for half, ref in enumerate((mine_ref, other_ref)):
            for j in range(ROWS // STAT_TILE):
                rows = slice(j * STAT_TILE, (j + 1) * STAT_TILE)
                at = slice(half * ROWS + j * STAT_TILE, half * ROWS + (j + 1) * STAT_TILE)
                t_arg = (dot(protos, ref[1, rows, :], NT) * t_scale + shift).reshape(groups)
                s_arg = (dot(protos, ref[0, rows, :], NT) * s_scale).reshape(groups)
                t_top = jnp.max(t_arg, axis=0)
                s_top = jnp.max(s_arg, axis=0)
                t_exp = jnp.exp2(t_arg - t_top[None])
                s_exp = jnp.exp2(s_arg - s_top[None])
                acc[0, i, :, at] = t_top
                acc[1, i, :, at] = jnp.sum(t_exp, axis=0)
                acc[2, i, :, at] = jnp.sum(t_exp * s_arg, axis=0)
                acc[3, i, :, at] = s_top
                acc[4, i, :, at] = jnp.sum(s_exp, axis=0)
    for g in range(BOTH // 128):
        at = slice(g * 128, (g + 1) * 128)
        parts = [acc[q, :, :, at].reshape(Z * 8, 128) for q in range(STATS)]
        t_top = jnp.max(parts[0], axis=0, keepdims=True)
        s_top = jnp.max(parts[3], axis=0, keepdims=True)
        t_keep = jnp.exp2(parts[0] - t_top)
        s_keep = jnp.exp2(parts[3] - s_top)
        merged_rows = (
            t_top,
            jnp.sum(parts[1] * t_keep, axis=0, keepdims=True),
            jnp.sum(parts[2] * t_keep, axis=0, keepdims=True),
            s_top,
            jnp.sum(parts[4] * s_keep, axis=0, keepdims=True),
        )
        for q in range(STATS):
            block[q * 8 + g : q * 8 + g + 1, :] = merged_rows[q]
    first = jnp.sum(mine_ref[1, :ROWS, :].astype(f32), axis=0, keepdims=True)
    second = jnp.sum(other_ref[1, :ROWS, :].astype(f32), axis=0, keepdims=True)
    sum_ref[...] = jnp.broadcast_to(first + second, (8, D))


def local_stats(ids, prototypes, center, mine, other):
    smem = pl.BlockSpec(memory_space=pltpu.SMEM)
    vmem = pl.BlockSpec(memory_space=pltpu.VMEM)
    return pl.pallas_call(
        stats_kernel,
        in_specs=[smem, vmem, vmem, vmem, vmem],
        out_specs=[vmem] * 2,
        out_shape=[jax.ShapeDtypeStruct((STATS * 8, 128), f32), jax.ShapeDtypeStruct((8, D), f32)],
        scratch_shapes=[pltpu.VMEM((STATS, Z, 8, BOTH), f32)],
        compiler_params=params(24),
        cost_estimate=cost(4 * BOTH * Z * CHUNK * D, 6 << 20, 2 * BOTH * Z * CHUNK),
    )(ids, prototypes, center, mine, other)


def split3(value):
    top = value.astype(bf16)
    rest = value - top.astype(f32)
    middle = rest.astype(bf16)
    return top, middle, (rest - middle.astype(f32)).astype(bf16)


def tree(parts):
    while len(parts) > 1:
        parts = [parts[i] + parts[i + 1] for i in range(0, len(parts), 2)]
    return parts[0]


def merge(parts):
    t_top = functools.reduce(jnp.maximum, [p[0] for p in parts])
    s_top = functools.reduce(jnp.maximum, [p[3] for p in parts])
    t_keep = [jnp.exp2(p[0] - t_top) for p in parts]
    s_keep = [jnp.exp2(p[3] - s_top) for p in parts]
    t_sum = tree([p[1] * k for p, k in zip(parts, t_keep)])
    cross = tree([p[2] * k for p, k in zip(parts, t_keep)])
    s_sum = tree([p[4] * k for p, k in zip(parts, s_keep)])
    return t_top, t_sum, cross, s_top, s_sum


def flip(value):
    return jnp.concatenate([value[LOCAL:], value[:LOCAL]], axis=0)


def rows_of(ref):
    return [ref[q * 8 : (q + 1) * 8, :] for q in range(STATS)]


def core_merge_kernel(mine_ref, got_ref, out_ref):
    parts = [rows_of(mine_ref), [flip(value) for value in rows_of(got_ref)]]
    for q, value in enumerate(merge(parts)):
        out_ref[q * 8 : (q + 1) * 8, :] = value


def y_merge_kernel(a, b, c, d, out_ref):
    for q, value in enumerate(merge([rows_of(ref) for ref in (a, b, c, d)])):
        out_ref[q * 8 : (q + 1) * 8, :] = value


def x_merge_kernel(ids_ref, scale_ref, a, b, c, d, mine_ref, other_ref, sum_ref, coef_ref, misc_ref):
    t_top, t_sum, cross, s_top, s_sum = merge([rows_of(ref) for ref in (a, b, c, d)])
    counts = [ref[0, ROWS:, :128].astype(f32)[:LOCAL] for ref in (mine_ref, other_ref)]
    count = jnp.concatenate(counts, axis=0)
    slot = lax.broadcasted_iota(jnp.int32, (8, 128), 1).astype(f32)
    live = slot < count
    weight = 1.0 / (IMAGES * jnp.maximum(count, 1.0))
    s_lse = s_top + jnp.log2(s_sum)
    ce = (s_lse - cross / t_sum) * ln2
    factor = jnp.log2(weight * (scale_ref[0] * inverse_temp))
    s_coef = jnp.where(live, factor - s_lse, low)
    t_coef = jnp.where(live, factor - t_top - jnp.log2(t_sum), low)
    for g in range(8):
        coef_ref[0:1, g * 128 : (g + 1) * 128] = s_coef[g : g + 1]
        coef_ref[1:2, g * 128 : (g + 1) * 128] = t_coef[g : g + 1]
    coef_ref[2:8, :] = jnp.zeros((6, BOTH), f32)
    part = jnp.sum(jnp.where(live, weight * ce, 0.0), axis=1, keepdims=True)
    first = jnp.sum(part[:LOCAL], axis=0, keepdims=True)
    second = jnp.sum(part[LOCAL:], axis=0, keepdims=True)
    row = lax.broadcasted_iota(jnp.int32, (EXTRA, D), 0)
    mine = jnp.bitwise_and(row, Z - 1) == ids_ref[0]
    row_sum = split3(sum_ref[0:1, :])
    losses = split3(jnp.broadcast_to(first + second, (1, D)))
    block = jnp.zeros((EXTRA, D), f32)
    for i in range(2):
        block = jnp.where(row // Z == i, row_sum[i].astype(f32), block)
        block = jnp.where(row // Z == 2 + i, losses[i].astype(f32), block)
    misc_ref[...] = jnp.where(mine, block, 0.0).astype(bf16)


def small_call(kernel, out_shape, *args, smem=()):
    specs = [
        pl.BlockSpec(memory_space=pltpu.SMEM if i in smem else pltpu.VMEM) for i in range(len(args))
    ]
    vmem = pl.BlockSpec(memory_space=pltpu.VMEM)
    return pl.pallas_call(
        kernel,
        out_shape=out_shape,
        in_specs=specs,
        out_specs=jax.tree.map(lambda _: vmem, out_shape),
        compiler_params=params(),
        cost_estimate=cost(1 << 20, 1 << 18),
    )(*args)


def grad_kernel(ids_ref, p_ref, c_ref, mine_ref, other_ref, coef_ref, misc_ref, *refs):
    n = len(OFFSETS)
    outs, send_ref, du_ref = refs[: n + 1], refs[n + 1], refs[n + 2]
    core = ids_ref[1]
    order = [lax.rem(ids_ref[0] + Z + d * (1 - 2 * core), Z) for d in OFFSETS]
    for i in range(n):
        columns = chunk_columns(order[i], core)
        wide_p = p_ref[:, columns]
        protos = wide_p.T
        shift = wide(turned(c_ref[:, columns]), TILE // 128)
        total = None
        for half, ref in enumerate((mine_ref, other_ref)):
            for j in range(ROWS // TILE):
                rows = slice(j * TILE, (j + 1) * TILE)
                at = slice(half * ROWS + j * TILE, half * ROWS + (j + 1) * TILE)
                s_rows = ref[0, rows, :]
                t_arg = dot(protos, ref[1, rows, :], NT) * t_scale + shift + coef_ref[1:2, at]
                s_arg = dot(protos, s_rows, NT) * s_scale + coef_ref[0:1, at]
                dlogit = (jnp.exp2(s_arg) - jnp.exp2(t_arg)).astype(bf16)
                part = dot(dlogit, s_rows)
                total = part if total is None else total + part
                du = dot(wide_p, dlogit)
                if i == 0:
                    du_ref[:, at] = du
                else:
                    du_ref[:, at] += du
        if i == 0:
            half = CHUNK // 2
            outs[0][:half, :] = total[:half].astype(bf16)
            outs[0][half:, :] = misc_ref[...]
            outs[1][...] = total[half:].astype(bf16)
        else:
            outs[i + 1][...] = total.astype(bf16)
    send_ref[core] = du_ref[:, :ROWS].astype(bf16)
    send_ref[1 - core] = du_ref[:, ROWS:].astype(bf16)


def grads(ids, prototypes, center, mine, other, coef, misc):
    smem = pl.BlockSpec(memory_space=pltpu.SMEM)
    vmem = pl.BlockSpec(memory_space=pltpu.VMEM)
    n = len(OFFSETS)
    shapes = [(CHUNK // 2 + EXTRA, D), (CHUNK // 2, D)] + [(CHUNK, D)] * (n - 1) + [(CORES, D, ROWS)]
    return pl.pallas_call(
        grad_kernel,
        in_specs=[smem] + [vmem] * 6,
        out_specs=[vmem] * len(shapes),
        out_shape=[jax.ShapeDtypeStruct(shape, bf16) for shape in shapes],
        scratch_shapes=[pltpu.VMEM((D, BOTH), f32)],
        compiler_params=params(24),
        cost_estimate=cost(8 * BOTH * n * CHUNK * D, n << 20, 2 * BOTH * n * CHUNK),
    )(ids, prototypes, center, mine, other, coef, misc)


def du_sum_kernel(got_ref, out_ref):
    total = jnp.sum(got_ref[...].astype(f32), axis=0).astype(bf16)
    out_ref[...] = jnp.broadcast_to(total[None], (X * Y,) + total.shape)


def halves_kernel(offset, with_extra, far_ref, got_ref, misc_ref, out_ref):
    half = CHUNK // 2
    for i in range(2):
        rows = slice(i * half, (i + 1) * half)
        part = far_ref[rows, :].astype(f32)
        if i == offset:
            part = part + got_ref[:half, :].astype(f32)
        out_ref[rows, :] = part.astype(bf16)
    extra = misc_ref[...]
    if with_extra:
        extra = extra + got_ref[half:, :]
    out_ref[CHUNK:, :] = extra


def step_kernel(near_ref, got_ref, misc_ref, out_ref):
    out_ref[:CHUNK, :] = (near_ref[...].astype(f32) + got_ref[:CHUNK, :].astype(f32)).astype(bf16)
    out_ref[CHUNK:, :] = misc_ref[...] + got_ref[CHUNK:, :]


def finish_kernel(near_ref, a_ref, b_ref, misc_ref, p_ref, grad_ref, center_ref, loss_ref):
    width = p_ref.shape[1] // PIECES
    pieces = [pl.ds(i * width, width) for i in range(PIECES)]
    total = near_ref[...].astype(f32) + a_ref[:CHUNK, :].astype(f32)
    grad_ref[...] = total + b_ref[:CHUNK, :].astype(f32)
    extra = (misc_ref[...] + a_ref[CHUNK:, :] + b_ref[CHUNK:, :]).astype(f32)
    first = extra[0:8] + extra[8:16]
    loss = extra[16:24] + extra[24:32]
    total = jnp.broadcast_to(jnp.sum(first, axis=0, keepdims=True), (16, D))
    loss_ref[0, 0] = jnp.sum(loss[:, 0:1])
    stacked = jnp.concatenate(split3(total), axis=0)
    for at in pieces:
        three = dot(stacked, p_ref[:, at])
        center_ref[:, at] = (three[0:1] + three[16:17] + three[32:33]) * (1.0 / TOTAL)


def finish(near, a, b, misc, prototypes):
    width = prototypes.shape[1]
    smem = pl.BlockSpec(memory_space=pltpu.SMEM)
    vmem = pl.BlockSpec(memory_space=pltpu.VMEM)
    return pl.pallas_call(
        finish_kernel,
        in_specs=[vmem] * 5,
        out_specs=[vmem, vmem, smem],
        out_shape=[
            jax.ShapeDtypeStruct((CHUNK, D), f32),
            jax.ShapeDtypeStruct((1, width), f32),
            jax.ShapeDtypeStruct((1, 1), f32),
        ],
        compiler_params=params(),
        cost_estimate=cost(6 * 8 * D * width, 5 << 20),
    )(near, a, b, misc, prototypes)


def final_kernel(info_ref, s_ref, du_ref, out_ref):
    for i in range(LOCAL):
        patch = lax.broadcasted_iota(jnp.int32, (D, SLOTS), 0).astype(f32)
        slot = lax.broadcasted_iota(jnp.int32, (D, SLOTS), 1).astype(f32)
        hit = (patch == info_ref[LOCAL + i : LOCAL + i + 1, :]) & (slot < info_ref[i : i + 1, :])
        pick = jnp.where(hit, 1.0, 0.0).astype(bf16)
        unit, length = unit_rows(dot(pick, s_ref[i], TN))
        d_unit = du_ref[:, i * SLOTS : (i + 1) * SLOTS].astype(f32).T
        row = (d_unit - unit * jnp.sum(unit * d_unit, axis=1, keepdims=True)) / length
        top = row.astype(bf16)
        rest = (row - top.astype(f32)).astype(bf16)
        out_ref[i] = dot(pick, top) + dot(pick, rest)


def shards(student_rows, teacher_rows, prototypes, center, mask_index, mask_count, loss_scale):
    z, core, x, y = (lax.axis_index(a) for a in ("z", "core", "x", "y"))
    ids = jnp.stack([z, core, x, y]).astype(jnp.int32)
    peers = ("core", "x", "y")
    one_way, other_way = [], []
    for i in range(Z):
        below, above, here = (i - 1) % Z * CORES, (i + 1) % Z * CORES, i * CORES
        one_way += [(here, below), (here + 1, above + 1)]
        other_way += [(here, above), (here + 1, below + 1)]

    def swaps(value, axis):
        return [lax.ppermute(value, axis, [(i, i ^ k) for i in range(4)]) for k in (1, 2, 3)]

    def ring(value, pairs):
        return lax.ppermute(value, ("z", "core"), pairs)

    mine, info = prep(mask_count, mask_index, student_rows, teacher_rows)
    other = lax.ppermute(mine, "core", [(0, 1), (1, 0)])
    center = center.reshape(1, -1)
    stats, row_sum = local_stats(ids, prototypes, center, mine, other)
    shape = jax.ShapeDtypeStruct((STATS * 8, 128), f32)
    stats = small_call(core_merge_kernel, shape, stats, lax.ppermute(stats, "core", [(0, 1), (1, 0)]))
    stats = small_call(y_merge_kernel, shape, stats, *swaps(stats, "y"))
    coef, misc = small_call(
        x_merge_kernel,
        [jax.ShapeDtypeStruct((8, BOTH), f32), jax.ShapeDtypeStruct((EXTRA, D), bf16)],
        ids, loss_scale.reshape(1), stats, *swaps(stats, "x"), mine, other, row_sum,
        smem=(0, 1),
    )

    step_shape = jax.ShapeDtypeStruct((CHUNK + EXTRA, D), bf16)
    half_a, half_b, *near, send = grads(ids, prototypes, center, mine, other, coef, misc)
    got_a, got_b = ring(half_a, one_way), ring(half_b, other_way)
    part = D // (X * Y)
    got = lax.all_to_all(send.reshape(PEERS, part, ROWS), peers, 0, 0)
    own = small_call(du_sum_kernel, jax.ShapeDtypeStruct((X * Y, part, ROWS), bf16), got)
    for i in range(3):
        if i == 0:
            kernel_a = functools.partial(halves_kernel, 0, True)
            kernel_b = functools.partial(halves_kernel, 1, False)
        else:
            kernel_a = kernel_b = step_kernel
        send_a = small_call(kernel_a, step_shape, near[2 * i], got_a, misc)
        send_b = small_call(kernel_b, step_shape, near[2 * i + 1], got_b, misc)
        if i == 2:
            send_a, send_b, own = lax.optimization_barrier((send_a, send_b, own))
            du = lax.all_to_all(own, ("x", "y"), 0, 0)
        got_a, got_b = ring(send_a, one_way), ring(send_b, other_way)
    proto_grad, patch_center, loss = finish(near[6], got_a, got_b, misc, prototypes)
    student_grad = small_call(
        final_kernel,
        jax.ShapeDtypeStruct(student_rows.shape, f32),
        info, student_rows, du.reshape(D, ROWS),
    )
    return (loss.reshape(()), student_grad, proto_grad, patch_center.reshape(-1))


def solution(mesh):
    fine = Mesh(mesh.devices.reshape(Z, CORES, X, Y), ("z", "core", "x", "y"))
    dp, proto = ("z", "core"), ("x", "y")
    in_specs = (
        P(dp, None, None),
        P(dp, None, None),
        P(None, proto),
        P(proto),
        P(dp, None),
        P(dp),
        P(),
    )
    out_specs = (P(), P(dp, None, None), P(proto + dp, None), P(proto))
    return jax.shard_map(shards, mesh=fine, in_specs=in_specs, out_specs=out_specs, check_vma=False)
```

```python
import functools
import math

import jax
import jax.numpy as jnp
from jax import lax
from jax.experimental import pallas as pl
from jax.experimental.pallas import tpu as pltpu
from jax.sharding import Mesh, PartitionSpec as P

bf16 = jnp.bfloat16
f32 = jnp.float32
log2e = math.log2(math.e)
ln2 = math.log(2.0)
t_scale = log2e / 0.04
s_scale = log2e / 0.1
inverse_temp = 10.0
norm_epsilon = 1e-06
low = -1e30

Z, CORES, X, Y = 8, 2, 4, 4
D = 256
SLOTS = 128
IMAGES = 64
TOTAL = 4096
LOCAL = 4
ROWS = LOCAL * SLOTS
BOTH = 2 * ROWS
CHUNK = 512
TILE = 512
STAT_TILE = 256
EXTRA = 32
HELD = ROWS + 16
STATS = 5
PEERS = CORES * X * Y
OFFSETS = (4, -3, 3, -2, 2, -1, 1, 0)
PIECES = 4

NT = (((1,), (1,)), ((), ()))
TN = (((0,), (0,)), ((), ()))


def dot(a, b, dims=(((1,), (0,)), ((), ()))):
    return lax.dot_general(a, b, dims, preferred_element_type=f32)


def params(mebibytes=16):
    return pltpu.CompilerParams(vmem_limit_bytes=mebibytes * 1024 * 1024)


def cost(flops, nbytes, trans=0):
    return pl.CostEstimate(flops=flops, bytes_accessed=nbytes, transcendentals=trans)


def picks(index_ref, count, i):
    patch = lax.broadcasted_iota(jnp.int32, (D, SLOTS), 0)
    slot = lax.broadcasted_iota(jnp.int32, (D, SLOTS), 1)
    hit = (patch == index_ref[i : i + 1, :]) & (slot < count)
    return jnp.where(hit, 1.0, 0.0).astype(bf16)


def unit_rows(values):
    length = jnp.sqrt(jnp.sum(values * values, axis=1, keepdims=True) + norm_epsilon)
    return values / length, length


def prep_kernel(count_ref, index_ref, s_ref, t_ref, out_ref, info_ref):
    for i in range(LOCAL):
        pick = picks(index_ref, count_ref[i], i)
        for which, ref in enumerate((s_ref, t_ref)):
            unit, _ = unit_rows(dot(pick, ref[i], TN))
            out_ref[which, i * SLOTS : (i + 1) * SLOTS, :] = unit.astype(bf16)
    row = lax.broadcasted_iota(jnp.int32, (HELD - ROWS, D), 0)
    counts = jnp.zeros((HELD - ROWS, D), jnp.int32)
    for i in range(LOCAL):
        counts = jnp.where(row == i, count_ref[i], counts)
    counts = counts.astype(f32)
    for which in range(2):
        out_ref[which, ROWS:, :] = counts.astype(bf16)
    info_ref[:LOCAL, :] = counts[:LOCAL, :SLOTS]
    info_ref[LOCAL:, :] = index_ref[...].astype(f32)


def prep(count, index, student, teacher):
    smem = pl.BlockSpec(memory_space=pltpu.SMEM)
    vmem = pl.BlockSpec(memory_space=pltpu.VMEM)
    return pl.pallas_call(
        prep_kernel,
        out_shape=[jax.ShapeDtypeStruct((2, HELD, D), bf16), jax.ShapeDtypeStruct((2 * LOCAL, SLOTS), f32)],
        in_specs=[smem, vmem, vmem, vmem],
        out_specs=[vmem, vmem],
        compiler_params=params(),
        cost_estimate=cost(2 * 2 * ROWS * D * D, 1 << 21),
    )(count, index, student, teacher)


def wide(block, times):
    return jnp.concatenate([block] * times, axis=1)


def chunk_columns(i):
    return pl.ds(i * CHUNK, CHUNK) if isinstance(i, int) else pl.ds(pl.multiple_of(i * CHUNK, CHUNK), CHUNK)


def turned(held):
    return jnp.broadcast_to(held * -t_scale, (128, CHUNK)).T


def stats_kernel(ids_ref, p_ref, c_ref, mine_ref, other_ref, block, sum_ref, acc):
    groups = (CHUNK // 8, 8, STAT_TILE)
    for i in range(Z):
        columns = chunk_columns(i)
        protos = p_ref[:, columns].T
        shift = wide(turned(c_ref[:, columns]), STAT_TILE // 128)
        for half, ref in enumerate((mine_ref, other_ref)):
            for j in range(ROWS // STAT_TILE):
                rows = slice(j * STAT_TILE, (j + 1) * STAT_TILE)
                at = slice(half * ROWS + j * STAT_TILE, half * ROWS + (j + 1) * STAT_TILE)
                t_arg = (dot(protos, ref[1, rows, :], NT) * t_scale + shift).reshape(groups)
                s_arg = (dot(protos, ref[0, rows, :], NT) * s_scale).reshape(groups)
                t_top = jnp.max(t_arg, axis=0)
                s_top = jnp.max(s_arg, axis=0)
                t_exp = jnp.exp2(t_arg - t_top[None])
                s_exp = jnp.exp2(s_arg - s_top[None])
                acc[0, i, :, at] = t_top
                acc[1, i, :, at] = jnp.sum(t_exp, axis=0)
                acc[2, i, :, at] = jnp.sum(t_exp * s_arg, axis=0)
                acc[3, i, :, at] = s_top
                acc[4, i, :, at] = jnp.sum(s_exp, axis=0)
    for g in range(BOTH // 128):
        at = slice(g * 128, (g + 1) * 128)
        parts = [acc[q, :, :, at].reshape(Z * 8, 128) for q in range(STATS)]
        t_top = jnp.max(parts[0], axis=0, keepdims=True)
        s_top = jnp.max(parts[3], axis=0, keepdims=True)
        t_keep = jnp.exp2(parts[0] - t_top)
        s_keep = jnp.exp2(parts[3] - s_top)
        merged_rows = (
            t_top,
            jnp.sum(parts[1] * t_keep, axis=0, keepdims=True),
            jnp.sum(parts[2] * t_keep, axis=0, keepdims=True),
            s_top,
            jnp.sum(parts[4] * s_keep, axis=0, keepdims=True),
        )
        for q in range(STATS):
            block[q * 8 + g : q * 8 + g + 1, :] = merged_rows[q]
    first = jnp.sum(mine_ref[1, :ROWS, :].astype(f32), axis=0, keepdims=True)
    second = jnp.sum(other_ref[1, :ROWS, :].astype(f32), axis=0, keepdims=True)
    sum_ref[...] = jnp.broadcast_to(first + second, (8, D))


def local_stats(ids, prototypes, center, mine, other):
    smem = pl.BlockSpec(memory_space=pltpu.SMEM)
    vmem = pl.BlockSpec(memory_space=pltpu.VMEM)
    return pl.pallas_call(
        stats_kernel,
        in_specs=[smem, vmem, vmem, vmem, vmem],
        out_specs=[vmem] * 2,
        out_shape=[jax.ShapeDtypeStruct((STATS * 8, 128), f32), jax.ShapeDtypeStruct((8, D), f32)],
        scratch_shapes=[pltpu.VMEM((STATS, Z, 8, BOTH), f32)],
        compiler_params=params(24),
        cost_estimate=cost(4 * BOTH * Z * CHUNK * D, 6 << 20, 2 * BOTH * Z * CHUNK),
    )(ids, prototypes, center, mine, other)


def split3(value):
    top = value.astype(bf16)
    rest = value - top.astype(f32)
    middle = rest.astype(bf16)
    return top, middle, (rest - middle.astype(f32)).astype(bf16)


def tree(parts):
    while len(parts) > 1:
        parts = [parts[i] + parts[i + 1] for i in range(0, len(parts), 2)]
    return parts[0]


def merge(parts):
    t_top = functools.reduce(jnp.maximum, [p[0] for p in parts])
    s_top = functools.reduce(jnp.maximum, [p[3] for p in parts])
    t_keep = [jnp.exp2(p[0] - t_top) for p in parts]
    s_keep = [jnp.exp2(p[3] - s_top) for p in parts]
    t_sum = tree([p[1] * k for p, k in zip(parts, t_keep)])
    cross = tree([p[2] * k for p, k in zip(parts, t_keep)])
    s_sum = tree([p[4] * k for p, k in zip(parts, s_keep)])
    return t_top, t_sum, cross, s_top, s_sum


def flip(value):
    return jnp.concatenate([value[LOCAL:], value[:LOCAL]], axis=0)


def rows_of(ref):
    return [ref[q * 8 : (q + 1) * 8, :] for q in range(STATS)]


def core_merge_kernel(mine_ref, got_ref, out_ref):
    parts = [rows_of(mine_ref), [flip(value) for value in rows_of(got_ref)]]
    for q, value in enumerate(merge(parts)):
        out_ref[q * 8 : (q + 1) * 8, :] = value


def y_merge_kernel(a, b, c, d, out_ref):
    for q, value in enumerate(merge([rows_of(ref) for ref in (a, b, c, d)])):
        out_ref[q * 8 : (q + 1) * 8, :] = value


def x_merge_kernel(ids_ref, scale_ref, a, b, c, d, mine_ref, other_ref, sum_ref, coef_ref, misc_ref):
    t_top, t_sum, cross, s_top, s_sum = merge([rows_of(ref) for ref in (a, b, c, d)])
    counts = [ref[0, ROWS:, :128].astype(f32)[:LOCAL] for ref in (mine_ref, other_ref)]
    count = jnp.concatenate(counts, axis=0)
    slot = lax.broadcasted_iota(jnp.int32, (8, 128), 1).astype(f32)
    live = slot < count
    weight = 1.0 / (IMAGES * jnp.maximum(count, 1.0))
    s_lse = s_top + jnp.log2(s_sum)
    ce = (s_lse - cross / t_sum) * ln2
    factor = jnp.log2(weight * (scale_ref[0] * inverse_temp))
    s_coef = jnp.where(live, factor - s_lse, low)
    t_coef = jnp.where(live, factor - t_top - jnp.log2(t_sum), low)
    for g in range(8):
        coef_ref[0:1, g * 128 : (g + 1) * 128] = s_coef[g : g + 1]
        coef_ref[1:2, g * 128 : (g + 1) * 128] = t_coef[g : g + 1]
    coef_ref[2:8, :] = jnp.zeros((6, BOTH), f32)
    part = jnp.sum(jnp.where(live, weight * ce, 0.0), axis=1, keepdims=True)
    first = jnp.sum(part[:LOCAL], axis=0, keepdims=True)
    second = jnp.sum(part[LOCAL:], axis=0, keepdims=True)
    row = lax.broadcasted_iota(jnp.int32, (EXTRA, D), 0)
    mine = jnp.bitwise_and(row, Z - 1) == ids_ref[0]
    row_sum = split3(sum_ref[0:1, :])
    losses = split3(jnp.broadcast_to(first + second, (1, D)))
    block = jnp.zeros((EXTRA, D), f32)
    for i in range(2):
        block = jnp.where(row // Z == i, row_sum[i].astype(f32), block)
        block = jnp.where(row // Z == 2 + i, losses[i].astype(f32), block)
    misc_ref[...] = jnp.where(mine, block, 0.0).astype(bf16)


def small_call(kernel, out_shape, *args, smem=()):
    specs = [
        pl.BlockSpec(memory_space=pltpu.SMEM if i in smem else pltpu.VMEM) for i in range(len(args))
    ]
    vmem = pl.BlockSpec(memory_space=pltpu.VMEM)
    return pl.pallas_call(
        kernel,
        out_shape=out_shape,
        in_specs=specs,
        out_specs=jax.tree.map(lambda _: vmem, out_shape),
        compiler_params=params(),
        cost_estimate=cost(1 << 20, 1 << 18),
    )(*args)


def grad_kernel(ids_ref, p_ref, c_ref, mine_ref, other_ref, coef_ref, misc_ref, *refs):
    n = len(OFFSETS)
    outs, send_ref, du_ref = refs[: n + 1], refs[n + 1], refs[n + 2]
    core = ids_ref[1]
    order = [lax.rem(ids_ref[0] + Z + d * (1 - 2 * core), Z) for d in OFFSETS]
    for i in range(n):
        columns = chunk_columns(order[i])
        wide_p = p_ref[:, columns]
        protos = wide_p.T
        shift = wide(turned(c_ref[:, columns]), TILE // 128)
        total = None
        for half, ref in enumerate((mine_ref, other_ref)):
            for j in range(ROWS // TILE):
                rows = slice(j * TILE, (j + 1) * TILE)
                at = slice(half * ROWS + j * TILE, half * ROWS + (j + 1) * TILE)
                s_rows = ref[0, rows, :]
                t_arg = dot(protos, ref[1, rows, :], NT) * t_scale + shift + coef_ref[1:2, at]
                s_arg = dot(protos, s_rows, NT) * s_scale + coef_ref[0:1, at]
                dlogit = (jnp.exp2(s_arg) - jnp.exp2(t_arg)).astype(bf16)
                part = dot(dlogit, s_rows)
                total = part if total is None else total + part
                du = dot(wide_p, dlogit)
                if i == 0:
                    du_ref[:, at] = du
                else:
                    du_ref[:, at] += du
        if i == 0:
            half = CHUNK // 2
            outs[0][:half, :] = total[:half].astype(bf16)
            outs[0][half:, :] = misc_ref[...]
            outs[1][...] = total[half:].astype(bf16)
        else:
            outs[i + 1][...] = total.astype(bf16)
    send_ref[core] = du_ref[:, :ROWS].astype(bf16)
    send_ref[1 - core] = du_ref[:, ROWS:].astype(bf16)


def grads(ids, prototypes, center, mine, other, coef, misc):
    smem = pl.BlockSpec(memory_space=pltpu.SMEM)
    vmem = pl.BlockSpec(memory_space=pltpu.VMEM)
    n = len(OFFSETS)
    shapes = [(CHUNK // 2 + EXTRA, D), (CHUNK // 2, D)] + [(CHUNK, D)] * (n - 1) + [(CORES, D, ROWS)]
    return pl.pallas_call(
        grad_kernel,
        in_specs=[smem] + [vmem] * 6,
        out_specs=[vmem] * len(shapes),
        out_shape=[jax.ShapeDtypeStruct(shape, bf16) for shape in shapes],
        scratch_shapes=[pltpu.VMEM((D, BOTH), f32)],
        compiler_params=params(24),
        cost_estimate=cost(8 * BOTH * n * CHUNK * D, n << 20, 2 * BOTH * n * CHUNK),
    )(ids, prototypes, center, mine, other, coef, misc)


def du_sum_kernel(got_ref, out_ref):
    total = jnp.sum(got_ref[...].astype(f32), axis=0).astype(bf16)
    out_ref[...] = jnp.broadcast_to(total[None], (X * Y,) + total.shape)


def halves_kernel(offset, with_extra, far_ref, got_ref, misc_ref, out_ref):
    half = CHUNK // 2
    for i in range(2):
        rows = slice(i * half, (i + 1) * half)
        part = far_ref[rows, :].astype(f32)
        if i == offset:
            part = part + got_ref[:half, :].astype(f32)
        out_ref[rows, :] = part.astype(bf16)
    extra = misc_ref[...]
    if with_extra:
        extra = extra + got_ref[half:, :]
    out_ref[CHUNK:, :] = extra


def step_kernel(near_ref, got_ref, misc_ref, out_ref):
    out_ref[:CHUNK, :] = (near_ref[...].astype(f32) + got_ref[:CHUNK, :].astype(f32)).astype(bf16)
    out_ref[CHUNK:, :] = misc_ref[...] + got_ref[CHUNK:, :]


def finish_kernel(near_ref, a_ref, b_ref, misc_ref, p_ref, grad_ref, center_ref, loss_ref):
    width = p_ref.shape[1] // PIECES
    pieces = [pl.ds(i * width, width) for i in range(PIECES)]
    total = near_ref[...].astype(f32) + a_ref[:CHUNK, :].astype(f32)
    grad_ref[...] = total + b_ref[:CHUNK, :].astype(f32)
    extra = (misc_ref[...] + a_ref[CHUNK:, :] + b_ref[CHUNK:, :]).astype(f32)
    first = extra[0:8] + extra[8:16]
    loss = extra[16:24] + extra[24:32]
    total = jnp.broadcast_to(jnp.sum(first, axis=0, keepdims=True), (16, D))
    loss_ref[0, 0] = jnp.sum(loss[:, 0:1])
    stacked = jnp.concatenate(split3(total), axis=0)
    for at in pieces:
        three = dot(stacked, p_ref[:, at])
        center_ref[:, at] = (three[0:1] + three[16:17] + three[32:33]) * (1.0 / TOTAL)


def finish(near, a, b, misc, prototypes):
    width = prototypes.shape[1]
    smem = pl.BlockSpec(memory_space=pltpu.SMEM)
    vmem = pl.BlockSpec(memory_space=pltpu.VMEM)
    return pl.pallas_call(
        finish_kernel,
        in_specs=[vmem] * 5,
        out_specs=[vmem, vmem, smem],
        out_shape=[
            jax.ShapeDtypeStruct((CHUNK, D), f32),
            jax.ShapeDtypeStruct((1, width), f32),
            jax.ShapeDtypeStruct((1, 1), f32),
        ],
        compiler_params=params(),
        cost_estimate=cost(6 * 8 * D * width, 5 << 20),
    )(near, a, b, misc, prototypes)


def final_kernel(info_ref, s_ref, du_ref, out_ref):
    for i in range(LOCAL):
        patch = lax.broadcasted_iota(jnp.int32, (D, SLOTS), 0).astype(f32)
        slot = lax.broadcasted_iota(jnp.int32, (D, SLOTS), 1).astype(f32)
        hit = (patch == info_ref[LOCAL + i : LOCAL + i + 1, :]) & (slot < info_ref[i : i + 1, :])
        pick = jnp.where(hit, 1.0, 0.0).astype(bf16)
        unit, length = unit_rows(dot(pick, s_ref[i], TN))
        d_unit = du_ref[:, i * SLOTS : (i + 1) * SLOTS].astype(f32).T
        row = (d_unit - unit * jnp.sum(unit * d_unit, axis=1, keepdims=True)) / length
        top = row.astype(bf16)
        rest = (row - top.astype(f32)).astype(bf16)
        out_ref[i] = dot(pick, top) + dot(pick, rest)


def shards(student_rows, teacher_rows, prototypes, center, mask_index, mask_count, loss_scale):
    z, core, x, y = (lax.axis_index(a) for a in ("z", "core", "x", "y"))
    ids = jnp.stack([z, core, x, y]).astype(jnp.int32)
    peers = ("core", "x", "y")
    one_way, other_way = [], []
    for i in range(Z):
        below, above, here = (i - 1) % Z * CORES, (i + 1) % Z * CORES, i * CORES
        one_way += [(here, below), (here + 1, above + 1)]
        other_way += [(here, above), (here + 1, below + 1)]

    def swaps(value, axis):
        return [lax.ppermute(value, axis, [(i, i ^ k) for i in range(4)]) for k in (1, 2, 3)]

    def ring(value, pairs):
        return lax.ppermute(value, ("z", "core"), pairs)

    mine, info = prep(mask_count, mask_index, student_rows, teacher_rows)
    other = lax.ppermute(mine, "core", [(0, 1), (1, 0)])
    center = center.reshape(1, -1)
    here = [(CORES * i + core) * CHUNK for i in range(Z)]
    half = jnp.concatenate([lax.dynamic_slice(prototypes, (0, at), (D, CHUNK)) for at in here], axis=1)
    center = jnp.concatenate([lax.dynamic_slice(center, (0, at), (1, CHUNK)) for at in here], axis=1)
    stats, row_sum = local_stats(ids, half, center, mine, other)
    shape = jax.ShapeDtypeStruct((STATS * 8, 128), f32)
    stats = small_call(core_merge_kernel, shape, stats, lax.ppermute(stats, "core", [(0, 1), (1, 0)]))
    stats = small_call(y_merge_kernel, shape, stats, *swaps(stats, "y"))
    coef, misc = small_call(
        x_merge_kernel,
        [jax.ShapeDtypeStruct((8, BOTH), f32), jax.ShapeDtypeStruct((EXTRA, D), bf16)],
        ids, loss_scale.reshape(1), stats, *swaps(stats, "x"), mine, other, row_sum,
        smem=(0, 1),
    )

    step_shape = jax.ShapeDtypeStruct((CHUNK + EXTRA, D), bf16)
    half_a, half_b, *near, send = grads(ids, half, center, mine, other, coef, misc)
    got_a, got_b = ring(half_a, one_way), ring(half_b, other_way)
    part = D // (X * Y)
    got = lax.all_to_all(send.reshape(PEERS, part, ROWS), peers, 0, 0)
    own = small_call(du_sum_kernel, jax.ShapeDtypeStruct((X * Y, part, ROWS), bf16), got)
    for i in range(3):
        if i == 0:
            kernel_a = functools.partial(halves_kernel, 0, True)
            kernel_b = functools.partial(halves_kernel, 1, False)
        else:
            kernel_a = kernel_b = step_kernel
        send_a = small_call(kernel_a, step_shape, near[2 * i], got_a, misc)
        send_b = small_call(kernel_b, step_shape, near[2 * i + 1], got_b, misc)
        if i == 2:
            send_a, send_b, own = lax.optimization_barrier((send_a, send_b, own))
            du = lax.all_to_all(own, ("x", "y"), 0, 0)
        got_a, got_b = ring(send_a, one_way), ring(send_b, other_way)
    proto_grad, patch_center, loss = finish(near[6], got_a, got_b, misc, prototypes)
    student_grad = small_call(
        final_kernel,
        jax.ShapeDtypeStruct(student_rows.shape, f32),
        info, student_rows, du.reshape(D, ROWS),
    )
    return (loss.reshape(()), student_grad, proto_grad, patch_center.reshape(-1))


def solution(mesh):
    fine = Mesh(mesh.devices.reshape(Z, CORES, X, Y), ("z", "core", "x", "y"))
    dp, proto = ("z", "core"), ("x", "y")
    in_specs = (
        P(dp, None, None),
        P(dp, None, None),
        P(None, proto),
        P(proto),
        P(dp, None),
        P(dp),
        P(),
    )
    out_specs = (P(), P(dp, None, None), P(proto + dp, None), P(proto))
    return jax.shard_map(shards, mesh=fine, in_specs=in_specs, out_specs=out_specs, check_vma=False)
```

```python
import functools
import math

import jax
import jax.numpy as jnp
from jax import lax
from jax.experimental import pallas as pl
from jax.experimental.pallas import tpu as pltpu
from jax.sharding import Mesh, PartitionSpec as P

bf16 = jnp.bfloat16
f32 = jnp.float32
log2e = math.log2(math.e)
ln2 = math.log(2.0)
t_scale = log2e / 0.04
s_scale = log2e / 0.1
inverse_temp = 10.0
norm_epsilon = 1e-06
low = -1e30

Z, CORES, X, Y = 8, 2, 4, 4
D = 256
SLOTS = 128
IMAGES = 64
TOTAL = 4096
LOCAL = 4
ROWS = LOCAL * SLOTS
BOTH = 2 * ROWS
CHUNK = 512
TILE = 512
STAT_TILE = 256
EXTRA = 32
HELD = ROWS + 16
STATS = 5
PEERS = CORES * X * Y
OFFSETS = (4, -3, 3, -2, 2, -1, 1, 0)
PIECES = 4

NT = (((1,), (1,)), ((), ()))
TN = (((0,), (0,)), ((), ()))


def dot(a, b, dims=(((1,), (0,)), ((), ()))):
    return lax.dot_general(a, b, dims, preferred_element_type=f32)


def params(mebibytes=16):
    return pltpu.CompilerParams(vmem_limit_bytes=mebibytes * 1024 * 1024)


def cost(flops, nbytes, trans=0):
    return pl.CostEstimate(flops=flops, bytes_accessed=nbytes, transcendentals=trans)


def picks(index_ref, count, i):
    patch = lax.broadcasted_iota(jnp.int32, (D, SLOTS), 0)
    slot = lax.broadcasted_iota(jnp.int32, (D, SLOTS), 1)
    hit = (patch == index_ref[i : i + 1, :]) & (slot < count)
    return jnp.where(hit, 1.0, 0.0).astype(bf16)


def unit_rows(values):
    length = jnp.sqrt(jnp.sum(values * values, axis=1, keepdims=True) + norm_epsilon)
    return values / length, length


def prep_kernel(count_ref, index_ref, s_ref, t_ref, out_ref, info_ref):
    for i in range(LOCAL):
        pick = picks(index_ref, count_ref[i], i)
        for which, ref in enumerate((s_ref, t_ref)):
            unit, _ = unit_rows(dot(pick, ref[i], TN))
            out_ref[which, i * SLOTS : (i + 1) * SLOTS, :] = unit.astype(bf16)
    row = lax.broadcasted_iota(jnp.int32, (HELD - ROWS, D), 0)
    counts = jnp.zeros((HELD - ROWS, D), jnp.int32)
    for i in range(LOCAL):
        counts = jnp.where(row == i, count_ref[i], counts)
    counts = counts.astype(f32)
    for which in range(2):
        out_ref[which, ROWS:, :] = counts.astype(bf16)
    info_ref[:LOCAL, :] = counts[:LOCAL, :SLOTS]
    info_ref[LOCAL:, :] = index_ref[...].astype(f32)


def prep(count, index, student, teacher):
    smem = pl.BlockSpec(memory_space=pltpu.SMEM)
    vmem = pl.BlockSpec(memory_space=pltpu.VMEM)
    return pl.pallas_call(
        prep_kernel,
        out_shape=[jax.ShapeDtypeStruct((2, HELD, D), bf16), jax.ShapeDtypeStruct((2 * LOCAL, SLOTS), f32)],
        in_specs=[smem, vmem, vmem, vmem],
        out_specs=[vmem, vmem],
        compiler_params=params(),
        cost_estimate=cost(2 * 2 * ROWS * D * D, 1 << 21),
    )(count, index, student, teacher)


def wide(block, times):
    return jnp.concatenate([block] * times, axis=1)


def chunk_columns(i, core):
    return pl.ds(pl.multiple_of((CORES * i + core) * CHUNK, CHUNK), CHUNK)


def turned(held):
    return jnp.broadcast_to(held * -t_scale, (128, CHUNK)).T


def stats_kernel(ids_ref, p_ref, c_ref, mine_ref, other_ref, block, sum_ref, acc):
    groups = (CHUNK // 8, 8, STAT_TILE)
    for i in range(Z):
        columns = chunk_columns(i, ids_ref[1])
        protos = p_ref[:, columns].T
        shift = wide(turned(c_ref[:, columns]), STAT_TILE // 128)
        for half, ref in enumerate((mine_ref, other_ref)):
            for j in range(ROWS // STAT_TILE):
                rows = slice(j * STAT_TILE, (j + 1) * STAT_TILE)
                at = slice(half * ROWS + j * STAT_TILE, half * ROWS + (j + 1) * STAT_TILE)
                t_arg = (dot(protos, ref[1, rows, :], NT) * t_scale + shift).reshape(groups)
                s_arg = (dot(protos, ref[0, rows, :], NT) * s_scale).reshape(groups)
                t_top = jnp.max(t_arg, axis=0)
                s_top = jnp.max(s_arg, axis=0)
                t_exp = jnp.exp2(t_arg - t_top[None])
                s_exp = jnp.exp2(s_arg - s_top[None])
                acc[0, i, :, at] = t_top
                acc[1, i, :, at] = jnp.sum(t_exp, axis=0)
                acc[2, i, :, at] = jnp.sum(t_exp * s_arg, axis=0)
                acc[3, i, :, at] = s_top
                acc[4, i, :, at] = jnp.sum(s_exp, axis=0)
    for g in range(BOTH // 128):
        at = slice(g * 128, (g + 1) * 128)
        parts = [acc[q, :, :, at].reshape(Z * 8, 128) for q in range(STATS)]
        t_top = jnp.max(parts[0], axis=0, keepdims=True)
        s_top = jnp.max(parts[3], axis=0, keepdims=True)
        t_keep = jnp.exp2(parts[0] - t_top)
        s_keep = jnp.exp2(parts[3] - s_top)
        merged_rows = (
            t_top,
            jnp.sum(parts[1] * t_keep, axis=0, keepdims=True),
            jnp.sum(parts[2] * t_keep, axis=0, keepdims=True),
            s_top,
            jnp.sum(parts[4] * s_keep, axis=0, keepdims=True),
        )
        for q in range(STATS):
            block[q * 8 + g : q * 8 + g + 1, :] = merged_rows[q]
    first = jnp.sum(mine_ref[1, :ROWS, :].astype(f32), axis=0, keepdims=True)
    second = jnp.sum(other_ref[1, :ROWS, :].astype(f32), axis=0, keepdims=True)
    sum_ref[...] = jnp.broadcast_to(first + second, (8, D))


def local_stats(ids, prototypes, center, mine, other):
    smem = pl.BlockSpec(memory_space=pltpu.SMEM)
    vmem = pl.BlockSpec(memory_space=pltpu.VMEM)
    return pl.pallas_call(
        stats_kernel,
        in_specs=[smem, vmem, vmem, vmem, vmem],
        out_specs=[vmem] * 2,
        out_shape=[jax.ShapeDtypeStruct((STATS * 8, 128), f32), jax.ShapeDtypeStruct((8, D), f32)],
        scratch_shapes=[pltpu.VMEM((STATS, Z, 8, BOTH), f32)],
        compiler_params=params(24),
        cost_estimate=cost(4 * BOTH * Z * CHUNK * D, 6 << 20, 2 * BOTH * Z * CHUNK),
    )(ids, prototypes, center, mine, other)


def split3(value):
    top = value.astype(bf16)
    rest = value - top.astype(f32)
    middle = rest.astype(bf16)
    return top, middle, (rest - middle.astype(f32)).astype(bf16)


def tree(parts):
    while len(parts) > 1:
        parts = [parts[i] + parts[i + 1] for i in range(0, len(parts), 2)]
    return parts[0]


def merge(parts):
    t_top = functools.reduce(jnp.maximum, [p[0] for p in parts])
    s_top = functools.reduce(jnp.maximum, [p[3] for p in parts])
    t_keep = [jnp.exp2(p[0] - t_top) for p in parts]
    s_keep = [jnp.exp2(p[3] - s_top) for p in parts]
    t_sum = tree([p[1] * k for p, k in zip(parts, t_keep)])
    cross = tree([p[2] * k for p, k in zip(parts, t_keep)])
    s_sum = tree([p[4] * k for p, k in zip(parts, s_keep)])
    return t_top, t_sum, cross, s_top, s_sum


def flip(value):
    return jnp.concatenate([value[LOCAL:], value[:LOCAL]], axis=0)


def rows_of(ref):
    return [ref[q * 8 : (q + 1) * 8, :] for q in range(STATS)]


def core_merge_kernel(mine_ref, got_ref, out_ref):
    parts = [rows_of(mine_ref), [flip(value) for value in rows_of(got_ref)]]
    for q, value in enumerate(merge(parts)):
        out_ref[q * 8 : (q + 1) * 8, :] = value


def y_merge_kernel(a, b, c, d, out_ref):
    for q, value in enumerate(merge([rows_of(ref) for ref in (a, b, c, d)])):
        out_ref[q * 8 : (q + 1) * 8, :] = value


def x_merge_kernel(ids_ref, scale_ref, a, b, c, d, mine_ref, other_ref, sum_ref, coef_ref, misc_ref):
    t_top, t_sum, cross, s_top, s_sum = merge([rows_of(ref) for ref in (a, b, c, d)])
    counts = [ref[0, ROWS:, :128].astype(f32)[:LOCAL] for ref in (mine_ref, other_ref)]
    count = jnp.concatenate(counts, axis=0)
    slot = lax.broadcasted_iota(jnp.int32, (8, 128), 1).astype(f32)
    live = slot < count
    weight = 1.0 / (IMAGES * jnp.maximum(count, 1.0))
    s_lse = s_top + jnp.log2(s_sum)
    ce = (s_lse - cross / t_sum) * ln2
    factor = jnp.log2(weight * (scale_ref[0] * inverse_temp))
    s_coef = jnp.where(live, factor - s_lse, low)
    t_coef = jnp.where(live, factor - t_top - jnp.log2(t_sum), low)
    for g in range(8):
        coef_ref[0:1, g * 128 : (g + 1) * 128] = s_coef[g : g + 1]
        coef_ref[1:2, g * 128 : (g + 1) * 128] = t_coef[g : g + 1]
    coef_ref[2:8, :] = jnp.zeros((6, BOTH), f32)
    part = jnp.sum(jnp.where(live, weight * ce, 0.0), axis=1, keepdims=True)
    first = jnp.sum(part[:LOCAL], axis=0, keepdims=True)
    second = jnp.sum(part[LOCAL:], axis=0, keepdims=True)
    row = lax.broadcasted_iota(jnp.int32, (EXTRA, D), 0)
    mine = jnp.bitwise_and(row, Z - 1) == ids_ref[0]
    row_sum = split3(sum_ref[0:1, :])
    losses = split3(jnp.broadcast_to(first + second, (1, D)))
    block = jnp.zeros((EXTRA, D), f32)
    for i in range(2):
        block = jnp.where(row // Z == i, row_sum[i].astype(f32), block)
        block = jnp.where(row // Z == 2 + i, losses[i].astype(f32), block)
    misc_ref[...] = jnp.where(mine, block, 0.0).astype(bf16)


def small_call(kernel, out_shape, *args, smem=()):
    specs = [
        pl.BlockSpec(memory_space=pltpu.SMEM if i in smem else pltpu.VMEM) for i in range(len(args))
    ]
    vmem = pl.BlockSpec(memory_space=pltpu.VMEM)
    return pl.pallas_call(
        kernel,
        out_shape=out_shape,
        in_specs=specs,
        out_specs=jax.tree.map(lambda _: vmem, out_shape),
        compiler_params=params(),
        cost_estimate=cost(1 << 20, 1 << 18),
    )(*args)


def grad_kernel(ids_ref, p_ref, c_ref, mine_ref, other_ref, coef_ref, misc_ref, *refs):
    n = len(OFFSETS)
    outs, send_ref, du_ref = refs[: n + 1], refs[n + 1], refs[n + 2]
    core = ids_ref[1]
    order = [lax.rem(ids_ref[0] + Z + d * (1 - 2 * core), Z) for d in OFFSETS]
    for i in range(n):
        columns = chunk_columns(order[i], core)
        wide_p = p_ref[:, columns]
        protos = wide_p.T
        shift = wide(turned(c_ref[:, columns]), TILE // 128)
        total = None
        for half, ref in enumerate((mine_ref, other_ref)):
            for j in range(ROWS // TILE):
                rows = slice(j * TILE, (j + 1) * TILE)
                at = slice(half * ROWS + j * TILE, half * ROWS + (j + 1) * TILE)
                s_rows = ref[0, rows, :]
                t_arg = dot(protos, ref[1, rows, :], NT) * t_scale + shift + coef_ref[1:2, at]
                s_arg = dot(protos, s_rows, NT) * s_scale + coef_ref[0:1, at]
                dlogit = (jnp.exp2(s_arg) - jnp.exp2(t_arg)).astype(bf16)
                part = dot(dlogit, s_rows)
                total = part if total is None else total + part
                du = dot(wide_p, dlogit)
                if i == 0:
                    du_ref[:, at] = du
                else:
                    du_ref[:, at] += du
        if i == 0:
            half = CHUNK // 2
            outs[0][:half, :] = total[:half].astype(bf16)
            outs[0][half:, :] = misc_ref[...]
            outs[1][...] = total[half:].astype(bf16)
        else:
            outs[i + 1][...] = total.astype(bf16)
    send_ref[core] = du_ref[:, :ROWS].astype(bf16)
    send_ref[1 - core] = du_ref[:, ROWS:].astype(bf16)


def grads(ids, prototypes, center, mine, other, coef, misc):
    smem = pl.BlockSpec(memory_space=pltpu.SMEM)
    vmem = pl.BlockSpec(memory_space=pltpu.VMEM)
    n = len(OFFSETS)
    shapes = [(CHUNK // 2 + EXTRA, D), (CHUNK // 2, D)] + [(CHUNK, D)] * (n - 1) + [(CORES, D, ROWS)]
    return pl.pallas_call(
        grad_kernel,
        in_specs=[smem] + [vmem] * 6,
        out_specs=[vmem] * len(shapes),
        out_shape=[jax.ShapeDtypeStruct(shape, bf16) for shape in shapes],
        scratch_shapes=[pltpu.VMEM((D, BOTH), f32)],
        compiler_params=params(24),
        cost_estimate=cost(8 * BOTH * n * CHUNK * D, n << 20, 2 * BOTH * n * CHUNK),
    )(ids, prototypes, center, mine, other, coef, misc)


def du_sum_kernel(got_ref, out_ref):
    total = jnp.sum(got_ref[...].astype(f32), axis=0).astype(bf16)
    out_ref[...] = jnp.broadcast_to(total[None], (X * Y,) + total.shape)


def halves_kernel(offset, with_extra, far_ref, got_ref, misc_ref, out_ref):
    half = CHUNK // 2
    for i in range(2):
        rows = slice(i * half, (i + 1) * half)
        part = far_ref[rows, :].astype(f32)
        if i == offset:
            part = part + got_ref[:half, :].astype(f32)
        out_ref[rows, :] = part.astype(bf16)
    extra = misc_ref[...]
    if with_extra:
        extra = extra + got_ref[half:, :]
    out_ref[CHUNK:, :] = extra


def step_kernel(near_ref, got_ref, misc_ref, out_ref):
    out_ref[:CHUNK, :] = (near_ref[...].astype(f32) + got_ref[:CHUNK, :].astype(f32)).astype(bf16)
    out_ref[CHUNK:, :] = misc_ref[...] + got_ref[CHUNK:, :]


def finish_kernel(near_ref, a_ref, b_ref, misc_ref, p_ref, grad_ref, center_ref, loss_ref):
    width = p_ref.shape[1] // PIECES
    pieces = [pl.ds(i * width, width) for i in range(PIECES)]
    total = near_ref[...].astype(f32) + a_ref[:CHUNK, :].astype(f32)
    grad_ref[...] = total + b_ref[:CHUNK, :].astype(f32)
    extra = (misc_ref[...] + a_ref[CHUNK:, :] + b_ref[CHUNK:, :]).astype(f32)
    first = extra[0:8] + extra[8:16]
    loss = extra[16:24] + extra[24:32]
    total = jnp.broadcast_to(jnp.sum(first, axis=0, keepdims=True), (16, D))
    loss_ref[0, 0] = jnp.sum(loss[:, 0:1])
    stacked = jnp.concatenate(split3(total), axis=0)
    for at in pieces:
        three = dot(stacked, p_ref[:, at])
        center_ref[:, at] = (three[0:1] + three[16:17] + three[32:33]) * (1.0 / TOTAL)


def finish(near, a, b, misc, prototypes):
    width = prototypes.shape[1]
    smem = pl.BlockSpec(memory_space=pltpu.SMEM)
    vmem = pl.BlockSpec(memory_space=pltpu.VMEM)
    return pl.pallas_call(
        finish_kernel,
        in_specs=[vmem] * 5,
        out_specs=[vmem, vmem, smem],
        out_shape=[
            jax.ShapeDtypeStruct((CHUNK, D), f32),
            jax.ShapeDtypeStruct((1, width), f32),
            jax.ShapeDtypeStruct((1, 1), f32),
        ],
        compiler_params=params(),
        cost_estimate=cost(6 * 8 * D * width, 5 << 20),
    )(near, a, b, misc, prototypes)


def final_kernel(info_ref, s_ref, du_ref, out_ref):
    for i in range(LOCAL):
        patch = lax.broadcasted_iota(jnp.int32, (D, SLOTS), 0).astype(f32)
        slot = lax.broadcasted_iota(jnp.int32, (D, SLOTS), 1).astype(f32)
        hit = (patch == info_ref[LOCAL + i : LOCAL + i + 1, :]) & (slot < info_ref[i : i + 1, :])
        pick = jnp.where(hit, 1.0, 0.0).astype(bf16)
        unit, length = unit_rows(dot(pick, s_ref[i], TN))
        d_unit = du_ref[:, i * SLOTS : (i + 1) * SLOTS].astype(f32).T
        row = (d_unit - unit * jnp.sum(unit * d_unit, axis=1, keepdims=True)) / length
        top = row.astype(bf16)
        rest = (row - top.astype(f32)).astype(bf16)
        out_ref[i] = dot(pick, top) + dot(pick, rest)


def shards(student_rows, teacher_rows, prototypes, center, mask_index, mask_count, loss_scale):
    z, core, x, y = (lax.axis_index(a) for a in ("z", "core", "x", "y"))
    ids = jnp.stack([z, core, x, y]).astype(jnp.int32)
    peers = ("core", "x", "y")
    one_way, other_way = [], []
    for i in range(Z):
        below, above, here = (i - 1) % Z * CORES, (i + 1) % Z * CORES, i * CORES
        one_way += [(here, below), (here + 1, above + 1)]
        other_way += [(here, above), (here + 1, below + 1)]

    def swaps(value, axis):
        return [lax.ppermute(value, axis, [(i, i ^ k) for i in range(4)]) for k in (1, 2, 3)]

    def ring(value, pairs):
        return lax.ppermute(value, ("z", "core"), pairs)

    mine, info = prep(mask_count, mask_index, student_rows, teacher_rows)
    other = lax.ppermute(mine, "core", [(0, 1), (1, 0)])
    center = center.reshape(1, -1)
    stats, row_sum = local_stats(ids, prototypes, center, mine, other)
    shape = jax.ShapeDtypeStruct((STATS * 8, 128), f32)
    stats = small_call(core_merge_kernel, shape, stats, lax.ppermute(stats, "core", [(0, 1), (1, 0)]))
    stats = small_call(y_merge_kernel, shape, stats, *swaps(stats, "y"))
    coef, misc = small_call(
        x_merge_kernel,
        [jax.ShapeDtypeStruct((8, BOTH), f32), jax.ShapeDtypeStruct((EXTRA, D), bf16)],
        ids, loss_scale.reshape(1), stats, *swaps(stats, "x"), mine, other, row_sum,
        smem=(0, 1),
    )

    step_shape = jax.ShapeDtypeStruct((CHUNK + EXTRA, D), bf16)
    half_a, half_b, *near, send = grads(ids, prototypes, center, mine, other, coef, misc)
    got_a, got_b = ring(half_a, one_way), ring(half_b, other_way)
    part = D // (X * Y)
    got = lax.all_to_all(send.reshape(PEERS, part, ROWS), peers, 0, 0)
    own = small_call(du_sum_kernel, jax.ShapeDtypeStruct((X * Y, part, ROWS), bf16), got)
    for i in range(3):
        if i == 0:
            kernel_a = functools.partial(halves_kernel, 0, True)
            kernel_b = functools.partial(halves_kernel, 1, False)
        else:
            kernel_a = kernel_b = step_kernel
        send_a = small_call(kernel_a, step_shape, near[2 * i], got_a, misc)
        send_b = small_call(kernel_b, step_shape, near[2 * i + 1], got_b, misc)
        if i == 2:
            send_a, send_b, own = lax.optimization_barrier((send_a, send_b, own))
            du = lax.all_to_all(own, ("x", "y"), 0, 0)
        got_a, got_b = ring(send_a, one_way), ring(send_b, other_way)
    proto_grad, patch_center, loss = finish(near[6], got_a, got_b, misc, prototypes)
    loss, du = lax.optimization_barrier((loss, du))
    student_grad = small_call(
        final_kernel,
        jax.ShapeDtypeStruct(student_rows.shape, f32),
        info, student_rows, du.reshape(D, ROWS),
    )
    return (loss.reshape(()), student_grad, proto_grad, patch_center.reshape(-1))


def solution(mesh):
    fine = Mesh(mesh.devices.reshape(Z, CORES, X, Y), ("z", "core", "x", "y"))
    dp, proto = ("z", "core"), ("x", "y")
    in_specs = (
        P(dp, None, None),
        P(dp, None, None),
        P(None, proto),
        P(proto),
        P(dp, None),
        P(dp),
        P(),
    )
    out_specs = (P(), P(dp, None, None), P(proto + dp, None), P(proto))
    return jax.shard_map(shards, mesh=fine, in_specs=in_specs, out_specs=out_specs, check_vma=False)
```
